32 devices in a mesh: seq: 4 (over y, core), dp: 8 (over z, x).
Axes of the slice: x: 2, y: 2, z: 4, core: 2. Of those that a mesh axis runs over, the one named last changes fastest.
Arguments:
- tokens: bfloat16 [8, 1024, 1280], P('dp', 'seq'), may hold values from -6 to 6
- lengths: int32 [8, 8], P('dp'), may hold values from 1 to 1016, as said below
- norm_attn: bfloat16 [1280], P(('seq', 'dp')), may hold values from 0.5 to 1.5
- norm_mlp: bfloat16 [1280], P(('seq', 'dp')), may hold values from 0.5 to 1.5
- query_scale: bfloat16 [1280], P(('seq', 'dp')), may hold values from -1 to 1.5
- query_proj: bfloat16 [1280, 1280], P(('seq', 'dp')), may hold values from -0.15625 to 0.15625
- key_proj: bfloat16 [1280, 1280], P(('seq', 'dp')), may hold values from -0.15625 to 0.15625
- value_proj: bfloat16 [1280, 1280], P(('seq', 'dp')), may hold values from -0.15625 to 0.15625
- output_proj: bfloat16 [1280, 1280], P(('seq', 'dp')), may hold values from -1.25 to 1.25
- gate_proj: bfloat16 [1280, 1280], P(('seq', 'dp')), may hold values from -0.15625 to 0.15625
- up_proj: bfloat16 [1280, 1280], P(('seq', 'dp')), may hold values from -0.15625 to 0.15625
- down_proj: bfloat16 [1280, 1280], P(('seq', 'dp')), may hold values from -0.15625 to 0.15625
- cotangent: bfloat16 [8, 1024, 1280], P('dp', 'seq'), may hold values from -6 to 6
Outputs:
- block_out: bfloat16 [8, 1024, 1280], P('dp', 'seq')
- grad_tokens: float32 [8, 1024, 1280], P('dp', 'seq')
- grad_norm_attn: float32 [1280], P(('seq', 'dp'))
- grad_norm_mlp: float32 [1280], P(('seq', 'dp'))
- grad_query_scale: float32 [1280], P(('seq', 'dp'))
- grad_query_proj: float32 [1280, 1280], P(('seq', 'dp'))
- grad_key_proj: float32 [1280, 1280], P(('seq', 'dp'))
- grad_value_proj: float32 [1280, 1280], P(('seq', 'dp'))
- grad_output_proj: float32 [1280, 1280], P(('seq', 'dp'))
- grad_gate_proj: float32 [1280, 1280], P(('seq', 'dp'))
- grad_up_proj: float32 [1280, 1280], P(('seq', 'dp'))
- grad_down_proj: float32 [1280, 1280], P(('seq', 'dp'))
The draws below stay inside these ranges and needn't reach their ends.
Inputs may be any that keep to these rules, and one draw needn't show every extreme that they name: Each row holds the lengths of 8 documents packed in order into one sequence of 1024 positions; their sum is less than 1024, and the positions past it are padding. In every row one document starts within the first 256 positions and ends within the last 256.
All inputs are finite; a program needn't handle non-finite values.
Results may differ from the reference program's by a relative error of at most 0.015.
Values may be sent and summed in bfloat16 or wider, within the bound.
No kernel may reach another device: no remote copies, remote signals or barrier semaphores. Data moves between devices by JAX's collectives and lax.ppermute only.
A program may use at most 256 MiB of HBM per device.

```python
import jax
import jax.numpy as jnp
from jax import lax

H = 16
HD = 80
FF = 1280
D = 1280
TOK_DEV = 256
NDOC = 8
LENGTH = 1024
SEQS = 8


def draw_lengths(key, part):
    key = jax.random.fold_in(key, 7)
    key_exp, key_bits, key_pad, key_long, key_row = jax.random.split(key, 5)
    small_most = max(1, TOK_DEV // (2 * NDOC))
    top_exp = small_most.bit_length() - 1
    exponents = jax.random.randint(key_exp, (SEQS, NDOC), 0, top_exp + 1)
    raw_bits = jax.random.randint(key_bits, (SEQS, NDOC), 0, 1 << 30)
    small_docs = 1 + raw_bits % jnp.left_shift(jnp.ones_like(exponents), exponents)
    padding = jax.random.randint(key_pad, (SEQS, 1), 1, max(2, TOK_DEV // 2))
    tight_row = jax.random.randint(key_row, (), 0, SEQS)
    row_ids = jnp.arange(SEQS, dtype=jnp.int32)[:, None]
    is_tight = row_ids == tight_row
    small_docs = jnp.where(is_tight, 1, small_docs)
    padding = jnp.where(is_tight, 1, padding)
    long_slot = jax.random.randint(key_long, (SEQS, 1), 0, NDOC)
    slots = jnp.arange(NDOC, dtype=jnp.int32)[None, :]
    small_docs = jnp.where(slots == long_slot, 0, small_docs)
    long_doc = LENGTH - padding - jnp.sum(small_docs, axis=1, keepdims=True)
    return jnp.where(slots == long_slot, long_doc, small_docs).astype(jnp.int32)


def level_of(key, dims, cuts, smallest, top_value):
    level = 1.0
    for dim, shards_of in cuts:
        draws = jax.random.uniform(jax.random.fold_in(jax.random.fold_in(key, 6), dim), (shards_of,), jnp.float32, smallest / len(cuts), top_value / len(cuts))
        level = level * jnp.repeat(jnp.exp(draws), dims[dim] // shards_of).reshape((-1,) + (1,) * (len(dims) - 1 - dim))
    return level


def centred(key, dims, scale, reach, pieces=(), held_as=jnp.bfloat16):
    result = scale * jax.random.normal(key, dims, jnp.float32)
    if pieces:
        result = result * level_of(key, dims, pieces, -0.22, 0.18)
    return jnp.clip(result, -reach, reach).astype(held_as)


def setup_inputs(seed: int = 0) -> dict:
    streams_of = jax.random.split(jax.random.key(seed), 14)
    return {
        "tokens": centred(streams_of[0], (SEQS, LENGTH, D), 1.0, 6.0, ((0, 8), (1, 4))),
        "lengths": draw_lengths(jax.random.fold_in(streams_of[13], 71), 0),
        "norm_attn": jnp.clip(1.0 + 0.1 * jax.random.normal(streams_of[2], (D,), jnp.float32), 0.5, 1.5).astype(jnp.bfloat16),
        "norm_mlp": jnp.clip(1.0 + 0.1 * jax.random.normal(streams_of[3], (D,), jnp.float32), 0.5, 1.5).astype(jnp.bfloat16),
        "query_scale": jnp.clip(-1.0 + 2.5 * jax.random.uniform(streams_of[4], (D,), jnp.float32) ** level_of(streams_of[4], (D,), ((0, 32),), -0.2, 0.2), -1.0, 1.5).astype(jnp.bfloat16),
        "query_proj": centred(streams_of[5], (D, D), D ** -0.5, 0.15625, ((0, 32),)),
        "key_proj": centred(streams_of[6], (D, D), D ** -0.5, 0.15625, ((0, 32),)),
        "value_proj": centred(streams_of[7], (D, D), D ** -0.5, 0.15625, ((0, 32),)),
        "output_proj": centred(streams_of[8], (D, D), (D // 64) ** -0.5, 1.25, ((0, 32),)),
        "gate_proj": centred(streams_of[9], (D, FF), D ** -0.5, 0.15625, ((0, 32),)),
        "up_proj": centred(streams_of[10], (D, FF), D ** -0.5, 0.15625, ((0, 32),)),
        "down_proj": centred(streams_of[11], (FF, D), FF ** -0.5, 0.15625, ((0, 32),)),
        "cotangent": centred(streams_of[12], (SEQS, LENGTH, D), 1.0, 6.0, ((0, 8), (1, 4))),
    }


EPSILON = 1e-06
R_SOFTPLUS = 1.442695041
MASKED = -1e+30
HIGHEST_PRECISION = lax.Precision.HIGHEST

@jax.custom_vjp
def low(v):
    return lax.optimization_barrier(v.astype(jnp.bfloat16)).astype(jnp.float32)

@jax.custom_vjp
def low_back(v):
    return v

def low_keep(v):
    return (low(v), None)

def low_pass(kept, grad):
    return (grad,)

def back_keep(v):
    return (v, None)

def back_low(kept, grad):
    return (low(grad),)
low.defvjp(low_keep, low_pass)
low_back.defvjp(back_keep, back_low)

def product(left, right):
    return jnp.dot(left, right, preferred_element_type=jnp.float32, precision=HIGHEST_PRECISION)

def norm_rows(values, gain):
    return values * lax.rsqrt(lax.optimization_barrier(jnp.mean(values * values, axis=-1, keepdims=True)) + EPSILON) * gain

def segment_rows(lengths_row, length):
    doc_ends = jnp.cumsum(lengths_row.astype(jnp.int32))
    places = jnp.arange(length, dtype=jnp.int32)
    segment = lax.optimization_barrier(jnp.sum((places[:, None] >= doc_ends[None, :]).astype(jnp.int32), axis=1))
    return (segment, places < doc_ends[-1])

def attend(queries, key_rows, value_rows, segment):
    length = queries.shape[0]
    block_size = min(512, length)
    query_heads = queries.reshape(length, H, HD)
    key_heads = key_rows.reshape(length, H, HD)
    value_heads = value_rows.reshape(length, H, HD)
    places = jnp.arange(length, dtype=jnp.int32)

    def one_block(row_start):
        query_block = lax.dynamic_slice_in_dim(query_heads, row_start, block_size, 0)
        row_ids = lax.dynamic_slice_in_dim(places, row_start, block_size, 0)
        row_segments = lax.dynamic_slice_in_dim(segment, row_start, block_size, 0)
        scores = low_back(jnp.einsum('qhd,khd->hqk', query_block, key_heads, precision=HIGHEST_PRECISION))
        allowed = (places[None, :] <= row_ids[:, None]) & (segment[None, :] == row_segments[:, None])
        scores = jnp.where(allowed[None], scores, MASKED)
        row_max = lax.optimization_barrier(jnp.max(scores, axis=2, keepdims=True))
        exp_scores = jnp.exp(scores - row_max)
        weights_p = low(exp_scores / lax.optimization_barrier(jnp.sum(exp_scores, axis=2, keepdims=True)))
        mixed_heads = jnp.einsum('hqk,khd->qhd', weights_p, value_heads, precision=HIGHEST_PRECISION)
        return mixed_heads.reshape(block_size, H * HD)
    starts = jnp.arange(length // block_size, dtype=jnp.int32) * block_size
    return lax.map(jax.checkpoint(one_block), starts).reshape(length, H * HD)

def layer(weights_f, inputs, segment):
    gain_a, gain_m, scale_logit, proj_q, proj_k, proj_v, proj_o, proj_g, proj_u, proj_d = weights_f
    normed = low(norm_rows(inputs, gain_a))
    q_raw = low_back(product(normed, proj_q))
    queries = low(q_raw * (R_SOFTPLUS * HD ** (-0.5) * jax.nn.softplus(scale_logit)))
    key_rows = low(low_back(product(normed, proj_k)))
    value_rows = low(low_back(product(normed, proj_v)))
    attended = low(low_back(attend(queries, key_rows, value_rows, segment)))
    hidden1 = inputs + low_back(product(attended, proj_o))
    normed_m = low(norm_rows(hidden1, gain_m))
    gate_pre = low_back(product(normed_m, proj_g))
    up_pre = low_back(product(normed_m, proj_u))
    hidden = low(jax.nn.silu(gate_pre) * up_pre)
    return hidden1 + low_back(product(hidden, proj_d))

def reference(tokens, lengths, norm_attn, norm_mlp, query_scale, query_proj, key_proj, value_proj, output_proj, gate_proj, up_proj, down_proj, cotangent):
    weights_f = tuple((weight.astype(jnp.float32) for weight in (norm_attn, norm_mlp, query_scale, query_proj, key_proj, value_proj, output_proj, gate_proj, up_proj, down_proj)))
    length = tokens.shape[1]

    def one_sequence(grad_totals, sequence_item):
        inputs, cot_rows, lengths_row = sequence_item
        segment, valid = segment_rows(lengths_row, length)
        outputs, pull_back = jax.vjp(lambda weight_args, rows_in: layer(weight_args, rows_in, segment), weights_f, inputs)
        grad_weights, grad_inputs = pull_back(cot_rows * valid[:, None].astype(jnp.float32))
        return (jax.tree.map(jnp.add, grad_totals, grad_weights), (outputs.astype(jnp.bfloat16), grad_inputs))
    zero_sums = tuple((jnp.zeros_like(weight) for weight in weights_f))
    grad_totals, (block_out, grad_tokens) = lax.scan(one_sequence, zero_sums, (tokens.astype(jnp.float32), cotangent.astype(jnp.float32), lengths))
    return (block_out, grad_tokens, grad_totals[0], grad_totals[1], grad_totals[2], grad_totals[3], grad_totals[4], grad_totals[5], grad_totals[6], grad_totals[7], grad_totals[8], grad_totals[9])
```

```python
import jax
import jax.numpy as jnp
from jax import lax
from jax.experimental import pallas as pl
from jax.experimental.pallas import tpu as pltpu
from jax.sharding import Mesh, PartitionSpec as P

H = 16
HD = 80
EPSILON = 1e-06
R_SOFTPLUS = 1.442695041
MASKED = -1e30
QUERY_ROWS = 256
VMEM_BYTES = 48 << 20
LONGEST_LINE = 4
F32 = jnp.float32
BF16 = jnp.bfloat16
GROUP = ("y", "z", "x")


def nn(left, right):
    return jnp.dot(left, right, preferred_element_type=F32)


def nt(left, right):
    return lax.dot_general(left, right, (((1,), (1,)), ((), ())), preferred_element_type=F32)


def tn(left, right):
    return lax.dot_general(left, right, (((0,), (0,)), ((), ())), preferred_element_type=F32)


def allowed_pairs(seg_rows, seg_keys, half, first, rows):
    total = seg_keys.shape[1]
    row_ids = lax.broadcasted_iota(jnp.int32, (rows, total), 0) + (first + half)
    col_ids = lax.broadcasted_iota(jnp.int32, (rows, total), 1)
    return (seg_rows == seg_keys) & (col_ids <= row_ids)


def forward_kernel(q_ref, k_ref, v_ref, segq_ref, segk_ref, out_ref, lse_ref):
    half, width = q_ref.shape
    for first in range(0, half, QUERY_ROWS):
        rows = slice(first, first + QUERY_ROWS)
        allowed = allowed_pairs(segq_ref[rows, :], segk_ref[...], half, first, QUERY_ROWS)
        outs, lses = [], []
        for head in range(width // HD):
            cols = slice(head * HD, (head + 1) * HD)
            scores = jnp.where(allowed, nt(q_ref[rows, cols], k_ref[:, cols]), MASKED)
            top = jnp.max(scores, axis=1, keepdims=True)
            exps = jnp.exp(scores - top)
            total = jnp.sum(exps, axis=1, keepdims=True)
            probs = (exps * (1.0 / total)).astype(BF16)
            outs.append(nn(probs, v_ref[:, cols]))
            lses.append(top + jnp.log(total))
        out_ref[rows, :] = jnp.concatenate(outs, axis=1)
        lse_ref[rows, :] = jnp.concatenate(lses, axis=1)


def backward_kernel(
    q_ref, k_ref, v_ref, go_ref, out_ref, lse_ref, segq_ref, segk_ref, dq_ref, dk_ref, dv_ref
):
    half, width = q_ref.shape
    heads = width // HD
    dks, dvs = [0.0] * heads, [0.0] * heads
    for first in range(0, half, QUERY_ROWS):
        rows = slice(first, first + QUERY_ROWS)
        allowed = allowed_pairs(segq_ref[rows, :], segk_ref[...], half, first, QUERY_ROWS)
        products = go_ref[rows, :].astype(F32) * out_ref[rows, :]
        dqs = []
        for head in range(heads):
            cols = slice(head * HD, (head + 1) * HD)
            queries, keys, values = q_ref[rows, cols], k_ref[:, cols], v_ref[:, cols]
            grads = go_ref[rows, cols]
            scores = jnp.where(allowed, nt(queries, keys), MASKED)
            probs = jnp.exp(scores - lse_ref[rows, head : head + 1])
            delta = jnp.sum(products[:, cols], axis=1, keepdims=True)
            grad_scores = (probs * (nt(grads, values) - delta)).astype(BF16)
            dqs.append(nn(grad_scores, keys))
            dks[head] = dks[head] + tn(grad_scores, queries)
            dvs[head] = dvs[head] + tn(probs.astype(BF16), grads)
        dq_ref[rows, :] = jnp.concatenate(dqs, axis=1)
    dk_ref[...] = jnp.concatenate(dks, axis=1).astype(dk_ref.dtype)
    dv_ref[...] = jnp.concatenate(dvs, axis=1).astype(dv_ref.dtype)


WHOLE = pl.BlockSpec(memory_space=pltpu.VMEM)


def attention_forward(q, k, v, segq, segk):
    return pl.pallas_call(
        forward_kernel,
        out_shape=(
            jax.ShapeDtypeStruct(q.shape, F32),
            jax.ShapeDtypeStruct((q.shape[0], q.shape[1] // HD), F32),
        ),
        in_specs=[WHOLE] * 5,
        out_specs=(WHOLE, WHOLE),
        compiler_params=pltpu.CompilerParams(vmem_limit_bytes=VMEM_BYTES),
        cost_estimate=pl.CostEstimate(flops=9000000000, bytes_accessed=8 << 20, transcendentals=4 << 20),
        name="attention_forward",
    )(q, k, v, segq, segk)


def attention_backward(q, k, v, grads, out, lse, segq, segk):
    return pl.pallas_call(
        backward_kernel,
        out_shape=(
            jax.ShapeDtypeStruct(q.shape, F32),
            jax.ShapeDtypeStruct(k.shape, BF16),
            jax.ShapeDtypeStruct(v.shape, BF16),
        ),
        in_specs=[WHOLE] * 8,
        out_specs=(WHOLE,) * 3,
        compiler_params=pltpu.CompilerParams(vmem_limit_bytes=VMEM_BYTES),
        cost_estimate=pl.CostEstimate(flops=13000000000, bytes_accessed=10 << 20, transcendentals=4 << 20),
        name="attention_backward",
    )(q, k, v, grads, out, lse, segq, segk)


def swap(value, axis):
    return lax.ppermute(value, axis, [(0, 1), (1, 0)])


def pick(pair, index):
    return jnp.where(index == 0, pair[0], pair[1])


def in_order(own, other, index, axis):
    return jnp.where(
        index == 0,
        jnp.concatenate([own, other], axis=axis),
        jnp.concatenate([other, own], axis=axis),
    )


def block_of(matrix, index, size, axis=0):
    return lax.dynamic_slice_in_dim(matrix, index * size, size, axis)


def norm_inverse(values):
    return lax.rsqrt(jnp.mean(values * values, axis=-1, keepdims=True) + EPSILON)


def norm_back(values, inverse, gain, upstream):
    scaled = upstream * gain
    return inverse * scaled - values * inverse**3 * jnp.mean(
        values * scaled, axis=-1, keepdims=True
    )


def line_scatter(parts, place, count):
    if count > LONGEST_LINE:
        return lax.psum_scatter(parts.astype(BF16), "z", scatter_dimension=0).astype(F32)
    right, left = 0.0, 0.0
    for step in range(1, count):
        ahead = lax.dynamic_index_in_dim(
            parts, jnp.minimum(place + count - step, count - 1), 0, keepdims=False
        )
        behind = lax.dynamic_index_in_dim(
            parts, jnp.maximum(place - count + step, 0), 0, keepdims=False
        )
        right = lax.ppermute(
            (ahead + right).astype(BF16), "z", [(i, i + 1) for i in range(step)]
        ).astype(F32)
        left = lax.ppermute(
            (behind + left).astype(BF16), "z", [(i, i - 1) for i in range(count - step, count)]
        ).astype(F32)
    return lax.dynamic_index_in_dim(parts, place, 0, keepdims=False) + right + left


def local(
    tokens,
    lengths,
    norm_attn,
    norm_mlp,
    query_scale,
    query_proj,
    key_proj,
    value_proj,
    output_proj,
    gate_proj,
    up_proj,
    down_proj,
    cotangent,
):
    y, c, z, x = (lax.axis_index(name) for name in ("y", "c", "z", "x"))
    line = lax.axis_size("z")
    rows = tokens.shape[1]
    share, width = query_proj.shape
    half = width // 2
    quarter = width // 4
    chip_rows = 2 * rows
    length = 4 * rows

    def halves(weight):
        split = weight.reshape(share, 2, 2, quarter)
        return [split[:, :, core].reshape(share, half) for core in range(2)]

    vector_rows = jnp.pad(
        jnp.concatenate([norm_attn, norm_mlp, query_scale])[None], ((0, 7), (0, half - 3 * share))
    )

    def by_columns(weights, tail):
        split = [halves(weight) for weight in weights]
        both = [jnp.concatenate([pair[core] for pair in split] + tail, axis=0) for core in range(2)]
        return in_order(pick(both, c), swap(pick(both, 1 - c), "c"), c, 1)

    first_message = by_columns([query_proj, key_proj, value_proj], [vector_rows])
    second_message = jnp.concatenate(
        [output_proj, down_proj, by_columns([gate_proj, up_proj], [])], axis=0
    )
    first = lax.all_gather(first_message, GROUP, axis=0, tiled=False)
    second = lax.all_gather(second_message, GROUP, axis=0, tiled=False)
    first = first.reshape((2, line, 2) + first.shape[1:])
    second = second.reshape((2, line, 2) + second.shape[1:])

    def column_weight(gathered, index):
        block = gathered[:, :, :, index * share : (index + 1) * share]
        block = block.reshape(2, line, 2, share, 2, half).transpose(0, 4, 1, 2, 3, 5)
        return block.reshape(width, half)

    def row_weight(gathered, index):
        return gathered[:, :, :, index * share : (index + 1) * share].reshape(half, width)

    proj_q, proj_k, proj_v = (column_weight(first, index) for index in range(3))
    proj_o, proj_d = (row_weight(second, index) for index in range(2))
    proj_g, proj_u = (column_weight(second, index) for index in (2, 3))
    vectors = first[:, :, :, 3 * share].reshape(2, line, 2, 2, half)[..., : 3 * share]
    vectors = vectors.reshape(2, line, 2, 2, 3, share).transpose(4, 0, 3, 1, 2, 5)
    vectors = vectors.reshape(3, width).astype(F32)
    gain_a, gain_m = vectors[0], vectors[1]
    scale_logit = lax.dynamic_index_in_dim(
        vectors[2].reshape(2, 2, quarter), c, 1, keepdims=False
    ).reshape(half)
    scale_vec = R_SOFTPLUS * HD ** (-0.5) * jax.nn.softplus(scale_logit)

    own_tokens = tokens[0]
    before = lax.ppermute(own_tokens, "y", [(0, 1)])
    chip_tokens = in_order(own_tokens, swap(own_tokens, "c"), c, 0)
    chip_before = in_order(before, swap(before, "c"), c, 0)
    doc_ends = jnp.cumsum(lengths[0])
    places = jnp.arange(length, dtype=jnp.int32)
    segment = jnp.sum((places[:, None] >= doc_ends[None, :]).astype(jnp.int32), axis=1)
    seg_here = block_of(segment, y, chip_rows)
    seg_before = jnp.where(y == 0, -1, segment[:chip_rows])
    seg_keys = jnp.concatenate([seg_before, seg_here])[None]
    valid = (y * chip_rows + jnp.arange(chip_rows, dtype=jnp.int32)) < doc_ends[-1]
    own_cotangent = cotangent[0]
    chip_cotangent = in_order(own_cotangent, swap(own_cotangent, "c"), c, 0)
    upstream_b = jnp.where(valid[:, None], chip_cotangent, 0).astype(BF16)
    upstream = block_of(upstream_b, c, rows).astype(F32)

    def reduce_rows(make):
        other = swap(make(1 - c), "c")
        return make(c) + other

    inputs = own_tokens.astype(F32)
    inverse_a = norm_inverse(inputs)
    all_tokens = jnp.concatenate([chip_before, chip_tokens], axis=0).astype(F32)
    normed = (all_tokens * norm_inverse(all_tokens) * gain_a).astype(BF16)
    normed_here = normed[chip_rows:]
    q_raw = nn(normed_here, proj_q)
    queries = (q_raw * scale_vec).astype(BF16)
    keys = nn(normed, proj_k).astype(BF16)
    values = nn(normed, proj_v).astype(BF16)
    attended_f, lse = attention_forward(queries, keys, values, seg_here[:, None], seg_keys)
    attended = attended_f.astype(BF16)
    hidden1 = inputs + reduce_rows(lambda core: nn(block_of(attended, core, rows), proj_o))
    inverse_m = norm_inverse(hidden1)
    own_normed_m = (hidden1 * inverse_m * gain_m).astype(BF16)
    normed_m = in_order(own_normed_m, swap(own_normed_m, "c"), c, 0)
    gate_pre = nn(normed_m, proj_g)
    up_pre = nn(normed_m, proj_u)
    sigmoid_gate = jax.nn.sigmoid(gate_pre)
    hidden = (gate_pre * sigmoid_gate * up_pre).astype(BF16)
    block_out = hidden1 + reduce_rows(lambda core: nn(block_of(hidden, core, rows), proj_d))

    def y_rows(left, right):
        size = left.shape[1] // 2
        other = swap(tn(block_of(left, 1 - y, size, 1), right).astype(BF16), "y")
        return tn(block_of(left, y, size, 1), right) + other.astype(F32)

    def column_grad(left, right):
        part = y_rows(left, right).reshape(2, line, 2, share, half)
        return part.transpose(1, 2, 3, 0, 4).reshape(line, 2, share, width)

    def row_grad(left, right):
        return y_rows(left, right).reshape(line, 2, share, width)

    def scatter(parts):
        part = line_scatter(jnp.concatenate(parts, axis=2), z, line)
        other = swap(pick(part, 1 - x).astype(BF16), "x").astype(F32)
        return pick(part, x) + other

    def whole_rows(part):
        split = part.reshape(part.shape[0], 2, half)
        mine, others = pick((split[:, 0], split[:, 1]), c), pick((split[:, 1], split[:, 0]), c)
        return mine, swap(others, "c")

    def whole_columns(part):
        mine, other = (side.reshape(-1, 2, 1, quarter) for side in whole_rows(part))
        return in_order(mine, other, c, 2).reshape(part.shape[0], width)

    grad_down = scatter([row_grad(hidden, upstream_b)])
    grad_hidden = nt(upstream_b, proj_d)
    grad_up = (grad_hidden * gate_pre * sigmoid_gate).astype(BF16)
    grad_gate = (
        grad_hidden * up_pre * sigmoid_gate * (1.0 + gate_pre * (1.0 - sigmoid_gate))
    ).astype(BF16)
    grad_mlp = scatter([column_grad(normed_m, grad_gate), column_grad(normed_m, grad_up)])
    grad_normed_m = reduce_rows(
        lambda core: nt(block_of(grad_gate, core, rows), proj_g)
        + nt(block_of(grad_up, core, rows), proj_u)
    )
    grad_gain_m = jnp.sum(grad_normed_m * hidden1 * inverse_m, axis=0)
    grad_hidden1 = upstream + norm_back(hidden1, inverse_m, gain_m, grad_normed_m)
    own_grad_hidden1 = grad_hidden1.astype(BF16)
    grad_hidden1_b = in_order(own_grad_hidden1, swap(own_grad_hidden1, "c"), c, 0)
    grad_output = scatter([row_grad(attended, grad_hidden1_b)])
    grad_attended = nt(grad_hidden1_b, proj_o).astype(BF16)
    grad_queries, grad_keys, grad_values = attention_backward(
        queries, keys, values, grad_attended, attended_f, lse, seg_here[:, None], seg_keys
    )
    grad_q_raw = (grad_queries * scale_vec).astype(BF16)
    grad_scale = (
        jnp.sum(q_raw * grad_queries, axis=0)
        * R_SOFTPLUS
        * HD ** (-0.5)
        * jax.nn.sigmoid(scale_logit)
    )
    grad_before = reduce_rows(
        lambda core: nt(block_of(grad_keys[:chip_rows], core, rows), proj_k)
        + nt(block_of(grad_values[:chip_rows], core, rows), proj_v)
    )
    grad_after = lax.ppermute(grad_before.astype(BF16), "y", [(1, 0)]).astype(F32)
    grad_normed = grad_after + reduce_rows(
        lambda core: nt(block_of(grad_q_raw, core, rows), proj_q)
        + nt(block_of(grad_keys[chip_rows:], core, rows), proj_k)
        + nt(block_of(grad_values[chip_rows:], core, rows), proj_v)
    )
    grad_gain_a = jnp.sum(grad_normed * inputs * inverse_a, axis=0)
    grad_inputs = grad_hidden1 + norm_back(inputs, inverse_a, gain_a, grad_normed)

    scale_rows = grad_scale.reshape(2, 1, quarter)
    scale_rows = jnp.where(
        c == 0,
        jnp.pad(scale_rows, ((0, 0), (0, 1), (0, 0))),
        jnp.pad(scale_rows, ((0, 0), (1, 0), (0, 0))),
    ).reshape(width)
    vector_terms = jnp.stack([grad_gain_a, grad_gain_m, scale_rows])
    vector_terms = vector_terms.reshape(3, 2, 2, line, 2, share).transpose(1, 3, 4, 2, 0, 5)
    vector_terms = vector_terms.reshape(2, line, 2, 1, 2, 3 * share)
    vector_terms = pick(vector_terms, y) + swap(pick(vector_terms, 1 - y), "y")
    vector_terms = jnp.pad(
        vector_terms, ((0, 0), (0, 0), (0, 7), (0, 0), (0, half - 3 * share))
    ).reshape(line, 2, 8, width)
    grad_attn = scatter(
        [
            column_grad(normed_here, grad_q_raw),
            column_grad(normed, grad_keys),
            column_grad(normed, grad_values),
            vector_terms,
        ]
    )
    vector_mine, vector_other = whole_rows(grad_attn[3 * share : 3 * share + 1])
    summed = (vector_mine + vector_other)[0, : 3 * share].reshape(3, share)
    attn_columns = whole_columns(grad_attn[: 3 * share])
    mlp_columns = whole_columns(grad_mlp)
    return (
        block_out.astype(BF16)[None],
        grad_inputs[None],
        summed[0],
        summed[1],
        summed[2],
        attn_columns[:share],
        attn_columns[share : 2 * share],
        attn_columns[2 * share :],
        grad_output,
        mlp_columns[:share],
        mlp_columns[share:],
        grad_down,
    )


def solution(mesh):
    seq, dp = mesh.devices.shape
    axes = Mesh(mesh.devices.reshape(seq // 2, 2, dp // 2, 2), ("y", "c", "z", "x"))
    batch, places, every = ("z", "x"), ("y", "c"), ("y", "c", "z", "x")
    activations = P(batch, places, None)
    vector, matrix = P(every), P(every, None)
    return jax.shard_map(
        local,
        mesh=axes,
        in_specs=(activations, P(batch, None)) + (vector,) * 3 + (matrix,) * 7 + (activations,),
        out_specs=(activations, activations) + (vector,) * 3 + (matrix,) * 7,
        check_vma=False,
    )
```

```python
import functools

import jax
import jax.numpy as jnp
from jax import lax
from jax.experimental import pallas as pl
from jax.experimental.pallas import tpu as pltpu
from jax.sharding import Mesh, PartitionSpec as P

H = 16
HD = 80
EPSILON = 1e-06
R_SOFTPLUS = 1.442695041
MASKED = -1e30
QUERY_ROWS = 256
VMEM_BYTES = 16 << 20
SPEED = 4600000000
COSTS = {
    "project": 5, "attention_forward": 13, "output_project": 3, "mlp_middle": 3, "gate_up_back": 3,
    "products": 6, "attention_backward": 10, "back_project": 10, "join": 3, "tokens_back": 3,
}
F32 = jnp.float32
BF16 = jnp.bfloat16


def nn(left, right):
    return jnp.dot(left, right, preferred_element_type=F32)


def nt(left, right):
    return lax.dot_general(left, right, (((1,), (1,)), ((), ())), preferred_element_type=F32)


def tn(left, right):
    return lax.dot_general(left, right, (((0,), (0,)), ((), ())), preferred_element_type=F32)


def allowed_pairs(seg_rows, seg_keys, half, first, rows):
    total = seg_keys.shape[1]
    row_ids = lax.broadcasted_iota(jnp.int32, (rows, total), 0) + (first + half)
    col_ids = lax.broadcasted_iota(jnp.int32, (rows, total), 1)
    return (seg_rows == seg_keys) & (col_ids <= row_ids)


WHOLE = pl.BlockSpec(memory_space=pltpu.VMEM)
SCALARS = pl.BlockSpec(memory_space=pltpu.SMEM)


def call(kernel, name, out_shape, scalars, *arrays):
    specs = [SCALARS] * len(scalars) + [WHOLE] * len(arrays)
    return pl.pallas_call(
        kernel,
        out_shape=out_shape,
        in_specs=specs,
        out_specs=jax.tree.map(lambda shape: WHOLE, out_shape),
        compiler_params=pltpu.CompilerParams(vmem_limit_bytes=VMEM_BYTES),
        cost_estimate=pl.CostEstimate(flops=COSTS.get(name, 2) * SPEED, bytes_accessed=0, transcendentals=0),
        name=name,
    )(*scalars, *arrays)


def shaped(shape, dtype):
    return jax.ShapeDtypeStruct(tuple(shape), dtype)


def project_kernel(
    core_ref, tokens_ref, weight_ref, raw_ref, q_ref, kv_ref, before_ref, here_ref, vectors_ref,
    scale_ref
):
    chip_rows, half = raw_ref.shape
    quarter = half // 2
    vectors = weight_ref[:, 3 * half :].astype(F32).T[:8]
    vectors_ref[...] = vectors
    gain = vectors[0:1]
    logits = [
        jnp.concatenate(
            [vectors[2:3, side * half + core * quarter :][:, :quarter] for side in range(2)], axis=1
        )
        for core in range(2)
    ]
    logit = jnp.where(core_ref[0] == 0, logits[0], logits[1])
    softplus = jnp.maximum(logit, 0.0) + jnp.log1p(jnp.exp(-jnp.abs(logit)))
    scale = R_SOFTPLUS * HD ** (-0.5) * softplus
    scale_ref[0:1] = scale
    scale_ref[1:2] = R_SOFTPLUS * HD ** (-0.5) / (1.0 + jnp.exp(-logit))
    for first in range(0, 2 * chip_rows, QUERY_ROWS):
        rows = slice(first, first + QUERY_ROWS)
        values = tokens_ref[rows, :].astype(F32)
        inverse = lax.rsqrt(jnp.mean(values * values, axis=1, keepdims=True) + EPSILON)
        normed = (values * inverse * gain).astype(BF16)
        kv_ref[rows, :] = nn(normed, weight_ref[:, half : 3 * half]).astype(BF16)
        if first >= chip_rows:
            here = slice(first - chip_rows, first - chip_rows + QUERY_ROWS)
            here_ref[here, :] = normed
            raw = nn(normed, weight_ref[:, :half])
            raw_ref[here, :] = raw
            q_ref[here, :] = (raw * scale).astype(BF16)
        else:
            before_ref[rows, :] = normed


def project(core, tokens, weights):
    rows, width = tokens.shape
    half = width // 2
    shapes = (
        shaped((rows // 2, half), F32),
        shaped((rows // 2, half), BF16),
        shaped((rows, width), BF16),
        shaped((rows // 2, width), BF16),
        shaped((rows // 2, width), BF16),
        shaped((8, width), F32),
        shaped((2, half), F32),
    )
    return call(project_kernel, "project", shapes, (core.reshape(1),), tokens, weights)


def forward_kernel(q_ref, kv_ref, segq_ref, segk_ref, out_ref, low_ref, lse_ref):
    half, width = q_ref.shape
    for first in range(0, half, QUERY_ROWS):
        rows = slice(first, first + QUERY_ROWS)
        end = half + first + QUERY_ROWS
        allowed = allowed_pairs(segq_ref[rows, :], segk_ref[:, :end], half, first, QUERY_ROWS)
        outs, lses = [], []
        for head in range(width // HD):
            cols = slice(head * HD, (head + 1) * HD)
            value_cols = slice(width + head * HD, width + (head + 1) * HD)
            scores = jnp.where(allowed, nt(q_ref[rows, cols], kv_ref[:end, cols]), MASKED)
            top = jnp.max(scores, axis=1, keepdims=True)
            exps = jnp.exp(scores - top)
            total = jnp.sum(exps, axis=1, keepdims=True)
            probs = (exps * (1.0 / total)).astype(BF16)
            outs.append(nn(probs, kv_ref[:end, value_cols]))
            lses.append(top + jnp.log(total))
        out = jnp.concatenate(outs, axis=1)
        out_ref[rows, :] = out
        low_ref[rows, :] = out.astype(BF16)
        lse_ref[rows, :] = jnp.concatenate(lses, axis=1)


def attention_forward(q, kv, segq, segk):
    shapes = (
        shaped(q.shape, F32),
        shaped(q.shape, BF16),
        shaped((q.shape[0], q.shape[1] // HD), F32),
    )
    return call(forward_kernel, "attention_forward", shapes, (), q, kv, segq, segk)


def backward_kernel(first_head, last_head, *refs):
    q_ref, kv_ref, go_ref, out_ref, lse_ref, segq_ref, segk_ref, raw_ref, scale_ref = refs[:9]
    dq_ref, dkv_ref, sum_ref = refs[9:]
    half, width = q_ref.shape
    heads = range(first_head, last_head)
    span = slice(first_head * HD, last_head * HD)
    dks, dvs = [None] * len(heads), [None] * len(heads)
    sums = 0.0
    for first in reversed(range(0, half, QUERY_ROWS)):
        rows = slice(first, first + QUERY_ROWS)
        end = half + first + QUERY_ROWS
        allowed = allowed_pairs(segq_ref[rows, :], segk_ref[:, :end], half, first, QUERY_ROWS)
        products = go_ref[rows, :].astype(F32) * out_ref[rows, :]
        dqs = []
        for number, head in enumerate(heads):
            cols = slice(head * HD, (head + 1) * HD)
            value_cols = slice(width + head * HD, width + (head + 1) * HD)
            queries, keys, values = q_ref[rows, cols], kv_ref[:end, cols], kv_ref[:end, value_cols]
            grads = go_ref[rows, cols]
            scores = jnp.where(allowed, nt(queries, keys), MASKED)
            probs = jnp.exp(scores - lse_ref[rows, head : head + 1])
            delta = jnp.sum(products[:, cols], axis=1, keepdims=True)
            grad_scores = (probs * (nt(grads, values) - delta)).astype(BF16)
            dqs.append(nn(grad_scores, keys))
            for sums_of, term in (
                (dks, tn(grad_scores, queries)),
                (dvs, tn(probs.astype(BF16), grads)),
            ):
                held = sums_of[number]
                if held is None:
                    sums_of[number] = term
                else:
                    sums_of[number] = jnp.concatenate([held[:end] + term, held[end:]], axis=0)
        dq = jnp.concatenate(dqs, axis=1)
        sums = sums + jnp.sum(dq * raw_ref[rows, span], axis=0, keepdims=True)
        dq_ref[rows, :] = (dq * scale_ref[:, span]).astype(BF16)
    sum_ref[...] = sums
    dkv_ref[...] = jnp.concatenate(dks + dvs, axis=1).astype(BF16)


def attention_backward(first_head, last_head, q, kv, *rest):
    columns = (last_head - first_head) * HD
    shapes = (
        shaped((q.shape[0], columns), BF16),
        shaped((kv.shape[0], 2 * columns), BF16),
        shaped((1, columns), F32),
    )
    kernel = functools.partial(backward_kernel, first_head, last_head)
    return call(kernel, "attention_backward", shapes, (), q, kv, *rest)


def output_kernel(core_ref, attended_ref, weight_ref, own_ref, sent_ref):
    rows = own_ref.shape[0]
    for block in range(2):
        result = nn(attended_ref[block * rows : (block + 1) * rows, :], weight_ref[...])
        side = core_ref[0] ^ block

        def store(out_ref):
            out_ref[...] = result

        pl.when(side == 0)(functools.partial(store, own_ref))
        pl.when(side == 1)(functools.partial(store, sent_ref))


def output_project(core, attended, weight):
    shape = shaped((attended.shape[0] // 2, weight.shape[1]), F32)
    return call(
        output_kernel, "output_project", (shape, shape), (core.reshape(1),), attended, weight
    )


def norm_kernel(own_ref, came_ref, tokens_ref, gain_ref, hidden_ref, normed_ref):
    hidden = tokens_ref[...].astype(F32) + own_ref[...] + came_ref[...]
    hidden_ref[...] = hidden
    inverse = lax.rsqrt(jnp.mean(hidden * hidden, axis=1, keepdims=True) + EPSILON)
    normed_ref[...] = (hidden * inverse * gain_ref[...]).astype(BF16)


def norm_middle(own, came, tokens, gain):
    shapes = shaped(own.shape, F32), shaped(own.shape, BF16)
    return call(norm_kernel, "norm_middle", shapes, (), own, came, tokens, gain[None])


def mlp_kernel(*refs):
    normed_refs, upstream_refs = refs[:2], refs[2:4]
    gate_up_ref, down_ref, hidden_ref, gate_ref, up_ref, normed_ref, upstream_ref = refs[4:]
    half = hidden_ref.shape[1]
    count = normed_refs[0].shape[0]
    for block in range(2):
        rows = slice(block * count, (block + 1) * count)
        normed = normed_refs[block][...]
        normed_ref[rows, :] = normed
        upstream = upstream_refs[block][...]
        upstream_ref[rows, :] = upstream
        gate_up = nn(normed, gate_up_ref[...])
        gate, up = gate_up[:, :half], gate_up[:, half:]
        sigmoid = jax.nn.sigmoid(gate)
        hidden_ref[rows, :] = (gate * sigmoid * up).astype(BF16)
        grad = nt(upstream, down_ref[...])
        gate_ref[rows, :] = (
            grad * up * sigmoid * (1.0 + gate * (1.0 - sigmoid))
        ).astype(BF16)
        up_ref[rows, :] = (grad * gate * sigmoid).astype(BF16)


def mlp_middle(normed, upstream, gate_up, down):
    rows, width = normed[0].shape
    whole = shaped((2 * rows, width), BF16)
    columns = shaped((2 * rows, width // 2), BF16)
    shapes = columns, columns, columns, whole, whole
    return call(mlp_kernel, "mlp_middle", shapes, (), *normed, *upstream, gate_up, down)


def rows_kernel(transposed, *refs):
    *left_refs, right_ref, own_ref, sent_ref = refs
    rows = own_ref.shape[0]
    for block, out_ref in enumerate((own_ref, sent_ref)):
        total, start = 0.0, 0
        for left_ref in left_refs:
            left = left_ref[block * rows : (block + 1) * rows, :]
            if transposed:
                total = total + nt(left, right_ref[:, start : start + left.shape[1]])
            else:
                total = total + nn(left, right_ref[start : start + left.shape[1], :])
            start += left.shape[1]
        out_ref[...] = total


def rows_product(lefts, right, transposed, name):
    columns = right.shape[0] if transposed else right.shape[1]
    shape = shaped((lefts[0].shape[0] // 2, columns), F32)
    kernel = functools.partial(rows_kernel, transposed)
    return call(kernel, name, (shape, shape), (), *lefts, right)


def norm_back(values, gain, upstream):
    inverse = lax.rsqrt(jnp.mean(values * values, axis=1, keepdims=True) + EPSILON)
    scaled = upstream * gain
    back = inverse * scaled - values * inverse**3 * jnp.mean(values * scaled, axis=1, keepdims=True)
    return back, jnp.sum(upstream * values * inverse, axis=0, keepdims=True)


def middle_back_kernel(own_ref, came_ref, hidden_ref, upstream_ref, gain_ref, grad_ref, low_ref, sum_ref):
    back, sums = norm_back(hidden_ref[...], gain_ref[...], own_ref[...] + came_ref[...])
    grad = upstream_ref[...].astype(F32) + back
    grad_ref[...] = grad
    low_ref[...] = grad.astype(BF16)
    sum_ref[...] = sums


def middle_back(own, came, hidden, upstream, gain):
    shapes = shaped(own.shape, F32), shaped(own.shape, BF16), shaped((1, own.shape[1]), F32)
    return call(
        middle_back_kernel, "middle_back", shapes, (), own, came, hidden, upstream, gain[None]
    )


def attended_kernel(core_ref, own_ref, other_ref, weight_ref, grad_ref, rows_ref):
    rows = own_ref.shape[0]
    for block, ref in enumerate((own_ref, other_ref)):
        place = pl.ds(pl.multiple_of((core_ref[0] ^ block) * rows, rows), rows)
        grad_ref[place, :] = nt(ref[...], weight_ref[...]).astype(BF16)
        rows_ref[place, :] = ref[...]


def attended_back(core, own, other, weight):
    rows, width = own.shape
    shapes = shaped((2 * rows, weight.shape[0]), BF16), shaped((2 * rows, width), BF16)
    return call(
        attended_kernel, "attended_back", shapes, (core.reshape(1),), own, other, weight
    )


def gain_kernel(own_ref, came_ref, tokens_ref, before_ref, here_ref, sent_ref, sum_ref):
    total = 0.0
    for part, ref in enumerate((tokens_ref, before_ref)):
        grad = own_ref[part] + came_ref[part]
        values = ref[...].astype(F32)
        inverse = lax.rsqrt(jnp.mean(values * values, axis=1, keepdims=True) + EPSILON)
        total = total + jnp.sum(grad * values * inverse, axis=0, keepdims=True)
        if part == 0:
            here_ref[...] = grad
        else:
            sent_ref[...] = grad.astype(BF16)
    sum_ref[...] = total


def gain_terms(own, came, tokens, before):
    rows, width = tokens.shape
    shapes = shaped((rows, width), F32), shaped((rows, width), BF16), shaped((1, width), F32)
    return call(gain_kernel, "gain_terms", shapes, (), own, came, tokens, before)


def tokens_kernel(first_ref, here_ref, after_ref, tokens_ref, gain_ref, hidden_ref, out_ref):
    later = jnp.where(first_ref[0] == 0, after_ref[...].astype(F32), 0.0)
    back, _ = norm_back(tokens_ref[...].astype(F32), gain_ref[...], here_ref[...] + later)
    out_ref[...] = hidden_ref[...] + back


def tokens_back(first, here, after_rows, tokens, gain, grad_hidden):
    shape = shaped(here.shape, F32)
    arrays = here, after_rows, tokens, gain[None], grad_hidden
    return call(tokens_kernel, "tokens_back", shape, (first.reshape(1),), *arrays)


def pick(pair, index):
    return jnp.where(index == 0, pair[0], pair[1])


def in_order(own, other, index, axis):
    return jnp.where(
        index == 0,
        jnp.concatenate([own, other], axis=axis),
        jnp.concatenate([other, own], axis=axis),
    )


def block_of(matrix, index, size, axis=0):
    return lax.dynamic_slice_in_dim(matrix, index * size, size, axis)


def across(value, axis, bit):
    count = lax.axis_size(axis)
    return lax.ppermute(value, axis, [(place, place ^ bit) for place in range(count)])


def line_bits(count):
    return [1 << power for power in range(count.bit_length() - 1)]


def after(values, *earlier):
    return lax.optimization_barrier((values, earlier))[0]


def gather_far(block, far, before=(), then=()):
    held = block[None]
    arrived = ()
    for axis, bit in far:
        sent = after(held, *before) if before else held
        arrived = (across(sent, axis, bit),)
        held = jnp.concatenate([held, after(arrived[0], *then) if then else arrived[0]], axis=0)
    return held, arrived


def join_kernel(starts, *refs):
    count = len(refs) // 3
    for number, start in enumerate(starts):
        first_ref, second_ref, out_ref = refs[number], refs[count + number], refs[2 * count + number]
        size, _, columns = first_ref.shape
        out_ref[:size] = first_ref[...]
        out_ref[size:] = second_ref[start : start + size, :, :columns]


def join(firsts, seconds, starts):
    shapes = [shaped((2 * first.shape[0],) + first.shape[1:], first.dtype) for first in firsts]
    kernel = functools.partial(join_kernel, starts)
    return call(kernel, "join", shapes, (), *firsts, *seconds)


class Chain:
    def __init__(self, held, order, step):
        self.sides = held.shape[1]
        self.held, self.last, self.start = None, held.reshape((-1,) + held.shape[2:]), 0
        self.order, self.step = order, step


def take_all(chains, *earlier):
    lasts = [after(chain.last, *earlier) if earlier else chain.last for chain in chains]
    if chains[0].held is None:
        helds = lasts
    else:
        starts = [chain.start for chain in chains]
        helds = join([chain.held for chain in chains], lasts, starts)
    for chain, held in zip(chains, helds):
        chain.held, chain.start = held, 0


def advance_all(chains, *earlier):
    take_all(chains, *earlier)
    for chain in chains:
        chain.last = across(chain.held, *chain.order[chain.step])
        chain.step += 1
    return [chain.last for chain in chains]


def together_kernel(count, *refs):
    for number in range(count):
        first_ref, second_ref, short_ref, out_ref = refs[number::count]
        size = first_ref.shape[0]
        out_ref[:size] = first_ref[...]
        out_ref[size : 2 * size] = second_ref[...]
        out_ref[2 * size :, :, : short_ref.shape[2]] = short_ref[...]


def advance_together(longs, shorts):
    take_all(shorts)
    shapes = [
        shaped((2 * long.held.shape[0] + short.held.shape[0],) + long.held.shape[1:], BF16)
        for long, short in zip(longs, shorts)
    ]
    arrays = [long.held for long in longs] + [long.last for long in longs]
    arrays += [short.held for short in shorts]
    kernel = functools.partial(together_kernel, len(longs))
    messages = call(kernel, "together", shapes, (), *arrays)
    for long, short, message in zip(longs, shorts, messages):
        came = across(message, *long.order[long.step])
        count = 2 * long.held.shape[0]
        long.held, long.last, long.count = message, came, count
        short.last, short.start = came, count
        long.step += 1
        short.step += 1


def layout_kernel(plans, count_out, place_ref, *refs):
    out_refs = refs[-count_out:]
    for source, (line, sides, count, columns, steps, base, placed) in enumerate(plans):
        devices = 4 * line
        for index in range(count // sides):
            flips = dict(base)
            for power, (axis, bit) in enumerate(steps):
                if index >> power & 1:
                    flips[axis] = flips.get(axis, 0) ^ bit
            for number, by_column, side, core_flip, column in placed:
                strides = {"y": devices, "z": 2, "x": 1, "c": devices // 2}
                if not by_column:
                    strides["y"], strides["c"] = devices // 2, 0
                flips["c"] = core_flip
                target = 0
                for at, axis in enumerate(("y", "c", "z", "x")):
                    target += (place_ref[at] ^ flips.get(axis, 0)) * strides[axis]
                out_refs[number][target, :, column : column + columns] = refs[source][
                    index * sides + side, :, :columns
                ]


def layout_blocks(place, line, widths, chains):
    plans, sources = [], []
    for chain, columns, placed in chains:
        count = getattr(chain, "count", chain.held.shape[0])
        placed = [(number, widths[number][1], *rest) for number, *rest in placed]
        for base in ((), chain.order[-1:]):
            plans.append((line, chain.sides, count, columns, chain.order[:-1], base, placed))
        sources += [chain.held, chain.last]
    share = sources[0].shape[1]
    shapes = [
        shaped(((8 if by_column else 4) * line, share, width), BF16) for width, by_column in widths
    ]
    kernel = functools.partial(layout_kernel, plans, len(widths))
    outs = call(kernel, "layout_blocks", shapes, (place,), *sources)
    return [out.reshape(out.shape[0] * share, out.shape[2]) for out in outs]


def sides_kernel(core_ref, *refs):
    *weight_refs, vector_ref, attn_ref, gate_up_ref = refs
    share, width = weight_refs[0].shape
    half, quarter = width // 2, width // 4
    for number, weight_ref in enumerate(weight_refs):
        out_ref, column = (attn_ref, number) if number < 3 else (gate_up_ref, number - 3)
        for core in range(2):
            parts = [
                weight_ref[:, side * half + core * quarter : side * half + (core + 1) * quarter]
                for side in range(2)
            ]
            out_ref[core ^ core_ref[0], :, column * half : (column + 1) * half] = jnp.concatenate(
                parts, axis=1
            )
    for side in range(2):
        attn_ref[side, :, 3 * half :] = vector_ref[...]


def column_sides(core, weights, vectors):
    share, width = weights[0].shape
    shapes = (
        shaped((2, share, 3 * width // 2 + vectors.shape[1]), BF16),
        shaped((2, share, width), BF16),
    )
    return call(sides_kernel, "column_sides", shapes, (core.reshape(1),), *weights, vectors)


def products_kernel(plans, mine_ref, *refs):
    outputs = iter(refs[sum(lefts + rights for _, lefts, rights, _ in plans) :])
    at = 0
    for share, lefts, rights, chains in plans:
        left_refs, right_refs = refs[at : at + lefts], refs[at + lefts : at + lefts + rights]
        at += lefts + rights
        targets = [(next(outputs), next(outputs)) for _ in chains]
        size = left_refs[0].shape[1] // 2
        for row_side in range(2):
            parts = [left_ref[:, row_side * size : (row_side + 1) * size] for left_ref in left_refs]
            for (which, columns, places), (kept_ref, sent_ref) in zip(chains, targets):
                results = []
                for column in columns:
                    total, first = 0.0, 0
                    for left in parts:
                        right = right_refs[column][first : first + left.shape[0], :]
                        total = total + tn(left, right)
                        first += left.shape[0]
                    results.append(total)
                result = jnp.concatenate(results, axis=1)

                def store(mine):
                    for block in range(size // share):
                        digit, target = places[row_side * (size // share) + block]
                        out_ref = kept_ref if digit == mine else sent_ref
                        out_ref[target] = result[block * share : (block + 1) * share].astype(BF16)

                pl.when(mine_ref[which] == 0)(functools.partial(store, 0))
                pl.when(mine_ref[which] == 1)(functools.partial(store, 1))


def products(mine, share, groups):
    plans, inputs, shapes = [], [], []
    count = 0
    for lefts, rights, chains in groups:
        inputs += [*lefts, *rights]
        plan = []
        for columns, dims, digit in chains:
            places = []
            for block in range(lefts[0].shape[1] // share):
                index, rest = [], block
                for size in reversed(dims):
                    index.append(rest % size)
                    rest //= size
                index = index[::-1]
                value = index.pop(digit)
                flat = 0
                for size, digit_of in zip(dims[:digit] + dims[digit + 1 :], index):
                    flat = flat * size + digit_of
                places.append((value, flat))
            plan.append((count, columns, places))
            count += 1
            wide = sum(rights[column].shape[1] for column in columns)
            shape = (lefts[0].shape[1] // share // 2, share, wide)
            shapes += [shaped(shape, BF16)] * 2
        plans.append((share, len(lefts), len(rights), plan))
    kernel = functools.partial(products_kernel, plans)
    outs = call(kernel, "products", shapes, (mine,), *inputs)
    return list(zip(outs[::2], outs[1::2]))


def back_kernel(core_ref, *refs):
    grad_q_refs, grad_kv_refs = refs[:2], refs[2:4]
    weight_ref, own_ref, sent_ref = refs[4:]
    chip_rows, quarter = grad_q_refs[0].shape
    rows = chip_rows // 2

    def keys_values(span):
        total = 0.0
        for part, ref in enumerate(grad_kv_refs):
            for side in range(2):
                first = (2 + 2 * side + part) * quarter
                grads = ref[span, side * quarter : (side + 1) * quarter]
                total = total + nt(grads, weight_ref[:, first : first + quarter])
        return total

    for block in range(2):
        span = slice(block * rows, (block + 1) * rows)
        here = keys_values(slice(chip_rows + block * rows, chip_rows + (block + 1) * rows))
        for part, ref in enumerate(grad_q_refs):
            here = here + nt(ref[span, :], weight_ref[:, part * quarter : (part + 1) * quarter])
        before = keys_values(span)
        side = core_ref[0] ^ block

        def store(out_ref):
            out_ref[0] = here
            out_ref[1] = before

        pl.when(side == 0)(functools.partial(store, own_ref))
        pl.when(side == 1)(functools.partial(store, sent_ref))


def back_project(core, grad_q, grad_kv, weights):
    shape = shaped((2, grad_q[0].shape[0] // 2, weights.shape[0]), F32)
    arrays = *grad_q, *grad_kv, weights
    return call(back_kernel, "back_project", (shape, shape), (core.reshape(1),), *arrays)


def step_kernel(plans, mine_ref, *refs):
    for number, plan in enumerate(plans):
        held_ref, came_ref = refs[plan["held"]], refs[plan["came"]]
        count, share, columns = held_ref.shape
        came_at, came_column = plan["came_at"]
        sent_at, sent_column = plan["sent_at"]

        def store(mine):
            for index in range(count):
                value = held_ref[index].astype(F32) + came_ref[
                    came_at + index, :share, came_column : came_column + columns
                ].astype(F32)
                digit, target = plan["places"][index]
                if digit == mine:
                    kept_ref = refs[plan["kept"]]
                    kept_ref[target] = value.astype(kept_ref.dtype)
                else:
                    sent_ref = refs[plan["sent"]]
                    sent_ref[sent_at + target, :share, sent_column : sent_column + columns] = (
                        value.astype(sent_ref.dtype)
                    )

        if plan["digit"] is None:
            store(0)
        else:
            pl.when(mine_ref[plan["digit"]] == 0)(functools.partial(store, 0))
            pl.when(mine_ref[plan["digit"]] == 1)(functools.partial(store, 1))


def finish_kernel(plans, core_ref, *refs):
    *own_refs, other_ref = refs[: -len(plans)]
    first_core = core_ref[0] == 0
    for plan, out_ref in zip(plans, refs[-len(plans) :]):
        for side, (source, column, other_column) in enumerate(plan):
            half = out_ref.shape[1] // 2
            own = own_refs[source][:, column : column + half // 2]
            other = other_ref[:, other_column : other_column + half // 2]
            pair = [jnp.where(first_core, own, other), jnp.where(first_core, other, own)]
            out_ref[:, side * half : (side + 1) * half] = jnp.concatenate(pair, axis=1)


def finish_columns(core, own, other, half, mixed):
    quarter = half // 2
    plans = []
    for index in range(len(own)):
        sources = [index, index]
        columns = [0, quarter]
        if mixed and index >= len(own) - 2:
            sources = [len(own) - 2, len(own) - 1]
            columns = [(index - len(own) + 2) * quarter] * 2
        plans.append([(s, col, s * half + col) for s, col in zip(sources, columns)])
    shapes = [shaped((own[0].shape[0], 2 * half), F32)] * len(own)
    kernel = functools.partial(finish_kernel, plans)
    return call(kernel, "finish_columns", shapes, (core.reshape(1),), *own, other)


def local(
    tokens,
    lengths,
    norm_attn,
    norm_mlp,
    query_scale,
    query_proj,
    key_proj,
    value_proj,
    output_proj,
    gate_proj,
    up_proj,
    down_proj,
    cotangent,
):
    place = {name: lax.axis_index(name) for name in ("y", "c", "z", "x")}
    y, c, x = place["y"], place["c"], place["x"]
    line = lax.axis_size("z")
    bits = line_bits(line)
    rows = tokens.shape[1]
    share, width = query_proj.shape
    half = width // 2
    quarter = width // 4
    chip_rows = 2 * rows
    length = 4 * rows

    near = ("z", 1)
    far = [("z", bit) for bit in reversed(bits[1:])]
    orders = (
        far + [("x", 1), ("y", 1), near],
        far + [("y", 1), near, ("x", 1)],
        far + [near, ("x", 1), ("y", 1)],
    )
    vector_columns = jnp.pad(
        jnp.stack([norm_attn, norm_mlp, query_scale], axis=1), ((0, 0), (0, 125))
    )
    attn_block, gate_up_block = column_sides(
        c, (query_proj, key_proj, value_proj, gate_proj, up_proj), vector_columns
    )
    own_tokens = tokens[0]
    other_tokens = across(own_tokens, "c", 1)
    other_cotangent = across(cotangent[0], "c", 1)
    before = across(own_tokens, "y", 1)
    other_before = across(before, "c", 1)
    chip_tokens = in_order(own_tokens, other_tokens, c, 0)
    chip_before = in_order(before, other_before, c, 0)
    all_tokens = jnp.concatenate([chip_before, chip_tokens], axis=0)

    attn_far, first = gather_far(attn_block, far, (), (other_tokens, other_cotangent, before))

    def swap_sides(blocks):
        return jnp.stack([blocks[:, 0], across(blocks[:, 1], "c", 1)], axis=1)

    attn_sides = swap_sides(attn_far)
    cuts = (0, half, 2 * half, 3 * half + 128)
    attn_chains = [
        Chain(attn_sides[..., cut:end], order, len(far))
        for cut, end, order in zip(cuts, cuts[1:], orders)
    ]
    places_now = jnp.stack([place[name] for name in ("y", "c", "z", "x")])
    advance_all(attn_chains)
    gate_up_far, middle = gather_far(gate_up_block, far, first, ())
    third = advance_all(attn_chains, other_before, *middle)
    rows_far, _ = gather_far(jnp.stack([output_proj, down_proj]), far, middle, third)
    gate_up_sides = swap_sides(gate_up_far)
    mlp_chains = [
        Chain(
            jnp.concatenate(
                [gate_up_sides[..., cut : cut + half], rows_far[:, 1:, :, cut : cut + half]], axis=1
            ),
            order,
            len(far),
        )
        for cut, order in zip((0, half), orders)
    ]
    output_sides = jnp.stack([rows_far[:, 0, :, :half], rows_far[:, 0, :, half:]], axis=1)
    mlp_chains.append(Chain(output_sides, orders[2], len(far)))
    advance_together(attn_chains[1:] + attn_chains[:1], mlp_chains)
    advance_all(mlp_chains)

    doc_ends = jnp.cumsum(lengths[0])
    places = jnp.arange(length, dtype=jnp.int32)
    segment = jnp.sum((places[:, None] >= doc_ends[None, :]).astype(jnp.int32), axis=1)
    seg_here = block_of(segment, y, chip_rows)
    seg_before = jnp.where(y == 0, -1, segment[:chip_rows])
    seg_keys = jnp.concatenate([seg_before, seg_here])[None]
    seg_rows = seg_here[:, None]
    first_row = y * chip_rows + jnp.arange(rows, dtype=jnp.int32)
    upstream = [
        jnp.where((first_row + core * rows < doc_ends[-1])[:, None], rows_of, 0).astype(BF16)
        for core, rows_of in ((c, cotangent[0]), (1 - c, other_cotangent))
    ]
    both = ((0, 0), (1, 1))
    (attn_weights,) = layout_blocks(
        places_now,
        line,
        [(3 * half + 128, True)],
        [
            (chain, end - cut, [(0, side, flip, cut) for side, flip in both])
            for chain, cut, end in zip(attn_chains, cuts, cuts[1:])
        ],
    )
    mlp_last = advance_all(mlp_chains, attn_weights)
    attn_weights = after(attn_weights, *[chain.held for chain in mlp_chains])
    q_raw, queries, keys_values, normed_before, normed_here, vectors, scale_rows = project(
        c, all_tokens, attn_weights
    )
    gain_a, gain_m = vectors[0], vectors[1]
    attended_f, attended, lse = attention_forward(queries, keys_values, seg_rows, seg_keys)
    attended = after(attended, *mlp_last)
    for chain in mlp_chains:
        chain.last = after(chain.last, attended)

    (proj_o,) = layout_blocks(
        places_now,
        line,
        [(width, False)],
        [(mlp_chains[2], half, [(0, 0, 0, 0), (0, 1, 0, half)])],
    )
    output_own, output_sent = output_project(c, attended, proj_o)
    hidden1, normed_own = norm_middle(
        output_own, across(output_sent, "c", 1), own_tokens, gain_m
    )
    normed_other = across(normed_own, "c", 1)
    for chain in mlp_chains[:2]:
        chain.last = after(chain.last, output_sent)
    proj_gu, proj_d = layout_blocks(
        places_now,
        line,
        [(width, True), (width, False)],
        [
            (chain, half, [(0, side, flip, cut) for side, flip in both] + [(1, 2, 0, cut)])
            for chain, cut in zip(mlp_chains, (0, half))
        ],
    )
    hidden, grad_gate, grad_up, normed_m, upstream_b = mlp_middle(
        (normed_own, normed_other), upstream, proj_gu, proj_d
    )

    digits = [("y", 1), ("c", 1)] + [("z", bit) for bit in reversed(bits)] + [("x", 1)]
    scatter_orders = [order[len(far) :][::-1] for order in orders]

    def own_digit(axis, bit):
        return (place[axis] // bit) % 2

    def sizes_of(names, by_column):
        return tuple(1 if name == ("c", 1) and not by_column else 2 for name in names)

    def first_step(*groups, gate=()):
        mine, plans, states = [], [], []
        for lefts, rights, columns, chain_orders in groups:
            by_column = lefts[0].shape[1] == width
            dims = sizes_of(digits, by_column)
            chains = []
            for which, order in zip(columns, chain_orders):
                at = digits.index(order[0])
                chains.append((which, dims, at))
                mine.append(own_digit(*order[0]))
                names = digits[:at] + digits[at + 1 :]
                states.append({"names": names, "by_column": by_column, "order": order, "step": 1})
            plans.append((lefts, rights, chains))
        if share % 8 == 0:
            parts = products(jnp.stack(mine).astype(jnp.int32), share, plans)
        else:
            parts = []
            for lefts, rights, chains in plans:
                left = jnp.concatenate(lefts, axis=0)
                for which, dims, at in chains:
                    right = jnp.concatenate([rights[column] for column in which], axis=1)
                    part = tn(left, right).astype(BF16).reshape(dims + (share, right.shape[1]))
                    digit = mine[len(parts)]
                    parts.append(
                        [
                            lax.dynamic_index_in_dim(part, which_half, at, keepdims=False).reshape(
                                -1, share, right.shape[1]
                            )
                            for which_half in (digit, 1 - digit)
                        ]
                    )
        sent = [after(value, *gate) if gate else value for _, value in parts]
        for state, (kept, _), value in zip(states, parts, sent):
            state.update(held=kept, came=across(value, *state["order"][0]), came_at=(0, 0))
        return states, [value for _, value in parts]

    def step(states, names, *earlier, packed=None, dtype=BF16):
        mine, plans, inputs, shapes = [], [], [], []
        came = [after(state["came"], *earlier) if earlier else state["came"] for state in states]
        sources = {}
        for state, array in zip(states, came):
            key = id(state["came"])
            if key not in sources:
                sources[key] = len(inputs)
                inputs.append(array)
        new_states = []
        for number, (state, name) in enumerate(zip(states, names)):
            dims = sizes_of(state["names"], state["by_column"])
            held = state["held"]
            plan = {"came": sources[id(state["came"])], "came_at": state["came_at"]}
            plan["held"] = len(inputs)
            inputs.append(held)
            at = state["names"].index(name) if name in state["names"] else None
            if at is not None and dims[at] == 1:
                at = None
            rest = [index for index in range(len(dims)) if index != at]
            places = []
            for index in range(held.shape[0]):
                values, left_over = [], index
                for size in reversed(dims):
                    values.append(left_over % size)
                    left_over //= size
                values = values[::-1]
                flat = 0
                for axis_at in rest:
                    flat = flat * dims[axis_at] + values[axis_at]
                places.append((0 if at is None else values[at], flat))
            plan["places"] = places
            plan["digit"] = None if at is None else len(mine)
            if at is not None:
                mine.append(own_digit(*name))
            plan["sent_at"] = packed[1][number] if packed else (0, 0)
            plan["kept"] = len(shapes)
            count = held.shape[0] // (1 if at is None else 2)
            shapes.append(shaped((count,) + held.shape[1:], F32))
            if at is not None and not packed:
                plan["sent"] = len(shapes)
                shapes.append(shaped((count,) + held.shape[1:], dtype))
            plans.append(plan)
            names_left = [state["names"][axis_at] for axis_at in rest]
            new_states.append(dict(state, names=names_left, came_at=plan["sent_at"]))
        if packed:
            for plan in plans:
                plan["sent"] = len(shapes)
            shapes.append(shaped(packed[0], dtype))
        for plan in plans:
            plan["kept"] += 1 + len(inputs) - 1
            if "sent" in plan:
                plan["sent"] += len(inputs)
        if not mine:
            mine = [place["c"]]
        kernel = functools.partial(step_kernel, plans)
        outs = call(kernel, "step", shapes, (jnp.stack(mine).astype(jnp.int32),), *inputs)
        for plan, state in zip(plans, new_states):
            state["held"] = outs[plan["kept"] - len(inputs)]
        if packed:
            return new_states, outs[-1]
        return new_states, [
            outs[plan["sent"] - len(inputs)] if plan["digit"] is not None else None
            for plan in plans
        ]

    def halve(states, *earlier):
        names = [state["order"][state["step"]] for state in states]
        states, sent = step(states, names, *earlier)
        for state, value, name in zip(states, sent, names):
            state.update(came=across(value, *name), came_at=(0, 0), step=state["step"] + 1)
        return states, sent

    def halve_far(states, shape, places, *earlier):
        for axis, bit in far[::-1][:-1]:
            states, sent = step(states, [(axis, bit)] * len(states))
            for state, value in zip(states, sent):
                state.update(came=across(value, axis, bit), came_at=(0, 0))
        last = far[0]
        states, message = step(states, [last] * len(states), *earlier, packed=(shape, places))
        arrived = across(message, *last)
        for state in states:
            state.update(came=arrived)
        return states, message

    def received(states):
        return [state["came"] for state in states]

    gate_own, gate_sent = rows_product((grad_gate, grad_up), proj_gu, True, "gate_up_back")
    mlp_states, mlp_sent = first_step(
        ((hidden,), (upstream_b,), ((0,),), scatter_orders[:1]),
        ((normed_m,), after((grad_gate, grad_up), gate_sent), ((0,), (1,)), scatter_orders[1:]),
    )
    gate_own = after(gate_own, *mlp_sent)
    grad_hidden1, low_own, grad_gain_m = middle_back(
        gate_own, across(gate_sent, "c", 1), hidden1, upstream[0], gain_m
    )
    grad_attended, grad_hidden1_b = attended_back(c, low_own, across(low_own, "c", 1), proj_o)
    scale_row = scale_rows[:1]
    heads = half // HD
    residuals = (queries, keys_values), (attended_f, lse, seg_rows, seg_keys, q_raw, scale_row)
    grad_q_early, grad_kv_early, early_sums = attention_backward(
        0, heads // 2, *residuals[0], grad_attended, *residuals[1]
    )
    mlp_states, mlp_sent = halve(mlp_states, grad_kv_early)
    grad_rows = after(grad_hidden1_b, grad_kv_early)
    output_rights = grad_rows[:, :half], grad_rows[:, half:]
    output_states, output_sent = first_step(
        ((attended,), output_rights, ((0,), (1,)), scatter_orders[1:])
    )
    grad_attended = after(grad_attended, *mlp_sent, *output_sent)
    grad_q_late, grad_kv_late, late_sums = attention_backward(
        heads // 2, heads, *residuals[0], grad_attended, *residuals[1]
    )
    grad_scale = jnp.concatenate([early_sums[0], late_sums[0]]) * scale_rows[1]
    grads = (grad_q_early, grad_q_late), (grad_kv_early, grad_kv_late)
    mlp_states, mlp_sent = halve(mlp_states, grad_kv_late)
    output_states, output_sent = halve(output_states, grad_kv_late)
    grads = after(grads, *mlp_sent, *output_sent)
    attn_states, attn_sent = first_step(
        ((normed_here,), grads[0], ((0, 1),), scatter_orders[:1]),
        ((normed_before, normed_here), grads[1], ((0,), (1,)), scatter_orders[1:]),
        gate=received(mlp_states + output_states),
    )
    first_done = received(attn_states)
    mlp_states, _ = halve_far(
        mlp_states, (3, share, width), ((2, 0), (0, 0), (0, half)), *attn_sent
    )
    output_states, _ = halve(output_states, *first_done)
    attn_states, attn_sent = halve(attn_states, mlp_states[0]["came"])
    second_done = received(attn_states)
    grads = after(grads, *attn_sent)
    back_own, back_sent = back_project(c, *grads, attn_weights)
    grad_here, grad_before, grad_gain_a = gain_terms(
        back_own, across(back_sent, "c", 1), own_tokens, before
    )
    attn_states, _ = halve(attn_states, grad_before, *received(output_states))
    third_done = received(attn_states)
    scale_rows = grad_scale.reshape(2, 1, quarter)
    scale_rows = jnp.where(
        c == 0,
        jnp.pad(scale_rows, ((0, 0), (0, 1), (0, 0))),
        jnp.pad(scale_rows, ((0, 0), (1, 0), (0, 0))),
    ).reshape(width)
    vector_terms = jnp.stack([grad_gain_a[0], grad_gain_m[0], scale_rows])
    vector_rows = min(8, share)
    vector_terms = jnp.moveaxis(vector_terms.reshape(3, -1, share), 0, 1)
    room = ((0, 0), (0, vector_rows - 3), (0, 128 - share))
    vector_terms = jnp.pad(vector_terms, room)
    vector_order = far[::-1] + [("y", 1), ("x", 1), near]
    vector_state = {"names": digits, "by_column": True, "order": vector_order, "step": 0}
    zero_terms = jnp.zeros(vector_terms.shape, BF16)
    vector_states = [dict(vector_state, held=vector_terms, came=zero_terms, came_at=(0, 0))]
    for _ in far:
        vector_states, _ = halve(vector_states)
    vector_states, _ = halve(vector_states, *third_done)
    vector_first = received(vector_states)
    grad_after = across(after(grad_before, *vector_first), "y", 1)
    grad_inputs = tokens_back(y, grad_here, grad_after, own_tokens, gain_a, grad_hidden1)

    attn_places = [(0, number * half) for number in range(3)]
    final_states, final_message = halve_far(
        attn_states + output_states,
        (3, share, 3 * half),
        attn_places + [(2, 0), (2, half)],
    )
    vector_states, _ = halve(vector_states)
    vector_second = received(vector_states)
    mlp_states, sent = step(
        mlp_states,
        [("c", 1)] * 3,
        final_message,
        packed=((1, share, width), ((0, 0), (0, 0), (0, half))),
        dtype=F32,
    )
    mlp_parts = [state["held"][0] for state in mlp_states]
    gate_up_other = across(sent[0], "c", 1)
    gate_up_grads = finish_columns(c, mlp_parts[1:], gate_up_other, half, False)
    down_own, down_sent = rows_product(
        (after(hidden, final_message),), proj_d, False, "down_project"
    )
    down_other = across(down_sent, "c", 1)
    block_out = hidden1 + down_own + down_other
    final_states, sent = step(
        final_states,
        [("c", 1)] * 5,
        grad_inputs,
        *gate_up_grads,
        block_out,
        *vector_second,
        packed=((1, share, 3 * half), attn_places + [(0, 0)] * 2),
        dtype=F32,
    )
    own_parts = [state["held"][0] for state in final_states]
    other = across(sent[0], "c", 1)
    attn_grads = finish_columns(c, own_parts[:3], other, half, True)
    vector_states, _ = halve(vector_states)
    vector_states, vector_sent = step(vector_states, [("c", 1)], dtype=F32)
    vector_other = across(vector_sent[0][0], "c", 1)
    summed = (vector_states[0]["held"][0] + vector_other)[:, :share]
    return (
        block_out.astype(BF16)[None],
        grad_inputs[None],
        summed[0],
        summed[1],
        summed[2],
        *attn_grads,
        jnp.concatenate(own_parts[3:], axis=1),
        *gate_up_grads,
        mlp_parts[0],
    )


def solution(mesh):
    seq, dp = mesh.devices.shape
    axes = Mesh(mesh.devices.reshape(seq // 2, 2, dp // 2, 2), ("y", "c", "z", "x"))
    batch, places, every = ("z", "x"), ("y", "c"), ("y", "c", "z", "x")
    activations = P(batch, places, None)
    vector, matrix = P(every), P(every, None)
    return jax.shard_map(
        local,
        mesh=axes,
        in_specs=(activations, P(batch, None)) + (vector,) * 3 + (matrix,) * 7 + (activations,),
        out_specs=(activations, activations) + (vector,) * 3 + (matrix,) * 7,
        check_vma=False,
    )
```

```python
import functools

import jax
import jax.numpy as jnp
from jax import lax
from jax.experimental import pallas as pl
from jax.experimental.pallas import tpu as pltpu
from jax.sharding import Mesh, PartitionSpec as P

H = 16
HD = 80
EPSILON = 1e-06
R_SOFTPLUS = 1.442695041
MASKED = -1e30
QUERY_ROWS = 256
VMEM_BYTES = 16 << 20
VMEM_MOST = 56 << 20
SPEED = 4600000000
COSTS = {
    "project": 5, "attention_forward": 13, "output_project": 3, "mlp_middle": 3, "gate_up_back": 3,
    "products": 6, "attention_backward": 10, "back_project": 0, "join": 3, "tokens_back": 3,
}
F32 = jnp.float32
BF16 = jnp.bfloat16


def nn(left, right):
    return jnp.dot(left, right, preferred_element_type=F32)


def nt(left, right):
    return lax.dot_general(left, right, (((1,), (1,)), ((), ())), preferred_element_type=F32)


def tn(left, right):
    return lax.dot_general(left, right, (((0,), (0,)), ((), ())), preferred_element_type=F32)


def allowed_pairs(seg_rows, seg_keys, half, first, rows):
    total = seg_keys.shape[1]
    row_ids = lax.broadcasted_iota(jnp.int32, (rows, total), 0) + (first + half)
    col_ids = lax.broadcasted_iota(jnp.int32, (rows, total), 1)
    return (seg_rows == seg_keys) & (col_ids <= row_ids)


WHOLE = pl.BlockSpec(memory_space=pltpu.VMEM)
SCALARS = pl.BlockSpec(memory_space=pltpu.SMEM)
ANYWHERE = pl.BlockSpec(memory_space=pl.ANY)


def call(kernel, name, out_shape, scalars, *arrays, scratch=()):
    specs = [SCALARS] * len(scalars) + [ANYWHERE if scratch else WHOLE] * len(arrays)
    return pl.pallas_call(
        kernel,
        out_shape=out_shape,
        in_specs=specs,
        out_specs=jax.tree.map(lambda shape: WHOLE, out_shape),
        compiler_params=pltpu.CompilerParams(vmem_limit_bytes=VMEM_MOST if scratch else VMEM_BYTES),
        scratch_shapes=scratch,
        cost_estimate=pl.CostEstimate(flops=COSTS.get(name, 2) * SPEED, bytes_accessed=0, transcendentals=0),
        name=name,
    )(*scalars, *arrays)


def shaped(shape, dtype):
    return jax.ShapeDtypeStruct(tuple(shape), dtype)


def project_kernel(
    core_ref, tokens_ref, weight_ref, raw_ref, q_ref, kv_ref, before_ref, here_ref, vectors_ref,
    scale_ref
):
    chip_rows, half = raw_ref.shape
    quarter = half // 2
    vectors = weight_ref[:, half : half + 128].astype(F32).T[:8]
    keys = half + 128
    vectors_ref[...] = vectors
    gain = vectors[0:1]
    logits = [
        jnp.concatenate(
            [vectors[2:3, side * half + core * quarter :][:, :quarter] for side in range(2)], axis=1
        )
        for core in range(2)
    ]
    logit = jnp.where(core_ref[0] == 0, logits[0], logits[1])
    softplus = jnp.maximum(logit, 0.0) + jnp.log1p(jnp.exp(-jnp.abs(logit)))
    scale = R_SOFTPLUS * HD ** (-0.5) * softplus
    scale_ref[0:1] = scale
    scale_ref[1:2] = R_SOFTPLUS * HD ** (-0.5) / (1.0 + jnp.exp(-logit))
    for first in range(0, 2 * chip_rows, QUERY_ROWS):
        rows = slice(first, first + QUERY_ROWS)
        values = tokens_ref[rows, :].astype(F32)
        inverse = lax.rsqrt(jnp.mean(values * values, axis=1, keepdims=True) + EPSILON)
        normed = (values * inverse * gain).astype(BF16)
        kv_ref[rows, :] = nn(normed, weight_ref[:, keys : keys + 2 * half]).astype(BF16)
        if first >= chip_rows:
            here = slice(first - chip_rows, first - chip_rows + QUERY_ROWS)
            here_ref[here, :] = normed
            raw = nn(normed, weight_ref[:, :half])
            raw_ref[here, :] = raw
            q_ref[here, :] = (raw * scale).astype(BF16)
        else:
            before_ref[rows, :] = normed


def project(core, tokens, weights):
    rows, width = tokens.shape
    half = width // 2
    shapes = (
        shaped((rows // 2, half), F32),
        shaped((rows // 2, half), BF16),
        shaped((rows, width), BF16),
        shaped((rows // 2, width), BF16),
        shaped((rows // 2, width), BF16),
        shaped((8, width), F32),
        shaped((2, half), F32),
    )
    return call(project_kernel, "project", shapes, (core.reshape(1),), tokens, weights)


def key_value_columns(head, width):
    half = width // 2
    start = head * HD // half * width + head * HD % half
    return slice(start, start + HD), slice(start + half, start + half + HD)


def forward_kernel(q_ref, kv_ref, segq_ref, segk_ref, out_ref, low_ref, lse_ref):
    half, width = q_ref.shape
    for first in range(0, half, QUERY_ROWS):
        rows = slice(first, first + QUERY_ROWS)
        end = half + first + QUERY_ROWS
        allowed = allowed_pairs(segq_ref[rows, :], segk_ref[:, :end], half, first, QUERY_ROWS)
        outs, lses = [], []
        for head in range(width // HD):
            cols = slice(head * HD, (head + 1) * HD)
            key_cols, value_cols = key_value_columns(head, width)
            scores = jnp.where(allowed, nt(q_ref[rows, cols], kv_ref[:end, key_cols]), MASKED)
            top = jnp.max(scores, axis=1, keepdims=True)
            exps = jnp.exp(scores - top)
            total = jnp.sum(exps, axis=1, keepdims=True)
            probs = (exps * (1.0 / total)).astype(BF16)
            outs.append(nn(probs, kv_ref[:end, value_cols]))
            lses.append(top + jnp.log(total))
        out = jnp.concatenate(outs, axis=1)
        out_ref[rows, :] = out
        low_ref[rows, :] = out.astype(BF16)
        lse_ref[rows, :] = jnp.concatenate(lses, axis=1)


def attention_forward(q, kv, segq, segk):
    shapes = (
        shaped(q.shape, F32),
        shaped(q.shape, BF16),
        shaped((q.shape[0], q.shape[1] // HD), F32),
    )
    return call(forward_kernel, "attention_forward", shapes, (), q, kv, segq, segk)


def backward_kernel(first_head, last_head, *refs):
    q_ref, kv_ref, go_ref, out_ref, lse_ref, segq_ref, segk_ref, raw_ref, scale_ref = refs[:9]
    dq_ref, dkv_ref, sum_ref = refs[9:]
    half, width = q_ref.shape
    heads = range(first_head, last_head)
    span = slice(first_head * HD, last_head * HD)
    dks, dvs = [None] * len(heads), [None] * len(heads)
    sums = 0.0
    for first in reversed(range(0, half, QUERY_ROWS)):
        rows = slice(first, first + QUERY_ROWS)
        end = half + first + QUERY_ROWS
        allowed = allowed_pairs(segq_ref[rows, :], segk_ref[:, :end], half, first, QUERY_ROWS)
        products = go_ref[rows, :].astype(F32) * out_ref[rows, :]
        dqs = []
        for number, head in enumerate(heads):
            cols = slice(head * HD, (head + 1) * HD)
            key_cols, value_cols = key_value_columns(head, width)
            queries, keys = q_ref[rows, cols], kv_ref[:end, key_cols]
            values = kv_ref[:end, value_cols]
            grads = go_ref[rows, cols]
            scores = jnp.where(allowed, nt(queries, keys), MASKED)
            probs = jnp.exp(scores - lse_ref[rows, head : head + 1])
            delta = jnp.sum(products[:, cols], axis=1, keepdims=True)
            grad_scores = (probs * (nt(grads, values) - delta)).astype(BF16)
            dqs.append(nn(grad_scores, keys))
            for sums_of, term in (
                (dks, tn(grad_scores, queries)),
                (dvs, tn(probs.astype(BF16), grads)),
            ):
                held = sums_of[number]
                if held is None:
                    sums_of[number] = term
                else:
                    sums_of[number] = jnp.concatenate([held[:end] + term, held[end:]], axis=0)
        dq = jnp.concatenate(dqs, axis=1)
        sums = sums + jnp.sum(dq * raw_ref[rows, span], axis=0, keepdims=True)
        dq_ref[rows, :] = (dq * scale_ref[:, span]).astype(BF16)
    sum_ref[...] = sums
    dkv_ref[...] = jnp.concatenate(dks + dvs, axis=1).astype(BF16)


def attention_backward(first_head, last_head, q, kv, *rest):
    columns = (last_head - first_head) * HD
    shapes = (
        shaped((q.shape[0], columns), BF16),
        shaped((kv.shape[0], 2 * columns), BF16),
        shaped((1, columns), F32),
    )
    kernel = functools.partial(backward_kernel, first_head, last_head)
    return call(kernel, "attention_backward", shapes, (), q, kv, *rest)


def output_kernel(core_ref, attended_ref, weight_ref, own_ref, sent_ref):
    rows = own_ref.shape[0]
    for block in range(2):
        result = nn(attended_ref[block * rows : (block + 1) * rows, :], weight_ref[...])
        side = core_ref[0] ^ block

        def store(out_ref):
            out_ref[...] = result

        pl.when(side == 0)(functools.partial(store, own_ref))
        pl.when(side == 1)(functools.partial(store, sent_ref))


def output_project(core, attended, weight):
    shape = shaped((attended.shape[0] // 2, weight.shape[1]), F32)
    return call(
        output_kernel, "output_project", (shape, shape), (core.reshape(1),), attended, weight
    )


def norm_kernel(own_ref, came_ref, tokens_ref, gain_ref, hidden_ref, normed_ref):
    hidden = tokens_ref[...].astype(F32) + own_ref[...] + came_ref[...]
    hidden_ref[...] = hidden
    inverse = lax.rsqrt(jnp.mean(hidden * hidden, axis=1, keepdims=True) + EPSILON)
    normed_ref[...] = (hidden * inverse * gain_ref[...]).astype(BF16)


def norm_middle(own, came, tokens, gain):
    shapes = shaped(own.shape, F32), shaped(own.shape, BF16)
    return call(norm_kernel, "norm_middle", shapes, (), own, came, tokens, gain[None])


def mlp_kernel(*refs):
    normed_refs, upstream_refs = refs[:2], refs[2:4]
    gate_up_ref, down_ref, hidden_ref, gate_ref, up_ref, normed_ref, upstream_ref = refs[4:]
    half = hidden_ref.shape[1]
    count = normed_refs[0].shape[0]
    for block in range(2):
        rows = slice(block * count, (block + 1) * count)
        normed = normed_refs[block][...]
        normed_ref[rows, :] = normed
        upstream = upstream_refs[block][...]
        upstream_ref[rows, :] = upstream
        gate_up = nn(normed, gate_up_ref[...])
        gate, up = gate_up[:, :half], gate_up[:, half:]
        sigmoid = jax.nn.sigmoid(gate)
        hidden_ref[rows, :] = (gate * sigmoid * up).astype(BF16)
        grad = nt(upstream, down_ref[...])
        gate_ref[rows, :] = (
            grad * up * sigmoid * (1.0 + gate * (1.0 - sigmoid))
        ).astype(BF16)
        up_ref[rows, :] = (grad * gate * sigmoid).astype(BF16)


def mlp_middle(normed, upstream, gate_up, down):
    rows, width = normed[0].shape
    whole = shaped((2 * rows, width), BF16)
    columns = shaped((2 * rows, width // 2), BF16)
    shapes = columns, columns, columns, whole, whole
    return call(mlp_kernel, "mlp_middle", shapes, (), *normed, *upstream, gate_up, down)


def rows_kernel(transposed, *refs):
    *left_refs, right_ref, own_ref, sent_ref = refs
    rows = own_ref.shape[0]
    for block, out_ref in enumerate((own_ref, sent_ref)):
        total, start = 0.0, 0
        for left_ref in left_refs:
            left = left_ref[block * rows : (block + 1) * rows, :]
            if transposed:
                total = total + nt(left, right_ref[:, start : start + left.shape[1]])
            else:
                total = total + nn(left, right_ref[start : start + left.shape[1], :])
            start += left.shape[1]
        out_ref[...] = total


def rows_product(lefts, right, transposed, name):
    columns = right.shape[0] if transposed else right.shape[1]
    shape = shaped((lefts[0].shape[0] // 2, columns), F32)
    kernel = functools.partial(rows_kernel, transposed)
    return call(kernel, name, (shape, shape), (), *lefts, right)


def norm_back(values, gain, upstream):
    inverse = lax.rsqrt(jnp.mean(values * values, axis=1, keepdims=True) + EPSILON)
    scaled = upstream * gain
    back = inverse * scaled - values * inverse**3 * jnp.mean(values * scaled, axis=1, keepdims=True)
    return back, jnp.sum(upstream * values * inverse, axis=0, keepdims=True)


def middle_back_kernel(own_ref, came_ref, hidden_ref, upstream_ref, gain_ref, grad_ref, low_ref, sum_ref):
    back, sums = norm_back(hidden_ref[...], gain_ref[...], own_ref[...] + came_ref[...])
    grad = upstream_ref[...].astype(F32) + back
    grad_ref[...] = grad
    low_ref[...] = grad.astype(BF16)
    sum_ref[...] = sums


def middle_back(own, came, hidden, upstream, gain):
    shapes = shaped(own.shape, F32), shaped(own.shape, BF16), shaped((1, own.shape[1]), F32)
    return call(
        middle_back_kernel, "middle_back", shapes, (), own, came, hidden, upstream, gain[None]
    )


def attended_kernel(core_ref, own_ref, other_ref, weight_ref, grad_ref, rows_ref):
    rows = own_ref.shape[0]
    for block, ref in enumerate((own_ref, other_ref)):
        place = pl.ds(pl.multiple_of((core_ref[0] ^ block) * rows, rows), rows)
        grad_ref[place, :] = nt(ref[...], weight_ref[...]).astype(BF16)
        rows_ref[place, :] = ref[...]


def attended_back(core, own, other, weight):
    rows, width = own.shape
    shapes = shaped((2 * rows, weight.shape[0]), BF16), shaped((2 * rows, width), BF16)
    return call(
        attended_kernel, "attended_back", shapes, (core.reshape(1),), own, other, weight
    )


def gain_kernel(own_ref, came_ref, tokens_ref, before_ref, here_ref, sent_ref, sum_ref):
    total = 0.0
    for part, ref in enumerate((tokens_ref, before_ref)):
        grad = own_ref[part] + came_ref[part]
        values = ref[...].astype(F32)
        inverse = lax.rsqrt(jnp.mean(values * values, axis=1, keepdims=True) + EPSILON)
        total = total + jnp.sum(grad * values * inverse, axis=0, keepdims=True)
        if part == 0:
            here_ref[...] = grad
        else:
            sent_ref[...] = grad.astype(BF16)
    sum_ref[...] = total


def gain_terms(own, came, tokens, before):
    rows, width = tokens.shape
    shapes = shaped((rows, width), F32), shaped((rows, width), BF16), shaped((1, width), F32)
    return call(gain_kernel, "gain_terms", shapes, (), own, came, tokens, before)


def tokens_kernel(first_ref, here_ref, after_ref, tokens_ref, gain_ref, hidden_ref, out_ref):
    later = jnp.where(first_ref[0] == 0, after_ref[...].astype(F32), 0.0)
    back, _ = norm_back(tokens_ref[...].astype(F32), gain_ref[...], here_ref[...] + later)
    out_ref[...] = hidden_ref[...] + back


def tokens_back(first, here, after_rows, tokens, gain, grad_hidden):
    shape = shaped(here.shape, F32)
    arrays = here, after_rows, tokens, gain[None], grad_hidden
    return call(tokens_kernel, "tokens_back", shape, (first.reshape(1),), *arrays)


def pick(pair, index):
    return jnp.where(index == 0, pair[0], pair[1])


def in_order(own, other, index, axis):
    return jnp.where(
        index == 0,
        jnp.concatenate([own, other], axis=axis),
        jnp.concatenate([other, own], axis=axis),
    )


def block_of(matrix, index, size, axis=0):
    return lax.dynamic_slice_in_dim(matrix, index * size, size, axis)


def across(value, axis, bit):
    count = lax.axis_size(axis)
    return lax.ppermute(value, axis, [(place, place ^ bit) for place in range(count)])


def line_bits(count):
    return [1 << power for power in range(count.bit_length() - 1)]


def after(values, *earlier):
    return lax.optimization_barrier((values, earlier))[0]


def gather_far(block, far, before=(), then=()):
    held = block[None]
    arrived = ()
    for axis, bit in far:
        sent = after(held, *before) if before else held
        arrived = (across(sent, axis, bit),)
        held = jnp.concatenate([held, after(arrived[0], *then) if then else arrived[0]], axis=0)
    return held, arrived


def join_kernel(starts, *refs):
    count = len(refs) // 3
    for number, start in enumerate(starts):
        first_ref, second_ref, out_ref = refs[number], refs[count + number], refs[2 * count + number]
        size, _, columns = first_ref.shape
        out_ref[:size] = first_ref[...]
        out_ref[size:] = second_ref[start : start + size, :, :columns]


def join(firsts, seconds, starts):
    shapes = [shaped((2 * first.shape[0],) + first.shape[1:], first.dtype) for first in firsts]
    kernel = functools.partial(join_kernel, starts)
    return call(kernel, "join", shapes, (), *firsts, *seconds)


class Chain:
    def __init__(self, held, order, step):
        self.sides = held.shape[1]
        self.held, self.last, self.start = None, held.reshape((-1,) + held.shape[2:]), 0
        self.order, self.step = order, step


def take_all(chains, *earlier):
    lasts = [after(chain.last, *earlier) if earlier else chain.last for chain in chains]
    if chains[0].held is None:
        helds = lasts
    else:
        starts = [chain.start for chain in chains]
        helds = join([chain.held for chain in chains], lasts, starts)
    for chain, held in zip(chains, helds):
        chain.held, chain.start = held, 0


def advance_all(chains, *earlier):
    take_all(chains, *earlier)
    for chain in chains:
        chain.last = across(chain.held, *chain.order[chain.step])
        chain.step += 1
    return [chain.last for chain in chains]


def together_kernel(count, *refs):
    for number in range(count):
        first_ref, second_ref, short_ref, out_ref = refs[number::count]
        size = first_ref.shape[0]
        out_ref[:size] = first_ref[...]
        out_ref[size : 2 * size] = second_ref[...]
        out_ref[2 * size :, :, : short_ref.shape[2]] = short_ref[...]


def advance_together(longs, shorts):
    take_all(shorts)
    shapes = [
        shaped((2 * long.held.shape[0] + short.held.shape[0],) + long.held.shape[1:], BF16)
        for long, short in zip(longs, shorts)
    ]
    arrays = [long.held for long in longs] + [long.last for long in longs]
    arrays += [short.held for short in shorts]
    kernel = functools.partial(together_kernel, len(longs))
    messages = call(kernel, "together", shapes, (), *arrays)
    for long, short, message in zip(longs, shorts, messages):
        came = across(message, *long.order[long.step])
        count = 2 * long.held.shape[0]
        long.held, long.last, long.count = message, came, count
        short.last, short.start = came, count
        long.step += 1
        short.step += 1


def layout_kernel(plans, count_out, place_ref, *refs):
    out_refs = refs[-count_out:]
    for source, (line, sides, count, columns, steps, base, placed) in enumerate(plans):
        devices = 4 * line
        for index in range(count // sides):
            flips = dict(base)
            for power, (axis, bit) in enumerate(steps):
                if index >> power & 1:
                    flips[axis] = flips.get(axis, 0) ^ bit
            for number, by_column, side, core_flip, column in placed:
                strides = {"y": devices, "z": 2, "x": 1, "c": devices // 2}
                if not by_column:
                    strides["y"], strides["c"] = devices // 2, 0
                flips["c"] = core_flip
                target = 0
                for at, axis in enumerate(("y", "c", "z", "x")):
                    target += (place_ref[at] ^ flips.get(axis, 0)) * strides[axis]
                out_refs[number][target, :, column : column + columns] = refs[source][
                    index * sides + side, :, :columns
                ]


def layout_blocks(place, line, widths, chains):
    plans, sources = [], []
    for chain, columns, placed in chains:
        count = getattr(chain, "count", chain.held.shape[0])
        placed = [(number, widths[number][1], *rest) for number, *rest in placed]
        for base in ((), chain.order[-1:]):
            plans.append((line, chain.sides, count, columns, chain.order[:-1], base, placed))
        sources += [chain.held, chain.last]
    share = sources[0].shape[1]
    shapes = [
        shaped(((8 if by_column else 4) * line, share, width), BF16) for width, by_column in widths
    ]
    kernel = functools.partial(layout_kernel, plans, len(widths))
    outs = call(kernel, "layout_blocks", shapes, (place,), *sources)
    return [out.reshape(out.shape[0] * share, out.shape[2]) for out in outs]


def gathered_kernel(kernel, count, core_ref, *refs):
    copies = [
        pltpu.make_async_copy(refs[number], refs[number - count - 1], refs[-1].at[number])
        for number in range(count)
    ]
    for copy in copies:
        copy.start()
    for copy in copies:
        copy.wait()
    kernel(core_ref, *refs[-count - 1 : -1], *refs[count : -count - 1])


def sides_kernel(core_ref, *refs):
    *weight_refs, vector_ref, attn_ref, gate_up_ref = refs
    share, width = weight_refs[0].shape
    half, quarter = width // 2, width // 4
    for number, weight_ref in enumerate(weight_refs):
        out_ref, column = (attn_ref, number) if number < 3 else (gate_up_ref, number - 3)
        start = column * half
        for core in range(2):
            parts = [
                weight_ref[:, side * half + core * quarter : side * half + (core + 1) * quarter]
                for side in range(2)
            ]
            side = core ^ core_ref[0]
            if 0 < number < 3:
                for part in range(2):
                    start = half + 128 + part * half + (number - 1) * quarter
                    attn_ref[side, :, start : start + quarter] = parts[part]
            else:
                out_ref[side, :, start : start + half] = jnp.concatenate(parts, axis=1)
    for side in range(2):
        attn_ref[side, :, half : half + 128] = vector_ref[...]


def column_sides(core, weights, vectors):
    share, width = weights[0].shape
    shapes = (
        shaped((2, share, 3 * width // 2 + vectors.shape[1]), BF16),
        shaped((2, share, width), BF16),
    )
    arrays = [*weights, vectors]
    kernel = functools.partial(gathered_kernel, sides_kernel, len(arrays))
    return call(
        kernel, "column_sides", shapes, (core.reshape(1),), *arrays,
        scratch=[pltpu.VMEM(array.shape, array.dtype) for array in arrays]
        + [pltpu.SemaphoreType.DMA((len(arrays),))],
    )


def products_kernel(plans, mine_ref, *refs):
    outputs = iter(refs[sum(plan[1] + plan[2] for plan in plans) :])
    at = 0
    for share, lefts, rights, turned, chains in plans:
        left_refs, right_refs = refs[at : at + lefts], refs[at + lefts : at + lefts + rights]
        at += lefts + rights
        targets = [(next(outputs), next(outputs)) for _ in chains]
        size = left_refs[0].shape[0 if turned else 1] // 2
        wide = [ref[...] for ref in right_refs]
        wide = wide[0] if len(wide) == 1 else jnp.concatenate(wide, axis=1)
        starts = [sum(ref.shape[1] for ref in right_refs[:index]) for index in range(rights + 1)]
        for row_side in range(2):
            span = slice(row_side * size, (row_side + 1) * size)
            total, first = 0.0, 0
            for left_ref in left_refs:
                count = left_ref.shape[1 if turned else 0]
                right = wide[first : first + count]
                if turned:
                    total = total + nn(left_ref[span, :], right)
                else:
                    total = total + tn(left_ref[:, span], right)
                first += count
            for (which, columns, places), (kept_ref, sent_ref) in zip(chains, targets):
                result = total[:, starts[columns[0]] : starts[columns[-1] + 1]]

                def store(mine):
                    for block in range(size // share):
                        digit, target = places[row_side * (size // share) + block]
                        out_ref = kept_ref if digit == mine else sent_ref
                        out_ref[target] = result[block * share : (block + 1) * share].astype(BF16)

                pl.when(mine_ref[which] == 0)(functools.partial(store, 0))
                pl.when(mine_ref[which] == 1)(functools.partial(store, 1))


def products(mine, share, groups):
    plans, inputs, shapes = [], [], []
    count = 0
    for lefts, rights, chains, turned in groups:
        inputs += [*lefts, *rights]
        plan = []
        rows = lefts[0].shape[0 if turned else 1]
        for columns, dims, digit in chains:
            places = []
            for block in range(rows // share):
                index, rest = [], block
                for size in reversed(dims):
                    index.append(rest % size)
                    rest //= size
                index = index[::-1]
                value = index.pop(digit)
                flat = 0
                for size, digit_of in zip(dims[:digit] + dims[digit + 1 :], index):
                    flat = flat * size + digit_of
                places.append((value, flat))
            plan.append((count, columns, places))
            count += 1
            wide = sum(rights[column].shape[1] for column in columns)
            shape = (rows // share // 2, share, wide)
            shapes += [shaped(shape, BF16)] * 2
        plans.append((share, len(lefts), len(rights), turned, plan))
    kernel = functools.partial(products_kernel, plans)
    outs = call(kernel, "products", shapes, (mine,), *inputs)
    return list(zip(outs[::2], outs[1::2]))


def back_kernel(core_ref, *refs):
    grad_q_refs, grad_kv_refs = refs[:2], refs[2:4]
    weight_ref, own_ref, sent_ref = refs[4:]
    chip_rows, quarter = grad_q_refs[0].shape
    rows = chip_rows // 2
    keys = weight_ref.shape[1] - 4 * quarter
    both = 0.0
    for part in range(2):
        first = keys + 2 * part * quarter
        both = both + nt(grad_kv_refs[part][...], weight_ref[:, first : first + 2 * quarter])
    grad_q = jnp.concatenate([ref[...] for ref in grad_q_refs], axis=1)
    here = nt(grad_q, weight_ref[:, : 2 * quarter]) + both[chip_rows:]
    for block in range(2):
        span = slice(block * rows, (block + 1) * rows)
        side = core_ref[0] ^ block

        def store(out_ref):
            out_ref[0] = here[span].astype(out_ref.dtype)
            out_ref[1] = both[span].astype(out_ref.dtype)

        pl.when(side == 0)(functools.partial(store, own_ref))
        pl.when(side == 1)(functools.partial(store, sent_ref))


def back_project(core, grad_q, grad_kv, weights):
    shape = (2, grad_q[0].shape[0] // 2, weights.shape[0])
    shapes = shaped(shape, F32), shaped(shape, BF16)
    arrays = *grad_q, *grad_kv, weights
    return call(back_kernel, "back_project", shapes, (core.reshape(1),), *arrays)


def step_kernel(plans, mine_ref, *refs):
    for number, plan in enumerate(plans):
        held_ref, came_ref = refs[plan["held"]], refs[plan["came"]]
        count, share, columns = held_ref.shape
        came_at, came_column = plan["came_at"]
        sent_at, sent_column = plan["sent_at"]

        def store(mine):
            for index in range(count):
                value = held_ref[index].astype(F32) + came_ref[
                    came_at + index, :share, came_column : came_column + columns
                ].astype(F32)
                digit, target = plan["places"][index]
                if digit == mine:
                    kept_ref = refs[plan["kept"]]
                    kept_ref[target] = value.astype(kept_ref.dtype)
                else:
                    sent_ref = refs[plan["sent"]]
                    sent_ref[sent_at + target, :share, sent_column : sent_column + columns] = (
                        value.astype(sent_ref.dtype)
                    )

        if plan["digit"] is None:
            store(0)
        else:
            pl.when(mine_ref[plan["digit"]] == 0)(functools.partial(store, 0))
            pl.when(mine_ref[plan["digit"]] == 1)(functools.partial(store, 1))


def finish_kernel(plans, core_ref, *refs):
    *own_refs, other_ref = refs[: -len(plans)]
    first_core = core_ref[0] == 0
    for plan, out_ref in zip(plans, refs[-len(plans) :]):
        for side, (source, column, other_column) in enumerate(plan):
            half = out_ref.shape[1] // 2
            own = own_refs[source][:, column : column + half // 2]
            other = other_ref[:, other_column : other_column + half // 2]
            pair = [jnp.where(first_core, own, other), jnp.where(first_core, other, own)]
            out_ref[:, side * half : (side + 1) * half] = jnp.concatenate(pair, axis=1)


def finish_columns(core, own, other, half, mixed):
    quarter = half // 2
    plans = []
    for index in range(len(own)):
        sources = [index, index]
        columns = [0, quarter]
        if mixed and index >= len(own) - 2:
            sources = [len(own) - 2, len(own) - 1]
            columns = [(index - len(own) + 2) * quarter] * 2
        plans.append([(s, col, s * half + col) for s, col in zip(sources, columns)])
    shapes = [shaped((own[0].shape[0], 2 * half), F32)] * len(own)
    kernel = functools.partial(finish_kernel, plans)
    return call(kernel, "finish_columns", shapes, (core.reshape(1),), *own, other)


def local(
    tokens,
    lengths,
    norm_attn,
    norm_mlp,
    query_scale,
    query_proj,
    key_proj,
    value_proj,
    output_proj,
    gate_proj,
    up_proj,
    down_proj,
    cotangent,
):
    place = {name: lax.axis_index(name) for name in ("y", "c", "z", "x")}
    y, c, x = place["y"], place["c"], place["x"]
    line = lax.axis_size("z")
    bits = line_bits(line)
    rows = tokens.shape[1]
    share, width = query_proj.shape
    half = width // 2
    quarter = width // 4
    chip_rows = 2 * rows
    length = 4 * rows

    near = ("z", 1)
    far = [("z", bit) for bit in reversed(bits[1:])]
    orders = (
        far + [("x", 1), ("y", 1), near],
        far + [("y", 1), near, ("x", 1)],
        far + [near, ("x", 1), ("y", 1)],
    )
    vector_columns = jnp.pad(
        jnp.stack([norm_attn, norm_mlp, query_scale], axis=1), ((0, 0), (0, 125))
    )
    attn_block, gate_up_block = column_sides(
        c, (query_proj, key_proj, value_proj, gate_proj, up_proj), vector_columns
    )
    own_tokens = tokens[0]
    other_tokens = across(own_tokens, "c", 1)
    other_cotangent = across(cotangent[0], "c", 1)
    before = across(own_tokens, "y", 1)
    other_before = across(before, "c", 1)
    chip_tokens = in_order(own_tokens, other_tokens, c, 0)
    chip_before = in_order(before, other_before, c, 0)
    all_tokens = jnp.concatenate([chip_before, chip_tokens], axis=0)

    attn_far, first = gather_far(attn_block, far, (), (other_tokens, other_cotangent, before))

    def swap_sides(blocks):
        return jnp.stack([blocks[:, 0], across(blocks[:, 1], "c", 1)], axis=1)

    attn_sides = swap_sides(attn_far)
    cuts = (0, half + 128, 2 * half + 128, 3 * half + 128)
    attn_chains = [
        Chain(attn_sides[..., cut:end], order, len(far))
        for cut, end, order in zip(cuts, cuts[1:], orders)
    ]
    places_now = jnp.stack([place[name] for name in ("y", "c", "z", "x")])
    advance_all(attn_chains)
    first_far, middle = gather_far(
        jnp.concatenate([gate_up_block, output_proj[None]], axis=0), far, first
    )
    third = advance_all(attn_chains, other_before, *middle)
    down_far, _ = gather_far(down_proj, far, middle, third)
    gate_up_sides = swap_sides(first_far)
    mlp_chains = [
        Chain(
            jnp.concatenate(
                [gate_up_sides[..., cut : cut + half], down_far[:, None, :, cut : cut + half]], axis=1
            ),
            order,
            len(far),
        )
        for cut, order in zip((0, half), orders)
    ]
    output_sides = jnp.stack([first_far[:, 2, :, :half], first_far[:, 2, :, half:]], axis=1)
    mlp_chains.append(Chain(output_sides, orders[2], len(far)))
    advance_together(attn_chains[1:] + attn_chains[:1], mlp_chains)
    advance_all(mlp_chains)

    doc_ends = jnp.cumsum(lengths[0])
    places = jnp.arange(length, dtype=jnp.int32)
    segment = jnp.sum((places[:, None] >= doc_ends[None, :]).astype(jnp.int32), axis=1)
    seg_here = block_of(segment, y, chip_rows)
    seg_before = jnp.where(y == 0, -1, segment[:chip_rows])
    seg_keys = jnp.concatenate([seg_before, seg_here])[None]
    seg_rows = seg_here[:, None]
    first_row = y * chip_rows + jnp.arange(rows, dtype=jnp.int32)
    upstream = [
        jnp.where((first_row + core * rows < doc_ends[-1])[:, None], rows_of, 0).astype(BF16)
        for core, rows_of in ((c, cotangent[0]), (1 - c, other_cotangent))
    ]
    both = ((0, 0), (1, 1))
    (attn_weights,) = layout_blocks(
        places_now,
        line,
        [(3 * half + 128, True)],
        [
            (chain, end - cut, [(0, side, flip, cut) for side, flip in both])
            for chain, cut, end in zip(attn_chains, cuts, cuts[1:])
        ],
    )
    mlp_last = advance_all(mlp_chains, attn_weights)
    attn_weights = after(attn_weights, *[chain.held for chain in mlp_chains])
    q_raw, queries, keys_values, normed_before, normed_here, vectors, scale_rows = project(
        c, all_tokens, attn_weights
    )
    gain_a, gain_m = vectors[0], vectors[1]
    attended_f, attended, lse = attention_forward(queries, keys_values, seg_rows, seg_keys)
    attended = after(attended, *mlp_last, *upstream)
    for chain in mlp_chains:
        chain.last = after(chain.last, attended)

    (proj_o,) = layout_blocks(
        places_now,
        line,
        [(width, False)],
        [(mlp_chains[2], half, [(0, 0, 0, 0), (0, 1, 0, half)])],
    )
    output_own, output_sent = output_project(c, attended, proj_o)
    hidden1, normed_own = norm_middle(
        output_own, across(output_sent, "c", 1), own_tokens, gain_m
    )
    normed_other = across(normed_own, "c", 1)
    for chain in mlp_chains[:2]:
        chain.last = after(chain.last, output_sent)
    proj_gu, proj_d = layout_blocks(
        places_now,
        line,
        [(width, True), (width, False)],
        [
            (chain, half, [(0, side, flip, cut) for side, flip in both] + [(1, 2, 0, cut)])
            for chain, cut in zip(mlp_chains, (0, half))
        ],
    )
    hidden, grad_gate, grad_up, normed_m, upstream_b = mlp_middle(
        (normed_own, normed_other), upstream, proj_gu, proj_d
    )

    digits = [("y", 1), ("c", 1)] + [("z", bit) for bit in reversed(bits)] + [("x", 1)]
    scatter_orders = [order[len(far) :][::-1] for order in orders]

    output_orders = [("x", 1), ("y", 1), near], [("y", 1), ("x", 1), near]

    def own_digit(axis, bit):
        return (place[axis] // bit) % 2

    def sizes_of(names, by_column):
        return tuple(1 if name == ("c", 1) and not by_column else 2 for name in names)

    def first_step(*groups, gate=()):
        mine, plans, states = [], [], []
        for lefts, rights, columns, chain_orders, turned in groups:
            by_column = lefts[0].shape[0 if turned else 1] == width
            dims = sizes_of(digits, by_column)
            chains = []
            for which, order in zip(columns, chain_orders):
                at = digits.index(order[0])
                chains.append((which, dims, at))
                mine.append(own_digit(*order[0]))
                names = digits[:at] + digits[at + 1 :]
                states.append({"names": names, "by_column": by_column, "order": order, "step": 1})
            plans.append((lefts, rights, chains, turned))
        if share % 8 == 0:
            parts = products(jnp.stack(mine).astype(jnp.int32), share, plans)
        else:
            parts = []
            for lefts, rights, chains, turned in plans:
                left = jnp.concatenate([each.T if turned else each for each in lefts], axis=0)
                for which, dims, at in chains:
                    right = jnp.concatenate([rights[column] for column in which], axis=1)
                    part = tn(left, right).astype(BF16).reshape(dims + (share, right.shape[1]))
                    digit = mine[len(parts)]
                    parts.append(
                        [
                            lax.dynamic_index_in_dim(part, which_half, at, keepdims=False).reshape(
                                -1, share, right.shape[1]
                            )
                            for which_half in (digit, 1 - digit)
                        ]
                    )
        sent = [after(value, *gate) if gate else value for _, value in parts]
        for state, (kept, _), value in zip(states, parts, sent):
            state.update(held=kept, came=across(value, *state["order"][0]), came_at=(0, 0))
        return states, [value for _, value in parts]

    def step(states, names, *earlier, packed=None, dtype=BF16):
        mine, plans, inputs, shapes = [], [], [], []
        came = [after(state["came"], *earlier) if earlier else state["came"] for state in states]
        sources = {}
        for state, array in zip(states, came):
            key = id(state["came"])
            if key not in sources:
                sources[key] = len(inputs)
                inputs.append(array)
        new_states = []
        for number, (state, name) in enumerate(zip(states, names)):
            dims = sizes_of(state["names"], state["by_column"])
            held = state["held"]
            plan = {"came": sources[id(state["came"])], "came_at": state["came_at"]}
            plan["held"] = len(inputs)
            inputs.append(held)
            at = state["names"].index(name) if name in state["names"] else None
            if at is not None and dims[at] == 1:
                at = None
            rest = [index for index in range(len(dims)) if index != at]
            places = []
            for index in range(held.shape[0]):
                values, left_over = [], index
                for size in reversed(dims):
                    values.append(left_over % size)
                    left_over //= size
                values = values[::-1]
                flat = 0
                for axis_at in rest:
                    flat = flat * dims[axis_at] + values[axis_at]
                places.append((0 if at is None else values[at], flat))
            plan["places"] = places
            plan["digit"] = None if at is None else len(mine)
            if at is not None:
                mine.append(own_digit(*name))
            plan["sent_at"] = packed[1][number] if packed else (0, 0)
            plan["kept"] = len(shapes)
            count = held.shape[0] // (1 if at is None else 2)
            shapes.append(shaped((count,) + held.shape[1:], F32))
            if at is not None and not packed:
                plan["sent"] = len(shapes)
                shapes.append(shaped((count,) + held.shape[1:], dtype))
            plans.append(plan)
            names_left = [state["names"][axis_at] for axis_at in rest]
            new_states.append(dict(state, names=names_left, came_at=plan["sent_at"]))
        if packed:
            for plan in plans:
                plan["sent"] = len(shapes)
            shapes.append(shaped(packed[0], dtype))
        for plan in plans:
            plan["kept"] += 1 + len(inputs) - 1
            if "sent" in plan:
                plan["sent"] += len(inputs)
        if not mine:
            mine = [place["c"]]
        kernel = functools.partial(step_kernel, plans)
        outs = call(kernel, "step", shapes, (jnp.stack(mine).astype(jnp.int32),), *inputs)
        for plan, state in zip(plans, new_states):
            state["held"] = outs[plan["kept"] - len(inputs)]
        if packed:
            return new_states, outs[-1]
        return new_states, [
            outs[plan["sent"] - len(inputs)] if plan["digit"] is not None else None
            for plan in plans
        ]

    def halve(states, *earlier):
        names = [state["order"][state["step"]] for state in states]
        states, sent = step(states, names, *earlier)
        for state, value, name in zip(states, sent, names):
            state.update(came=across(value, *name), came_at=(0, 0), step=state["step"] + 1)
        return states, sent

    def halve_far(states, shape, places, *earlier):
        for axis, bit in far[::-1][:-1]:
            states, sent = step(states, [(axis, bit)] * len(states))
            for state, value in zip(states, sent):
                state.update(came=across(value, axis, bit), came_at=(0, 0))
        last = far[0]
        states, message = step(states, [last] * len(states), *earlier, packed=(shape, places))
        arrived = across(message, *last)
        for state in states:
            state.update(came=arrived)
        return states, message

    def join_columns(states):
        left, right = states
        joined = dict(left, came_at=(0, 0))
        for key in ("held", "came"):
            joined[key] = jnp.concatenate([left[key], right[key]], axis=2)
        return [joined]

    def received(states):
        return [state["came"] for state in states]

    gate_own, gate_sent = rows_product((grad_gate, grad_up), proj_gu, True, "gate_up_back")
    mlp_states, mlp_sent = first_step(
        ((hidden,), (upstream_b,), ((0,),), scatter_orders[:1], False),
        (
            (normed_m,),
            after((grad_gate, grad_up), gate_sent),
            ((0,), (1,)),
            scatter_orders[1:],
            False,
        ),
    )
    gate_own = after(gate_own, *mlp_sent)
    grad_hidden1, low_own, grad_gain_m = middle_back(
        gate_own, across(gate_sent, "c", 1), hidden1, upstream[0], gain_m
    )
    grad_attended, grad_hidden1_b = attended_back(c, low_own, across(low_own, "c", 1), proj_o)
    scale_row = scale_rows[:1]
    heads = half // HD
    residuals = (queries, keys_values), (attended_f, lse, seg_rows, seg_keys, q_raw, scale_row)
    grad_q_early, grad_kv_early, early_sums = attention_backward(
        0, heads // 2, *residuals[0], grad_attended, *residuals[1]
    )
    down_own, down_sent = rows_product(
        (after(hidden, grad_attended),), proj_d, False, "down_project"
    )
    down_other = across(down_sent, "c", 1)
    block_out = hidden1 + down_own + down_other
    mlp_states, mlp_sent = halve(mlp_states, grad_kv_early, down_other)
    grad_rows = after(grad_hidden1_b, *mlp_sent)
    output_rights = grad_rows[:, :half], grad_rows[:, half:]
    output_states, output_sent = first_step(
        ((attended,), output_rights, ((0,), (1,)), output_orders, False)
    )
    grad_attended = after(grad_attended, *mlp_sent, *output_sent)
    grad_q_late, grad_kv_late, late_sums = attention_backward(
        heads // 2, heads, *residuals[0], grad_attended, *residuals[1]
    )
    grad_scale = jnp.concatenate([early_sums[0], late_sums[0]]) * scale_rows[1]
    grads = (grad_q_early, grad_q_late), (grad_kv_early, grad_kv_late)
    mlp_states, mlp_sent = halve(mlp_states, grad_kv_late)
    output_states, output_sent = halve(output_states, grad_kv_late)
    grads = after(grads, *mlp_sent, *output_sent)
    attn_states, attn_sent = first_step(
        ((normed_here,), grads[0], ((0, 1),), scatter_orders[:1], False),
        ((normed_before, normed_here), grads[1], ((0,), (1,)), scatter_orders[1:], False),
        gate=received(mlp_states + output_states),
    )
    first_done = received(attn_states)
    grads = after(grads, *attn_sent)
    mlp_states, _ = halve_far(
        mlp_states, (3, share, width), ((2, 0), (0, 0), (0, half)), *attn_sent
    )
    back_own, back_sent = back_project(c, *grads, attn_weights)
    back_other = across(back_sent, "c", 1)
    output_states = join_columns(
        [dict(state, came=after(state["came"], *first_done)) for state in output_states]
    )
    output_states, _ = halve(output_states)
    attn_states, _ = halve(attn_states, mlp_states[0]["came"], back_own)
    second_done = received(attn_states)
    grad_here, grad_before, grad_gain_a = gain_terms(back_own, back_other, own_tokens, before)
    scale_rows = grad_scale.reshape(2, 1, quarter)
    scale_rows = jnp.where(
        c == 0,
        jnp.pad(scale_rows, ((0, 0), (0, 1), (0, 0))),
        jnp.pad(scale_rows, ((0, 0), (1, 0), (0, 0))),
    ).reshape(width)
    vector_terms = jnp.stack([grad_gain_a[0], grad_gain_m[0], scale_rows])
    vector_rows = min(8, share)
    vector_terms = jnp.moveaxis(vector_terms.reshape(3, -1, share), 0, 1)
    room = ((0, 0), (0, vector_rows - 3), (0, 128 - share))
    vector_terms = jnp.pad(vector_terms, room)
    vector_order = [near] + far[::-1] + [("x", 1), ("y", 1)]
    vector_state = {"names": digits, "by_column": True, "order": vector_order, "step": 0}
    zero_terms = jnp.zeros(vector_terms.shape, BF16)
    vector_states = [dict(vector_state, held=vector_terms, came=zero_terms, came_at=(0, 0))]
    vector_states, _ = halve(vector_states)
    attn_states, _ = halve(attn_states, *received(output_states + vector_states))
    third_done = received(attn_states)
    output_states, _ = halve_far(output_states, (1, share, width), ((0, 0),))
    for _ in far:
        vector_states, _ = halve(vector_states)
    vector_first = received(vector_states)
    vector_states, _ = halve(vector_states, *third_done)
    vector_second = received(vector_states)
    grad_after = across(after(grad_before, *third_done), "y", 1)
    grad_inputs = tokens_back(y, grad_here, grad_after, own_tokens, gain_a, grad_hidden1)

    attn_places = [(0, number * half) for number in range(3)]
    final_states, final_message = halve_far(
        attn_states, (2, share, 3 * half), attn_places, *received(output_states), *vector_first
    )
    vector_states, _ = halve(vector_states, grad_after)
    vector_third = received(vector_states)
    mlp_states, sent = step(
        mlp_states,
        [("c", 1)] * 3,
        final_message,
        packed=((1, share, width), ((0, 0), (0, 0), (0, half))),
        dtype=F32,
    )
    mlp_parts = [state["held"][0] for state in mlp_states]
    gate_up_other = across(sent[0], "c", 1)
    gate_up_grads = finish_columns(c, mlp_parts[1:], gate_up_other, half, False)
    final_states, sent = step(
        final_states,
        [("c", 1)] * 3,
        grad_after,
        gate_up_other,
        packed=((1, share, 3 * half), attn_places),
        dtype=F32,
    )
    output_states, _ = step(output_states, [("c", 1)], final_message)
    own_parts = [state["held"][0] for state in final_states + output_states]
    other = across(sent[0], "c", 1)
    attn_grads = finish_columns(c, own_parts[:3], other, half, True)
    vector_states, vector_sent = step(vector_states, [("c", 1)], dtype=F32)
    vector_other = across(vector_sent[0][0], "c", 1)
    summed = (vector_states[0]["held"][0] + vector_other)[:, :share]
    return (
        block_out.astype(BF16)[None],
        grad_inputs[None],
        summed[0],
        summed[1],
        summed[2],
        *attn_grads,
        own_parts[3],
        *gate_up_grads,
        mlp_parts[0],
    )


def solution(mesh):
    seq, dp = mesh.devices.shape
    axes = Mesh(mesh.devices.reshape(seq // 2, 2, dp // 2, 2), ("y", "c", "z", "x"))
    batch, places, every = ("z", "x"), ("y", "c"), ("y", "c", "z", "x")
    activations = P(batch, places, None)
    vector, matrix = P(every), P(every, None)
    return jax.shard_map(
        local,
        mesh=axes,
        in_specs=(activations, P(batch, None)) + (vector,) * 3 + (matrix,) * 7 + (activations,),
        out_specs=(activations, activations) + (vector,) * 3 + (matrix,) * 7,
        check_vma=False,
    )
```

```python
import functools

import jax
import jax.numpy as jnp
from jax import lax
from jax.experimental import pallas as pl
from jax.experimental.pallas import tpu as pltpu
from jax.sharding import Mesh, PartitionSpec as P

H = 16
HD = 80
EPSILON = 1e-06
R_SOFTPLUS = 1.442695041
MASKED = -1e30
QUERY_ROWS = 256
VMEM_BYTES = 24 << 20
VMEM_MOST = 56 << 20
SPEED = 4600000000
COSTS = {
    "project": 5,
    "attention_forward": 13,
    "output_project": 0,
    "mlp_middle": 3,
    "gate_up_back": 3,
    "products": 6,
    "attention_backward": 10,
    "back_project": 0,
    "join": 3,
    "tokens_back": 3,
    "layout_blocks": 2,
    "norm_middle": 0,
    "mlp_first": 2,
    "products_down": 2,
    "mlp_last": 2,
    "products_mlp": 4,
}
F32 = jnp.float32
BF16 = jnp.bfloat16


def nn(left, right):
    return jnp.dot(left, right, preferred_element_type=F32)


def nt(left, right):
    return lax.dot_general(left, right, (((1,), (1,)), ((), ())), preferred_element_type=F32)


def tn(left, right):
    return lax.dot_general(left, right, (((0,), (0,)), ((), ())), preferred_element_type=F32)


def allowed_pairs(seg_rows, seg_keys, half, first, rows):
    total = seg_keys.shape[1]
    row_ids = lax.broadcasted_iota(jnp.int32, (rows, total), 0) + (first + half)
    col_ids = lax.broadcasted_iota(jnp.int32, (rows, total), 1)
    return (seg_rows == seg_keys) & (col_ids <= row_ids)


WHOLE = pl.BlockSpec(memory_space=pltpu.VMEM)
SCALARS = pl.BlockSpec(memory_space=pltpu.SMEM)
ANYWHERE = pl.BlockSpec(memory_space=pl.ANY)


def call(kernel, name, out_shape, scalars, *arrays, scratch=()):
    specs = [SCALARS] * len(scalars) + [ANYWHERE if scratch else WHOLE] * len(arrays)
    return pl.pallas_call(
        kernel,
        out_shape=out_shape,
        in_specs=specs,
        out_specs=jax.tree.map(lambda shape: WHOLE, out_shape),
        compiler_params=pltpu.CompilerParams(vmem_limit_bytes=VMEM_MOST if scratch else VMEM_BYTES),
        scratch_shapes=scratch,
        cost_estimate=pl.CostEstimate(flops=COSTS.get(name, 2) * SPEED, bytes_accessed=0, transcendentals=0),
        name=name,
    )(*scalars, *arrays)


def shaped(shape, dtype):
    return jax.ShapeDtypeStruct(tuple(shape), dtype)


def project_kernel(
    core_ref, tokens_ref, weight_ref, raw_ref, q_ref, kv_ref, before_ref, here_ref, vectors_ref,
    scale_ref
):
    chip_rows, half = raw_ref.shape
    quarter = half // 2
    vectors = weight_ref[:, half : half + 128].astype(F32).T[:8]
    keys = half + 128
    vectors_ref[...] = vectors
    gain = vectors[0:1]
    logits = [
        jnp.concatenate(
            [vectors[2:3, side * half + core * quarter :][:, :quarter] for side in range(2)], axis=1
        )
        for core in range(2)
    ]
    logit = jnp.where(core_ref[0] == 0, logits[0], logits[1])
    softplus = jnp.maximum(logit, 0.0) + jnp.log1p(jnp.exp(-jnp.abs(logit)))
    scale = R_SOFTPLUS * HD ** (-0.5) * softplus
    scale_ref[0:1] = scale
    scale_ref[1:2] = R_SOFTPLUS * HD ** (-0.5) / (1.0 + jnp.exp(-logit))
    for first in range(0, 2 * chip_rows, QUERY_ROWS):
        rows = slice(first, first + QUERY_ROWS)
        values = tokens_ref[rows, :].astype(F32)
        inverse = lax.rsqrt(jnp.mean(values * values, axis=1, keepdims=True) + EPSILON)
        normed = (values * inverse * gain).astype(BF16)
        kv_ref[rows, :] = nn(normed, weight_ref[:, keys : keys + 2 * half]).astype(BF16)
        if first >= chip_rows:
            here = slice(first - chip_rows, first - chip_rows + QUERY_ROWS)
            here_ref[here, :] = normed
            raw = nn(normed, weight_ref[:, :half])
            raw_ref[here, :] = raw
            q_ref[here, :] = (raw * scale).astype(BF16)
        else:
            before_ref[rows, :] = normed


def project(core, tokens, weights):
    rows, width = tokens.shape
    half = width // 2
    shapes = (
        shaped((rows // 2, half), F32),
        shaped((rows // 2, half), BF16),
        shaped((rows, width), BF16),
        shaped((rows // 2, width), BF16),
        shaped((rows // 2, width), BF16),
        shaped((8, width), F32),
        shaped((2, half), F32),
    )
    return call(project_kernel, "project", shapes, (core.reshape(1),), tokens, weights)


def key_value_columns(head, width):
    half = width // 2
    start = head * HD // half * width + head * HD % half
    return slice(start, start + HD), slice(start + half, start + half + HD)


def forward_kernel(q_ref, kv_ref, segq_ref, segk_ref, out_ref, low_ref, lse_ref):
    half, width = q_ref.shape
    for first in range(0, half, QUERY_ROWS):
        rows = slice(first, first + QUERY_ROWS)
        end = half + first + QUERY_ROWS
        allowed = allowed_pairs(segq_ref[rows, :], segk_ref[:, :end], half, first, QUERY_ROWS)
        outs, lses = [], []
        for head in range(width // HD):
            cols = slice(head * HD, (head + 1) * HD)
            key_cols, value_cols = key_value_columns(head, width)
            scores = jnp.where(allowed, nt(q_ref[rows, cols], kv_ref[:end, key_cols]), MASKED)
            top = jnp.max(scores, axis=1, keepdims=True)
            exps = jnp.exp(scores - top)
            total = jnp.sum(exps, axis=1, keepdims=True)
            probs = (exps * (1.0 / total)).astype(BF16)
            outs.append(nn(probs, kv_ref[:end, value_cols]))
            lses.append(top + jnp.log(total))
        out = jnp.concatenate(outs, axis=1)
        out_ref[rows, :] = out
        low_ref[rows, :] = out.astype(BF16)
        lse_ref[rows, :] = jnp.concatenate(lses, axis=1)


def attention_forward(q, kv, segq, segk):
    shapes = (
        shaped(q.shape, F32),
        shaped(q.shape, BF16),
        shaped((q.shape[0], q.shape[1] // HD), F32),
    )
    return call(forward_kernel, "attention_forward", shapes, (), q, kv, segq, segk)


def backward_kernel(first_head, last_head, *refs):
    q_ref, kv_ref, go_ref, out_ref, lse_ref, segq_ref, segk_ref, raw_ref, scale_ref = refs[:9]
    dq_ref, dkv_ref, sum_ref = refs[9:]
    half, width = q_ref.shape
    heads = range(first_head, last_head)
    span = slice(first_head * HD, last_head * HD)
    dks, dvs = [None] * len(heads), [None] * len(heads)
    sums = 0.0
    for first in reversed(range(0, half, QUERY_ROWS)):
        rows = slice(first, first + QUERY_ROWS)
        end = half + first + QUERY_ROWS
        allowed = allowed_pairs(segq_ref[rows, :], segk_ref[:, :end], half, first, QUERY_ROWS)
        products = go_ref[rows, :].astype(F32) * out_ref[rows, :]
        dqs = []
        for number, head in enumerate(heads):
            cols = slice(head * HD, (head + 1) * HD)
            key_cols, value_cols = key_value_columns(head, width)
            queries, keys = q_ref[rows, cols], kv_ref[:end, key_cols]
            values = kv_ref[:end, value_cols]
            grads = go_ref[rows, cols]
            scores = jnp.where(allowed, nt(queries, keys), MASKED)
            probs = jnp.exp(scores - lse_ref[rows, head : head + 1])
            delta = jnp.sum(products[:, cols], axis=1, keepdims=True)
            grad_scores = (probs * (nt(grads, values) - delta)).astype(BF16)
            dqs.append(nn(grad_scores, keys))
            for sums_of, term in (
                (dks, tn(grad_scores, queries)),
                (dvs, tn(probs.astype(BF16), grads)),
            ):
                held = sums_of[number]
                if held is None:
                    sums_of[number] = term
                else:
                    sums_of[number] = jnp.concatenate([held[:end] + term, held[end:]], axis=0)
        dq = jnp.concatenate(dqs, axis=1)
        sums = sums + jnp.sum(dq * raw_ref[rows, span], axis=0, keepdims=True)
        dq_ref[rows, :] = (dq * scale_ref[:, span]).astype(BF16)
    sum_ref[...] = sums
    dkv_ref[...] = jnp.concatenate(dks + dvs, axis=1).astype(BF16)


def attention_backward(first_head, last_head, q, kv, *rest):
    columns = (last_head - first_head) * HD
    shapes = (
        shaped((q.shape[0], columns), BF16),
        shaped((kv.shape[0], 2 * columns), BF16),
        shaped((1, columns), F32),
    )
    kernel = functools.partial(backward_kernel, first_head, last_head)
    return call(kernel, "attention_backward", shapes, (), q, kv, *rest)


def output_kernel(core_ref, attended_ref, weight_ref, own_ref, sent_ref):
    rows = own_ref.shape[0]
    for block in range(2):
        result = nn(attended_ref[block * rows : (block + 1) * rows, :], weight_ref[...])
        side = core_ref[0] ^ block

        def store(out_ref):
            out_ref[...] = result

        pl.when(side == 0)(functools.partial(store, own_ref))
        pl.when(side == 1)(functools.partial(store, sent_ref))


def output_project(core, attended, weight):
    shape = shaped((attended.shape[0] // 2, weight.shape[1]), F32)
    return call(
        output_kernel, "output_project", (shape, shape), (core.reshape(1),), attended, weight
    )


def norm_kernel(own_ref, came_ref, tokens_ref, gain_ref, hidden_ref, normed_ref):
    hidden = tokens_ref[...].astype(F32) + own_ref[...] + came_ref[...]
    hidden_ref[...] = hidden
    inverse = lax.rsqrt(jnp.mean(hidden * hidden, axis=1, keepdims=True) + EPSILON)
    normed_ref[...] = (hidden * inverse * gain_ref[...]).astype(BF16)


def norm_middle(own, came, tokens, gain):
    shapes = shaped(own.shape, F32), shaped(own.shape, BF16)
    return call(norm_kernel, "norm_middle", shapes, (), own, came, tokens, gain[None])


def mlp_first_kernel(*refs):
    *normed_refs, weight_ref, hidden_ref, gate_ref, up_ref, normed_ref = refs
    half = hidden_ref.shape[1]
    start = 0
    for ref in normed_refs:
        rows = slice(start, start + ref.shape[0])
        start += ref.shape[0]
        normed = ref[...]
        normed_ref[rows, :] = normed
        gate_up = nn(normed, weight_ref[...])
        gate, up = gate_up[:, :half], gate_up[:, half:]
        gate_ref[rows, :] = gate
        up_ref[rows, :] = up
        hidden_ref[rows, :] = (gate * jax.nn.sigmoid(gate) * up).astype(BF16)


def mlp_first(normed, weight):
    rows = sum(part.shape[0] for part in normed)
    half = weight.shape[1] // 2
    wide = shaped((rows, half), F32)
    shapes = shaped((rows, half), BF16), wide, wide, shaped((rows, weight.shape[0]), BF16)
    return call(mlp_first_kernel, "mlp_first", shapes, (), *normed, weight)


def mlp_last_kernel(gate_in_ref, up_in_ref, down_ref, upstream_ref, gate_ref, up_ref):
    for first in range(0, gate_ref.shape[0], QUERY_ROWS):
        rows = slice(first, first + QUERY_ROWS)
        gate, up = gate_in_ref[rows, :], up_in_ref[rows, :]
        sigmoid = jax.nn.sigmoid(gate)
        grad = nt(upstream_ref[rows, :], down_ref[...])
        gate_ref[rows, :] = (
            grad * up * sigmoid * (1.0 + gate * (1.0 - sigmoid))
        ).astype(BF16)
        up_ref[rows, :] = (grad * gate * sigmoid).astype(BF16)


def mlp_last(gate, up, down, upstream):
    shape = shaped(gate.shape, BF16)
    return call(mlp_last_kernel, "mlp_last", (shape, shape), (), gate, up, down, upstream)


def rows_kernel(transposed, *refs):
    *left_refs, right_ref, own_ref, sent_ref = refs
    rows = own_ref.shape[0]
    for block, out_ref in enumerate((own_ref, sent_ref)):
        total, start = 0.0, 0
        for left_ref in left_refs:
            left = left_ref[block * rows : (block + 1) * rows, :]
            if transposed:
                total = total + nt(left, right_ref[:, start : start + left.shape[1]])
            else:
                total = total + nn(left, right_ref[start : start + left.shape[1], :])
            start += left.shape[1]
        out_ref[...] = total


def rows_product(lefts, right, transposed, name):
    columns = right.shape[0] if transposed else right.shape[1]
    shape = shaped((lefts[0].shape[0] // 2, columns), F32)
    kernel = functools.partial(rows_kernel, transposed)
    return call(kernel, name, (shape, shape), (), *lefts, right)


def norm_back(values, gain, upstream):
    inverse = lax.rsqrt(jnp.mean(values * values, axis=1, keepdims=True) + EPSILON)
    scaled = upstream * gain
    back = inverse * scaled - values * inverse**3 * jnp.mean(values * scaled, axis=1, keepdims=True)
    return back, jnp.sum(upstream * values * inverse, axis=0, keepdims=True)


def middle_back_kernel(own_ref, came_ref, hidden_ref, upstream_ref, gain_ref, grad_ref, low_ref, sum_ref):
    back, sums = norm_back(hidden_ref[...], gain_ref[...], own_ref[...] + came_ref[...])
    grad = upstream_ref[...].astype(F32) + back
    grad_ref[...] = grad
    low_ref[...] = grad.astype(BF16)
    sum_ref[...] = sums


def middle_back(own, came, hidden, upstream, gain):
    shapes = shaped(own.shape, F32), shaped(own.shape, BF16), shaped((1, own.shape[1]), F32)
    return call(
        middle_back_kernel, "middle_back", shapes, (), own, came, hidden, upstream, gain[None]
    )


def attended_kernel(core_ref, own_ref, other_ref, weight_ref, grad_ref, rows_ref):
    rows = own_ref.shape[0]
    for block, ref in enumerate((own_ref, other_ref)):
        place = pl.ds(pl.multiple_of((core_ref[0] ^ block) * rows, rows), rows)
        grad_ref[place, :] = nt(ref[...], weight_ref[...]).astype(BF16)
        rows_ref[place, :] = ref[...]


def attended_back(core, own, other, weight):
    rows, width = own.shape
    shapes = shaped((2 * rows, weight.shape[0]), BF16), shaped((2 * rows, width), BF16)
    return call(
        attended_kernel, "attended_back", shapes, (core.reshape(1),), own, other, weight
    )


def gain_kernel(own_ref, came_ref, tokens_ref, before_ref, here_ref, sent_ref, sum_ref):
    total = 0.0
    for part, ref in enumerate((tokens_ref, before_ref)):
        grad = own_ref[part] + came_ref[part]
        values = ref[...].astype(F32)
        inverse = lax.rsqrt(jnp.mean(values * values, axis=1, keepdims=True) + EPSILON)
        total = total + jnp.sum(grad * values * inverse, axis=0, keepdims=True)
        if part == 0:
            here_ref[...] = grad
        else:
            sent_ref[...] = grad.astype(BF16)
    sum_ref[...] = total


def gain_terms(own, came, tokens, before):
    rows, width = tokens.shape
    shapes = shaped((rows, width), F32), shaped((rows, width), BF16), shaped((1, width), F32)
    return call(gain_kernel, "gain_terms", shapes, (), own, came, tokens, before)


def tokens_kernel(first_ref, here_ref, after_ref, tokens_ref, gain_ref, hidden_ref, out_ref):
    later = jnp.where(first_ref[0] == 0, after_ref[...].astype(F32), 0.0)
    back, _ = norm_back(tokens_ref[...].astype(F32), gain_ref[...], here_ref[...] + later)
    out_ref[...] = hidden_ref[...] + back


def tokens_back(first, here, after_rows, tokens, gain, grad_hidden):
    shape = shaped(here.shape, F32)
    arrays = here, after_rows, tokens, gain[None], grad_hidden
    return call(tokens_kernel, "tokens_back", shape, (first.reshape(1),), *arrays)


def pick(pair, index):
    return jnp.where(index == 0, pair[0], pair[1])


def in_order(own, other, index, axis):
    return jnp.where(
        index == 0,
        jnp.concatenate([own, other], axis=axis),
        jnp.concatenate([other, own], axis=axis),
    )


def block_of(matrix, index, size, axis=0):
    return lax.dynamic_slice_in_dim(matrix, index * size, size, axis)


def across(value, axis, bit):
    count = lax.axis_size(axis)
    return lax.ppermute(value, axis, [(place, place ^ bit) for place in range(count)])


def line_bits(count):
    return [1 << power for power in range(count.bit_length() - 1)]


def after(values, *earlier):
    return lax.optimization_barrier((values, earlier))[0]


def far_pieces(block, far, before=(), then=()):
    pieces, arrived = [block], ()
    for axis, bit in far:
        message = block if len(pieces) == 1 else jnp.stack(pieces)
        came = across(after(message, *before) if before else message, axis, bit)
        arrived = (came,)
        came = after(came, *then) if then else came
        pieces += [came] if len(pieces) == 1 else [came[index] for index in range(len(pieces))]
    return pieces, arrived


def other_cores(pieces, *earlier):
    own = pieces[0][1]
    first = across(after(own, *earlier) if earlier else own, "c", 1)
    if len(pieces) == 2:
        return [first, across(pieces[1][1], "c", 1)]
    rest = [piece[1] for piece in pieces[1:]]
    return [first] + (list(across(jnp.stack(rest), "c", 1)) if rest else [])


def side_kernel(cuts, *refs):
    count = (len(refs) - len(cuts)) // 2
    for index in range(count):
        for (first, last), out_ref in zip(cuts, refs[2 * count :]):
            out_ref[2 * index] = refs[index][0, :, first:last]
            out_ref[2 * index + 1] = refs[count + index][:, first:last]


def side_blocks(pieces, others, cuts):
    share = pieces[0].shape[1]
    shapes = [shaped((2 * len(pieces), share, last - first), BF16) for first, last in cuts]
    kernel = functools.partial(side_kernel, cuts)
    return call(kernel, "side_blocks", shapes, (), *pieces, *others)


def join_kernel(starts, *refs):
    count = len(refs) // 3
    for number, start in enumerate(starts):
        first_ref, second_ref, out_ref = refs[number], refs[count + number], refs[2 * count + number]
        size, _, columns = first_ref.shape
        out_ref[:size] = first_ref[...]
        out_ref[size:] = second_ref[start : start + size, :, :columns]


def join(firsts, seconds, starts):
    shapes = [shaped((2 * first.shape[0],) + first.shape[1:], first.dtype) for first in firsts]
    kernel = functools.partial(join_kernel, starts)
    return call(kernel, "join", shapes, (), *firsts, *seconds)


class Chain:
    def __init__(self, held, sides, order, step):
        self.sides = sides
        self.held, self.last, self.start = None, held, 0
        self.order, self.step = order, step


def take_all(chains, *earlier):
    lasts = [after(chain.last, *earlier) if earlier else chain.last for chain in chains]
    if chains[0].held is None:
        helds = lasts
    else:
        starts = [chain.start for chain in chains]
        helds = join([chain.held for chain in chains], lasts, starts)
    for chain, held in zip(chains, helds):
        chain.held, chain.start = held, 0


def advance_all(chains, *earlier):
    take_all(chains, *earlier)
    for chain in chains:
        chain.last = across(chain.held, *chain.order[chain.step])
        chain.step += 1
    return [chain.last for chain in chains]


def together_kernel(count, *refs):
    for number in range(count):
        first_ref, second_ref, short_ref, out_ref = refs[number::count]
        size = first_ref.shape[0]
        out_ref[:size] = first_ref[...]
        out_ref[size : 2 * size] = second_ref[...]
        out_ref[2 * size :, :, : short_ref.shape[2]] = short_ref[...]


def advance_together(longs, shorts):
    take_all(shorts)
    shapes = [
        shaped((2 * long.held.shape[0] + short.held.shape[0],) + long.held.shape[1:], BF16)
        for long, short in zip(longs, shorts)
    ]
    arrays = [long.held for long in longs] + [long.last for long in longs]
    arrays += [short.held for short in shorts]
    kernel = functools.partial(together_kernel, len(longs))
    messages = call(kernel, "together", shapes, (), *arrays)
    for long, short, message in zip(longs, shorts, messages):
        came = across(message, *long.order[long.step])
        count = 2 * long.held.shape[0]
        long.held, long.last, long.count = message, came, count
        short.last, short.start = came, count
        long.step += 1
        short.step += 1


def layout_kernel(plans, count_out, place_ref, *refs):
    out_refs = refs[-count_out:]
    for source, (line, sides, count, columns, steps, base, placed) in enumerate(plans):
        devices = 4 * line
        for index in range(count // sides):
            flips = dict(base)
            for power, (axis, bit) in enumerate(steps):
                if index >> power & 1:
                    flips[axis] = flips.get(axis, 0) ^ bit
            for number, by_column, side, core_flip, column in placed:
                strides = {"y": devices, "z": 2, "x": 1, "c": devices // 2}
                if not by_column:
                    strides["y"], strides["c"] = devices // 2, 0
                flips["c"] = core_flip
                target = 0
                for at, axis in enumerate(("y", "c", "z", "x")):
                    target += (place_ref[at] ^ flips.get(axis, 0)) * strides[axis]
                out_refs[number][target, :, column : column + columns] = refs[source][
                    index * sides + side, :, :columns
                ]


def layout_blocks(place, line, widths, chains):
    plans, sources = [], []
    for chain, columns, placed in chains:
        count = getattr(chain, "count", chain.held.shape[0])
        placed = [(number, widths[number][1], *rest) for number, *rest in placed]
        for base in ((), chain.order[-1:]):
            plans.append((line, chain.sides, count, columns, chain.order[:-1], base, placed))
        sources += [chain.held, chain.last]
    share = sources[0].shape[1]
    shapes = [
        shaped(((8 if by_column else 4) * line, share, width), BF16) for width, by_column in widths
    ]
    kernel = functools.partial(layout_kernel, plans, len(widths))
    outs = call(kernel, "layout_blocks", shapes, (place,), *sources)
    return [out.reshape(out.shape[0] * share, out.shape[2]) for out in outs]


def gathered_kernel(kernel, count, core_ref, *refs):
    copies = [
        pltpu.make_async_copy(refs[number], refs[number - count - 1], refs[-1].at[number])
        for number in range(count)
    ]
    for copy in copies:
        copy.start()
    for copy in copies:
        copy.wait()
    kernel(core_ref, *refs[-count - 1 : -1], *refs[count : -count - 1])


def sides_kernel(core_ref, *refs):
    *weight_refs, vector_ref, attn_ref, gate_up_ref = refs
    share, width = weight_refs[0].shape
    half, quarter = width // 2, width // 4
    for number, weight_ref in enumerate(weight_refs):
        out_ref, column = (attn_ref, number) if number < 3 else (gate_up_ref, number - 3)
        start = column * half
        for core in range(2):
            parts = [
                weight_ref[:, side * half + core * quarter : side * half + (core + 1) * quarter]
                for side in range(2)
            ]
            side = core ^ core_ref[0]
            if 0 < number < 3:
                for part in range(2):
                    start = half + 128 + part * half + (number - 1) * quarter
                    attn_ref[side, :, start : start + quarter] = parts[part]
            else:
                out_ref[side, :, start : start + half] = jnp.concatenate(parts, axis=1)
    for side in range(2):
        attn_ref[side, :, half : half + 128] = vector_ref[...]


def column_sides(core, weights, vectors):
    share, width = weights[0].shape
    shapes = (
        shaped((2, share, 3 * width // 2 + vectors.shape[1]), BF16),
        shaped((2, share, width), BF16),
    )
    arrays = [*weights, vectors]
    kernel = functools.partial(gathered_kernel, sides_kernel, len(arrays))
    return call(
        kernel, "column_sides", shapes, (core.reshape(1),), *arrays,
        scratch=[pltpu.VMEM(array.shape, array.dtype) for array in arrays]
        + [pltpu.SemaphoreType.DMA((len(arrays),))],
    )


def products_kernel(plans, mine_ref, *refs):
    outputs = iter(refs[sum(plan[1] + plan[2] for plan in plans) :])
    at = 0
    for share, lefts, rights, turned, chains in plans:
        left_refs, right_refs = refs[at : at + lefts], refs[at + lefts : at + lefts + rights]
        at += lefts + rights
        targets = [(next(outputs), next(outputs)) for _ in chains]
        size = left_refs[0].shape[0 if turned else 1] // 2
        wide = [ref[...] for ref in right_refs]
        wide = wide[0] if len(wide) == 1 else jnp.concatenate(wide, axis=1)
        starts = [sum(ref.shape[1] for ref in right_refs[:index]) for index in range(rights + 1)]
        for row_side in range(2):
            span = slice(row_side * size, (row_side + 1) * size)
            total, first = 0.0, 0
            for left_ref in left_refs:
                count = left_ref.shape[1 if turned else 0]
                right = wide[first : first + count]
                if turned:
                    total = total + nn(left_ref[span, :], right)
                else:
                    total = total + tn(left_ref[:, span], right)
                first += count
            for (which, columns, places), (kept_ref, sent_ref) in zip(chains, targets):
                result = total[:, starts[columns[0]] : starts[columns[-1] + 1]]

                def store(mine):
                    for block in range(size // share):
                        digit, target = places[row_side * (size // share) + block]
                        out_ref = kept_ref if digit == mine else sent_ref
                        out_ref[target] = result[block * share : (block + 1) * share].astype(BF16)

                pl.when(mine_ref[which] == 0)(functools.partial(store, 0))
                pl.when(mine_ref[which] == 1)(functools.partial(store, 1))


def products(mine, share, groups, name):
    plans, inputs, shapes = [], [], []
    count = 0
    for lefts, rights, chains, turned in groups:
        inputs += [*lefts, *rights]
        plan = []
        rows = lefts[0].shape[0 if turned else 1]
        for columns, dims, digit in chains:
            places = []
            for block in range(rows // share):
                index, rest = [], block
                for size in reversed(dims):
                    index.append(rest % size)
                    rest //= size
                index = index[::-1]
                value = index.pop(digit)
                flat = 0
                for size, digit_of in zip(dims[:digit] + dims[digit + 1 :], index):
                    flat = flat * size + digit_of
                places.append((value, flat))
            plan.append((count, columns, places))
            count += 1
            wide = sum(rights[column].shape[1] for column in columns)
            shape = (rows // share // 2, share, wide)
            shapes += [shaped(shape, BF16)] * 2
        plans.append((share, len(lefts), len(rights), turned, plan))
    kernel = functools.partial(products_kernel, plans)
    outs = call(kernel, name, shapes, (mine,), *inputs)
    return list(zip(outs[::2], outs[1::2]))


def back_kernel(core_ref, *refs):
    grad_q_refs, grad_kv_refs = refs[:2], refs[2:4]
    weight_ref, own_ref, sent_ref = refs[4:]
    chip_rows, quarter = grad_q_refs[0].shape
    rows = chip_rows // 2
    keys = weight_ref.shape[1] - 4 * quarter
    both = 0.0
    for part in range(2):
        first = keys + 2 * part * quarter
        both = both + nt(grad_kv_refs[part][...], weight_ref[:, first : first + 2 * quarter])
    grad_q = jnp.concatenate([ref[...] for ref in grad_q_refs], axis=1)
    here = nt(grad_q, weight_ref[:, : 2 * quarter]) + both[chip_rows:]
    for block in range(2):
        span = slice(block * rows, (block + 1) * rows)
        side = core_ref[0] ^ block

        def store(out_ref):
            out_ref[0] = here[span].astype(out_ref.dtype)
            out_ref[1] = both[span].astype(out_ref.dtype)

        pl.when(side == 0)(functools.partial(store, own_ref))
        pl.when(side == 1)(functools.partial(store, sent_ref))


def back_project(core, grad_q, grad_kv, weights):
    shape = (2, grad_q[0].shape[0] // 2, weights.shape[0])
    shapes = shaped(shape, F32), shaped(shape, BF16)
    arrays = *grad_q, *grad_kv, weights
    return call(back_kernel, "back_project", shapes, (core.reshape(1),), *arrays)


def step_kernel(plans, mine_ref, *refs):
    for number, plan in enumerate(plans):
        held_ref, came_ref = refs[plan["held"]], refs[plan["came"]]
        count, share, columns = held_ref.shape
        came_at, came_column = plan["came_at"]
        sent_at, sent_column = plan["sent_at"]

        def store(mine):
            for index in range(count):
                value = held_ref[index].astype(F32) + came_ref[
                    came_at + index, :share, came_column : came_column + columns
                ].astype(F32)
                digit, target = plan["places"][index]
                if digit == mine:
                    kept_ref = refs[plan["kept"]]
                    kept_ref[target] = value.astype(kept_ref.dtype)
                else:
                    sent_ref = refs[plan["sent"]]
                    sent_ref[sent_at + target, :share, sent_column : sent_column + columns] = (
                        value.astype(sent_ref.dtype)
                    )

        if plan["digit"] is None:
            store(0)
        else:
            pl.when(mine_ref[plan["digit"]] == 0)(functools.partial(store, 0))
            pl.when(mine_ref[plan["digit"]] == 1)(functools.partial(store, 1))


def finish_kernel(plans, core_ref, *refs):
    *own_refs, other_ref = refs[: -len(plans)]
    first_core = core_ref[0] == 0
    for plan, out_ref in zip(plans, refs[-len(plans) :]):
        for side, (source, column, other_column) in enumerate(plan):
            half = out_ref.shape[1] // 2
            own = own_refs[source][:, column : column + half // 2]
            other = other_ref[:, other_column : other_column + half // 2]
            pair = [jnp.where(first_core, own, other), jnp.where(first_core, other, own)]
            out_ref[:, side * half : (side + 1) * half] = jnp.concatenate(pair, axis=1)


def finish_columns(core, own, other, half, mixed):
    quarter = half // 2
    plans = []
    for index in range(len(own)):
        sources = [index, index]
        columns = [0, quarter]
        if mixed and index >= len(own) - 2:
            sources = [len(own) - 2, len(own) - 1]
            columns = [(index - len(own) + 2) * quarter] * 2
        plans.append([(s, col, s * half + col) for s, col in zip(sources, columns)])
    shapes = [shaped((own[0].shape[0], 2 * half), F32)] * len(own)
    kernel = functools.partial(finish_kernel, plans)
    return call(kernel, "finish_columns", shapes, (core.reshape(1),), *own, other)


def local(
    tokens,
    lengths,
    norm_attn,
    norm_mlp,
    query_scale,
    query_proj,
    key_proj,
    value_proj,
    output_proj,
    gate_proj,
    up_proj,
    down_proj,
    cotangent,
):
    place = {name: lax.axis_index(name) for name in ("y", "c", "z", "x")}
    y, c, x = place["y"], place["c"], place["x"]
    line = lax.axis_size("z")
    bits = line_bits(line)
    rows = tokens.shape[1]
    share, width = query_proj.shape
    half = width // 2
    quarter = width // 4
    chip_rows = 2 * rows
    length = 4 * rows

    near = ("z", 1)
    far = [("z", bit) for bit in reversed(bits[1:])]
    orders = (
        far + [("x", 1), ("y", 1), near],
        far + [("y", 1), near, ("x", 1)],
        far + [near, ("x", 1), ("y", 1)],
    )
    vector_columns = jnp.pad(
        jnp.stack([norm_attn, norm_mlp, query_scale], axis=1), ((0, 0), (0, 125))
    )
    attn_block, gate_up_block = column_sides(
        c, (query_proj, key_proj, value_proj, gate_proj, up_proj), vector_columns
    )
    own_tokens = tokens[0]
    other_tokens = across(own_tokens, "c", 1)
    other_cotangent = across(cotangent[0], "c", 1)
    before = across(own_tokens, "y", 1)
    other_before = across(before, "c", 1)
    chip_tokens = in_order(own_tokens, other_tokens, c, 0)
    chip_before = in_order(before, other_before, c, 0)
    all_tokens = jnp.concatenate([chip_before, chip_tokens], axis=0)

    attn_pieces, first = far_pieces(attn_block, far, (), (before,))
    attn_others = other_cores(attn_pieces, other_tokens, other_cotangent)
    cuts = (0, half + 128, 2 * half + 128, 3 * half + 128)
    attn_chains = [
        Chain(blocks, 2, order, len(far))
        for blocks, order in zip(
            side_blocks(attn_pieces, attn_others, list(zip(cuts, cuts[1:]))), orders
        )
    ]
    places_now = jnp.stack([place[name] for name in ("y", "c", "z", "x")])
    second = advance_all(attn_chains)
    gate_up_pieces, middle = far_pieces(gate_up_block, far, first, second)
    third = advance_all(attn_chains, other_before, *middle)
    output_pieces, late = far_pieces(output_proj, far, (*middle, *second, other_before))
    gate_up_sent = jnp.stack([piece[1] for piece in gate_up_pieces])
    gate_up_others = across(after(gate_up_sent, other_before), "c", 1)
    gate_up_sides = side_blocks(
        gate_up_pieces, list(gate_up_others), [(0, half), (half, width)]
    )
    mlp_chains = [
        Chain(blocks, 2, order, len(far)) for blocks, order in zip(gate_up_sides, orders)
    ]
    output_sides = [piece[:, cut : cut + half] for piece in output_pieces for cut in (0, half)]
    mlp_chains.append(Chain(jnp.stack(output_sides), 2, orders[2], len(far)))
    advance_together(attn_chains[1:] + attn_chains[:1], mlp_chains)
    fourth = [chain.last for chain in attn_chains]
    mlp_third = advance_all(mlp_chains)
    down_pieces, _ = far_pieces(down_proj, far, third)
    down_chains = [
        Chain(jnp.stack([piece[:, cut : cut + half] for piece in down_pieces]), 1, order, len(far))
        for cut, order in zip((0, half), orders)
    ]
    down_second = advance_all(down_chains, *fourth)

    doc_ends = jnp.cumsum(lengths[0])
    places = jnp.arange(length, dtype=jnp.int32)
    segment = jnp.sum((places[:, None] >= doc_ends[None, :]).astype(jnp.int32), axis=1)
    seg_here = block_of(segment, y, chip_rows)
    seg_before = jnp.where(y == 0, -1, segment[:chip_rows])
    seg_keys = jnp.concatenate([seg_before, seg_here])[None]
    seg_rows = seg_here[:, None]
    first_row = y * chip_rows + jnp.arange(rows, dtype=jnp.int32)
    upstream_b = [
        jnp.where((first_row + core * rows < doc_ends[-1])[:, None], rows_of, 0).astype(BF16)
        for core, rows_of in ((c, cotangent[0]), (1 - c, other_cotangent))
    ]
    upstream = upstream_b[0]
    upstream_b = jnp.concatenate(upstream_b, axis=0)
    both = ((0, 0), (1, 1))
    (attn_weights,) = layout_blocks(
        places_now,
        line,
        [(3 * half + 128, True)],
        [
            (chain, end - cut, [(0, side, flip, cut) for side, flip in both])
            for chain, cut, end in zip(attn_chains, cuts, cuts[1:])
        ],
    )
    q_raw, queries, keys_values, normed_before, normed_here, vectors, scale_rows = project(
        c, all_tokens, attn_weights
    )
    gain_a, gain_m = vectors[0], vectors[1]
    mlp_sent_last = advance_all(mlp_chains, queries)
    down_third = advance_all(down_chains, queries)
    queries = after(queries, *[chain.held for chain in mlp_chains + down_chains])
    attended_f, attended, lse = attention_forward(queries, keys_values, seg_rows, seg_keys)
    attended = after(attended, *mlp_sent_last, *down_third, upstream_b)
    for chain in mlp_chains:
        chain.last = after(chain.last, attended)
    down_last = advance_all(down_chains, attended)

    (proj_o,) = layout_blocks(
        places_now,
        line,
        [(width, False)],
        [(mlp_chains[2], half, [(0, 0, 0, 0), (0, 1, 0, half)])],
    )
    output_own, output_sent = output_project(c, attended, proj_o)
    hidden1, normed_own = norm_middle(
        output_own, across(output_sent, "c", 1), own_tokens, gain_m
    )
    normed_others = [
        across(normed_own[start : start + rows // 2], "c", 1) for start in (0, rows // 2)
    ]
    for chain in mlp_chains[:2]:
        chain.last = after(chain.last, output_sent)
    (proj_gu,) = layout_blocks(
        places_now,
        line,
        [(width, True)],
        [
            (chain, half, [(0, side, flip, cut) for side, flip in both])
            for chain, cut in zip(mlp_chains, (0, half))
        ],
    )
    hidden, gate_pre, up_pre, normed_m = mlp_first((normed_own, *normed_others), proj_gu)
    for chain in down_chains:
        chain.last = after(chain.last, hidden)
    (proj_d,) = layout_blocks(
        places_now,
        line,
        [(width, False)],
        [(chain, half, [(0, 0, 0, cut)]) for chain, cut in zip(down_chains, (0, half))],
    )

    digits = [("y", 1), ("c", 1)] + [("z", bit) for bit in reversed(bits)] + [("x", 1)]
    scatter_orders = [order[len(far) :][::-1] for order in orders]

    output_orders = [("x", 1), ("y", 1), near], [("y", 1), ("x", 1), near]

    def own_digit(axis, bit):
        return (place[axis] // bit) % 2

    def sizes_of(names, by_column):
        return tuple(1 if name == ("c", 1) and not by_column else 2 for name in names)

    def first_step(*groups, gate=(), name="products"):
        mine, plans, states = [], [], []
        for lefts, rights, columns, chain_orders, turned in groups:
            by_column = lefts[0].shape[0 if turned else 1] == width
            dims = sizes_of(digits, by_column)
            chains = []
            for which, order in zip(columns, chain_orders):
                at = digits.index(order[0])
                chains.append((which, dims, at))
                mine.append(own_digit(*order[0]))
                names = digits[:at] + digits[at + 1 :]
                states.append({"names": names, "by_column": by_column, "order": order, "step": 1})
            plans.append((lefts, rights, chains, turned))
        if share % 8 == 0:
            parts = products(jnp.stack(mine).astype(jnp.int32), share, plans, name)
        else:
            parts = []
            for lefts, rights, chains, turned in plans:
                left = jnp.concatenate([each.T if turned else each for each in lefts], axis=0)
                for which, dims, at in chains:
                    right = jnp.concatenate([rights[column] for column in which], axis=1)
                    part = tn(left, right).astype(BF16).reshape(dims + (share, right.shape[1]))
                    digit = mine[len(parts)]
                    parts.append(
                        [
                            lax.dynamic_index_in_dim(part, which_half, at, keepdims=False).reshape(
                                -1, share, right.shape[1]
                            )
                            for which_half in (digit, 1 - digit)
                        ]
                    )
        sent = [after(value, *gate) if gate else value for _, value in parts]
        for state, (kept, _), value in zip(states, parts, sent):
            state.update(held=kept, came=across(value, *state["order"][0]), came_at=(0, 0))
        return states, [value for _, value in parts]

    def step(states, names, *earlier, packed=None, dtype=BF16):
        mine, plans, inputs, shapes = [], [], [], []
        came = [after(state["came"], *earlier) if earlier else state["came"] for state in states]
        sources = {}
        for state, array in zip(states, came):
            key = id(state["came"])
            if key not in sources:
                sources[key] = len(inputs)
                inputs.append(array)
        new_states = []
        for number, (state, name) in enumerate(zip(states, names)):
            dims = sizes_of(state["names"], state["by_column"])
            held = state["held"]
            plan = {"came": sources[id(state["came"])], "came_at": state["came_at"]}
            plan["held"] = len(inputs)
            inputs.append(held)
            at = state["names"].index(name) if name in state["names"] else None
            if at is not None and dims[at] == 1:
                at = None
            rest = [index for index in range(len(dims)) if index != at]
            places = []
            for index in range(held.shape[0]):
                values, left_over = [], index
                for size in reversed(dims):
                    values.append(left_over % size)
                    left_over //= size
                values = values[::-1]
                flat = 0
                for axis_at in rest:
                    flat = flat * dims[axis_at] + values[axis_at]
                places.append((0 if at is None else values[at], flat))
            plan["places"] = places
            plan["digit"] = None if at is None else len(mine)
            if at is not None:
                mine.append(own_digit(*name))
            plan["sent_at"] = packed[1][number] if packed else (0, 0)
            plan["kept"] = len(shapes)
            count = held.shape[0] // (1 if at is None else 2)
            shapes.append(shaped((count,) + held.shape[1:], F32))
            if at is not None and not packed:
                plan["sent"] = len(shapes)
                shapes.append(shaped((count,) + held.shape[1:], dtype))
            plans.append(plan)
            names_left = [state["names"][axis_at] for axis_at in rest]
            new_states.append(dict(state, names=names_left, came_at=plan["sent_at"]))
        if packed:
            for plan in plans:
                plan["sent"] = len(shapes)
            shapes.append(shaped(packed[0], dtype))
        for plan in plans:
            plan["kept"] += 1 + len(inputs) - 1
            if "sent" in plan:
                plan["sent"] += len(inputs)
        if not mine:
            mine = [place["c"]]
        kernel = functools.partial(step_kernel, plans)
        outs = call(kernel, "step", shapes, (jnp.stack(mine).astype(jnp.int32),), *inputs)
        for plan, state in zip(plans, new_states):
            state["held"] = outs[plan["kept"] - len(inputs)]
        if packed:
            return new_states, outs[-1]
        return new_states, [
            outs[plan["sent"] - len(inputs)] if plan["digit"] is not None else None
            for plan in plans
        ]

    def halve(states, *earlier):
        names = [state["order"][state["step"]] for state in states]
        states, sent = step(states, names, *earlier)
        for state, value, name in zip(states, sent, names):
            state.update(came=across(value, *name), came_at=(0, 0), step=state["step"] + 1)
        return states, sent

    def halve_far(states, shape, places, *earlier):
        for axis, bit in far[::-1][:-1]:
            states, sent = step(states, [(axis, bit)] * len(states))
            for state, value in zip(states, sent):
                state.update(came=across(value, axis, bit), came_at=(0, 0))
        last = far[0]
        states, message = step(states, [last] * len(states), *earlier, packed=(shape, places))
        arrived = across(message, *last)
        for state in states:
            state.update(came=arrived)
        return states, message

    def join_columns(states):
        left, right = states
        joined = dict(left, came_at=(0, 0))
        for key in ("held", "came"):
            joined[key] = jnp.concatenate([left[key], right[key]], axis=2)
        return [joined]

    def received(states):
        return [state["came"] for state in states]

    down_states, down_sent = first_step(
        ((hidden,), (upstream_b,), ((0,),), scatter_orders[:1], False), name="products_down"
    )
    grad_gate, grad_up = mlp_last(gate_pre, up_pre, proj_d, after(upstream_b, *down_sent))
    gate_own, gate_sent = rows_product((grad_gate, grad_up), proj_gu, True, "gate_up_back")
    mlp_states, mlp_sent = first_step(
        (
            (normed_m,),
            after((grad_gate, grad_up), gate_sent),
            ((0,), (1,)),
            scatter_orders[1:],
            False,
        ),
        name="products_mlp",
    )
    mlp_states = down_states + mlp_states
    gate_own = after(gate_own, *mlp_sent)
    grad_hidden1, low_own, grad_gain_m = middle_back(
        gate_own, across(gate_sent, "c", 1), hidden1, upstream, gain_m
    )
    grad_attended, grad_hidden1_b = attended_back(c, low_own, across(low_own, "c", 1), proj_o)
    scale_row = scale_rows[:1]
    heads = half // HD
    residuals = (queries, keys_values), (attended_f, lse, seg_rows, seg_keys, q_raw, scale_row)
    grad_q_early, grad_kv_early, early_sums = attention_backward(
        0, heads // 2, *residuals[0], grad_attended, *residuals[1]
    )
    down_own, down_sent = rows_product(
        (after(hidden, grad_attended),), proj_d, False, "down_project"
    )
    down_other = across(down_sent, "c", 1)
    block_out = hidden1 + down_own + down_other
    mlp_states, mlp_sent = halve(mlp_states, grad_kv_early, down_other)
    grad_rows = after(grad_hidden1_b, *mlp_sent)
    output_rights = grad_rows[:, :half], grad_rows[:, half:]
    output_states, output_sent = first_step(
        ((attended,), output_rights, ((0,), (1,)), output_orders, False)
    )
    grad_attended = after(grad_attended, *mlp_sent, *output_sent)
    grad_q_late, grad_kv_late, late_sums = attention_backward(
        heads // 2, heads, *residuals[0], grad_attended, *residuals[1]
    )
    grad_scale = jnp.concatenate([early_sums[0], late_sums[0]]) * scale_rows[1]
    grads = (grad_q_early, grad_q_late), (grad_kv_early, grad_kv_late)
    mlp_states, mlp_sent = halve(mlp_states, grad_kv_late)
    output_states, output_sent = halve(output_states, grad_kv_late)
    grads = after(grads, *mlp_sent, *output_sent)
    attn_states, attn_sent = first_step(
        ((normed_here,), grads[0], ((0, 1),), scatter_orders[:1], False),
        ((normed_before, normed_here), grads[1], ((0,), (1,)), scatter_orders[1:], False),
        gate=received(mlp_states + output_states),
    )
    first_done = received(attn_states)
    grads = after(grads, *attn_sent)
    mlp_states, _ = halve_far(
        mlp_states, (3, share, width), ((2, 0), (0, 0), (0, half)), *attn_sent
    )
    back_own, back_sent = back_project(c, *grads, attn_weights)
    back_other = across(back_sent, "c", 1)
    output_states = join_columns(
        [dict(state, came=after(state["came"], *first_done)) for state in output_states]
    )
    output_states, _ = halve(output_states)
    attn_states, _ = halve(attn_states, mlp_states[0]["came"], back_own)
    second_done = received(attn_states)
    grad_here, grad_before, grad_gain_a = gain_terms(back_own, back_other, own_tokens, before)
    scale_rows = grad_scale.reshape(2, 1, quarter)
    scale_rows = jnp.where(
        c == 0,
        jnp.pad(scale_rows, ((0, 0), (0, 1), (0, 0))),
        jnp.pad(scale_rows, ((0, 0), (1, 0), (0, 0))),
    ).reshape(width)
    vector_terms = jnp.stack([grad_gain_a[0], grad_gain_m[0], scale_rows])
    vector_rows = min(8, share)
    vector_terms = jnp.moveaxis(vector_terms.reshape(3, -1, share), 0, 1)
    room = ((0, 0), (0, vector_rows - 3), (0, 128 - share))
    vector_terms = jnp.pad(vector_terms, room)
    vector_order = [near] + far[::-1] + [("x", 1), ("y", 1)]
    vector_state = {"names": digits, "by_column": True, "order": vector_order, "step": 0}
    zero_terms = jnp.zeros(vector_terms.shape, BF16)
    vector_states = [dict(vector_state, held=vector_terms, came=zero_terms, came_at=(0, 0))]
    vector_states, _ = halve(vector_states)
    attn_states, _ = halve(attn_states, *received(output_states + vector_states))
    third_done = received(attn_states)
    output_states, _ = halve_far(output_states, (1, share, width), ((0, 0),))
    for _ in far:
        vector_states, _ = halve(vector_states)
    vector_first = received(vector_states)
    vector_states, _ = halve(vector_states, *third_done)
    vector_second = received(vector_states)
    grad_after = across(after(grad_before, *third_done), "y", 1)
    grad_inputs = tokens_back(y, grad_here, grad_after, own_tokens, gain_a, grad_hidden1)

    attn_places = [(0, number * half) for number in range(3)]
    final_states, final_message = halve_far(
        attn_states, (2, share, 3 * half), attn_places, *received(output_states), *vector_first
    )
    vector_states, _ = halve(vector_states, grad_after)
    vector_third = received(vector_states)
    mlp_states, sent = step(
        mlp_states,
        [("c", 1)] * 3,
        final_message,
        packed=((1, share, width), ((0, 0), (0, 0), (0, half))),
        dtype=F32,
    )
    mlp_parts = [state["held"][0] for state in mlp_states]
    gate_up_other = across(sent[0], "c", 1)
    gate_up_grads = finish_columns(c, mlp_parts[1:], gate_up_other, half, False)
    final_states, sent = step(
        final_states,
        [("c", 1)] * 3,
        grad_after,
        gate_up_other,
        packed=((1, share, 3 * half), attn_places),
        dtype=F32,
    )
    output_states, _ = step(output_states, [("c", 1)], final_message)
    own_parts = [state["held"][0] for state in final_states + output_states]
    other = across(sent[0], "c", 1)
    attn_grads = finish_columns(c, own_parts[:3], other, half, True)
    vector_states, vector_sent = step(vector_states, [("c", 1)], dtype=F32)
    vector_other = across(vector_sent[0][0], "c", 1)
    summed = (vector_states[0]["held"][0] + vector_other)[:, :share]
    return (
        block_out.astype(BF16)[None],
        grad_inputs[None],
        summed[0],
        summed[1],
        summed[2],
        *attn_grads,
        own_parts[3],
        *gate_up_grads,
        mlp_parts[0],
    )


def solution(mesh):
    seq, dp = mesh.devices.shape
    axes = Mesh(mesh.devices.reshape(seq // 2, 2, dp // 2, 2), ("y", "c", "z", "x"))
    batch, places, every = ("z", "x"), ("y", "c"), ("y", "c", "z", "x")
    activations = P(batch, places, None)
    vector, matrix = P(every), P(every, None)
    return jax.shard_map(
        local,
        mesh=axes,
        in_specs=(activations, P(batch, None)) + (vector,) * 3 + (matrix,) * 7 + (activations,),
        out_specs=(activations, activations) + (vector,) * 3 + (matrix,) * 7,
        check_vma=False,
    )
```

```python
import functools

import jax
import jax.numpy as jnp
from jax import lax
from jax.experimental import pallas as pl
from jax.experimental.pallas import tpu as pltpu
from jax.sharding import Mesh, PartitionSpec as P

H = 16
HD = 80
EPSILON = 1e-06
R_SOFTPLUS = 1.442695041
MASKED = -1e30
QUERY_ROWS = 256
VMEM_BYTES = 24 << 20
VMEM_MOST = 56 << 20
SPEED = 4600000000
COSTS = {
    "project": 5,
    "attention_forward": 13,
    "output_project": 0,
    "mlp_middle": 3,
    "gate_up_back": 3,
    "products": 6,
    "attention_backward": 10,
    "back_project": 0,
    "join": 3,
    "tokens_back": 3,
    "layout_blocks": 2,
    "norm_middle": 0,
    "mlp_first": 2,
    "products_down": 2,
    "mlp_last": 2,
    "products_mlp": 4,
    "attention_early": 5,
}
F32 = jnp.float32
BF16 = jnp.bfloat16


def nn(left, right):
    return jnp.dot(left, right, preferred_element_type=F32)


def nt(left, right):
    return lax.dot_general(left, right, (((1,), (1,)), ((), ())), preferred_element_type=F32)


def tn(left, right):
    return lax.dot_general(left, right, (((0,), (0,)), ((), ())), preferred_element_type=F32)


def allowed_pairs(seg_rows, seg_keys, half, first, rows):
    total = seg_keys.shape[1]
    row_ids = lax.broadcasted_iota(jnp.int32, (rows, total), 0) + (first + half)
    col_ids = lax.broadcasted_iota(jnp.int32, (rows, total), 1)
    return (seg_rows == seg_keys) & (col_ids <= row_ids)


WHOLE = pl.BlockSpec(memory_space=pltpu.VMEM)
SCALARS = pl.BlockSpec(memory_space=pltpu.SMEM)
ANYWHERE = pl.BlockSpec(memory_space=pl.ANY)


def call(kernel, name, out_shape, scalars, *arrays, scratch=()):
    specs = [SCALARS] * len(scalars) + [ANYWHERE if scratch else WHOLE] * len(arrays)
    return pl.pallas_call(
        kernel,
        out_shape=out_shape,
        in_specs=specs,
        out_specs=jax.tree.map(lambda shape: WHOLE, out_shape),
        compiler_params=pltpu.CompilerParams(vmem_limit_bytes=VMEM_MOST if scratch else VMEM_BYTES),
        scratch_shapes=scratch,
        cost_estimate=pl.CostEstimate(flops=COSTS.get(name, 2) * SPEED, bytes_accessed=0, transcendentals=0),
        name=name,
    )(*scalars, *arrays)


def shaped(shape, dtype):
    return jax.ShapeDtypeStruct(tuple(shape), dtype)


def project_kernel(
    core_ref, tokens_ref, weight_ref, raw_ref, q_ref, kv_ref, before_ref, here_ref, vectors_ref,
    scale_ref
):
    chip_rows, half = raw_ref.shape
    quarter = half // 2
    vectors = weight_ref[:, half : half + 128].astype(F32).T[:8]
    keys = half + 128
    vectors_ref[...] = vectors
    gain = vectors[0:1]
    logits = [
        jnp.concatenate(
            [vectors[2:3, side * half + core * quarter :][:, :quarter] for side in range(2)], axis=1
        )
        for core in range(2)
    ]
    logit = jnp.where(core_ref[0] == 0, logits[0], logits[1])
    softplus = jnp.maximum(logit, 0.0) + jnp.log1p(jnp.exp(-jnp.abs(logit)))
    scale = R_SOFTPLUS * HD ** (-0.5) * softplus
    scale_ref[0:1] = scale
    scale_ref[1:2] = R_SOFTPLUS * HD ** (-0.5) / (1.0 + jnp.exp(-logit))
    for first in range(0, 2 * chip_rows, QUERY_ROWS):
        rows = slice(first, first + QUERY_ROWS)
        values = tokens_ref[rows, :].astype(F32)
        inverse = lax.rsqrt(jnp.mean(values * values, axis=1, keepdims=True) + EPSILON)
        normed = (values * inverse * gain).astype(BF16)
        kv_ref[rows, :] = nn(normed, weight_ref[:, keys : keys + 2 * half]).astype(BF16)
        if first >= chip_rows:
            here = slice(first - chip_rows, first - chip_rows + QUERY_ROWS)
            here_ref[here, :] = normed
            raw = nn(normed, weight_ref[:, :half])
            raw_ref[here, :] = raw
            q_ref[here, :] = (raw * scale).astype(BF16)
        else:
            before_ref[rows, :] = normed


def project(core, tokens, weights):
    rows, width = tokens.shape
    half = width // 2
    shapes = (
        shaped((rows // 2, half), F32),
        shaped((rows // 2, half), BF16),
        shaped((rows, width), BF16),
        shaped((rows // 2, width), BF16),
        shaped((rows // 2, width), BF16),
        shaped((8, width), F32),
        shaped((2, half), F32),
    )
    return call(project_kernel, "project", shapes, (core.reshape(1),), tokens, weights)


def key_value_columns(head, width):
    half = width // 2
    start = head * HD // half * width + head * HD % half
    return slice(start, start + HD), slice(start + half, start + half + HD)


def forward_kernel(q_ref, kv_ref, segq_ref, segk_ref, out_ref, low_ref, lse_ref):
    half, width = q_ref.shape
    for first in range(0, half, QUERY_ROWS):
        rows = slice(first, first + QUERY_ROWS)
        end = half + first + QUERY_ROWS
        allowed = allowed_pairs(segq_ref[rows, :], segk_ref[:, :end], half, first, QUERY_ROWS)
        outs, lses = [], []
        for head in range(width // HD):
            cols = slice(head * HD, (head + 1) * HD)
            key_cols, value_cols = key_value_columns(head, width)
            scores = jnp.where(allowed, nt(q_ref[rows, cols], kv_ref[:end, key_cols]), MASKED)
            top = jnp.max(scores, axis=1, keepdims=True)
            exps = jnp.exp(scores - top)
            total = jnp.sum(exps, axis=1, keepdims=True)
            probs = (exps * (1.0 / total)).astype(BF16)
            outs.append(nn(probs, kv_ref[:end, value_cols]))
            lses.append(top + jnp.log(total))
        out = jnp.concatenate(outs, axis=1)
        out_ref[rows, :] = out
        low_ref[rows, :] = out.astype(BF16)
        lse_ref[rows, :] = jnp.concatenate(lses, axis=1)


def attention_forward(q, kv, segq, segk):
    shapes = (
        shaped(q.shape, F32),
        shaped(q.shape, BF16),
        shaped((q.shape[0], q.shape[1] // HD), F32),
    )
    return call(forward_kernel, "attention_forward", shapes, (), q, kv, segq, segk)


def backward_kernel(first_head, last_head, *refs):
    q_ref, kv_ref, go_ref, out_ref, lse_ref, segq_ref, segk_ref, raw_ref, scale_ref = refs[:9]
    dq_ref, dkv_ref, sum_ref = refs[9:]
    half, width = q_ref.shape
    heads = range(first_head, last_head)
    span = slice(first_head * HD, last_head * HD)
    dks, dvs = [None] * len(heads), [None] * len(heads)
    sums = 0.0
    for first in reversed(range(0, half, QUERY_ROWS)):
        rows = slice(first, first + QUERY_ROWS)
        end = half + first + QUERY_ROWS
        allowed = allowed_pairs(segq_ref[rows, :], segk_ref[:, :end], half, first, QUERY_ROWS)
        products = go_ref[rows, :].astype(F32) * out_ref[rows, :]
        dqs = []
        for number, head in enumerate(heads):
            cols = slice(head * HD, (head + 1) * HD)
            key_cols, value_cols = key_value_columns(head, width)
            queries, keys = q_ref[rows, cols], kv_ref[:end, key_cols]
            values = kv_ref[:end, value_cols]
            grads = go_ref[rows, cols]
            scores = jnp.where(allowed, nt(queries, keys), MASKED)
            probs = jnp.exp(scores - lse_ref[rows, head : head + 1])
            delta = jnp.sum(products[:, cols], axis=1, keepdims=True)
            grad_scores = (probs * (nt(grads, values) - delta)).astype(BF16)
            dqs.append(nn(grad_scores, keys))
            for sums_of, term in (
                (dks, tn(grad_scores, queries)),
                (dvs, tn(probs.astype(BF16), grads)),
            ):
                held = sums_of[number]
                if held is None:
                    sums_of[number] = term
                else:
                    sums_of[number] = jnp.concatenate([held[:end] + term, held[end:]], axis=0)
        dq = jnp.concatenate(dqs, axis=1)
        sums = sums + jnp.sum(dq * raw_ref[rows, span], axis=0, keepdims=True)
        dq_ref[rows, :] = (dq * scale_ref[:, span]).astype(BF16)
    sum_ref[...] = sums
    dkv_ref[...] = jnp.concatenate(dks + dvs, axis=1).astype(BF16)


def attention_backward(first_head, last_head, q, kv, *rest):
    columns = (last_head - first_head) * HD
    shapes = (
        shaped((q.shape[0], columns), BF16),
        shaped((kv.shape[0], 2 * columns), BF16),
        shaped((1, columns), F32),
    )
    kernel = functools.partial(backward_kernel, first_head, last_head)
    name = "attention_backward" if first_head else "attention_early"
    return call(kernel, name, shapes, (), q, kv, *rest)


def output_kernel(core_ref, attended_ref, weight_ref, own_ref, sent_ref):
    rows = own_ref.shape[0]
    for block in range(2):
        result = nn(attended_ref[block * rows : (block + 1) * rows, :], weight_ref[...])
        side = core_ref[0] ^ block

        def store(out_ref):
            out_ref[...] = result

        pl.when(side == 0)(functools.partial(store, own_ref))
        pl.when(side == 1)(functools.partial(store, sent_ref))


def output_project(core, attended, weight):
    shape = shaped((attended.shape[0] // 2, weight.shape[1]), F32)
    return call(
        output_kernel, "output_project", (shape, shape), (core.reshape(1),), attended, weight
    )


def norm_kernel(own_ref, came_ref, tokens_ref, gain_ref, hidden_ref, normed_ref):
    hidden = tokens_ref[...].astype(F32) + own_ref[...] + came_ref[...]
    hidden_ref[...] = hidden
    inverse = lax.rsqrt(jnp.mean(hidden * hidden, axis=1, keepdims=True) + EPSILON)
    normed_ref[...] = (hidden * inverse * gain_ref[...]).astype(BF16)


def norm_middle(own, came, tokens, gain):
    shapes = shaped(own.shape, F32), shaped(own.shape, BF16)
    return call(norm_kernel, "norm_middle", shapes, (), own, came, tokens, gain[None])


def mlp_first_kernel(*refs):
    *normed_refs, weight_ref, hidden_ref, gate_ref, up_ref, normed_ref = refs
    half = hidden_ref.shape[1]
    start = 0
    for ref in normed_refs:
        rows = slice(start, start + ref.shape[0])
        start += ref.shape[0]
        normed = ref[...]
        normed_ref[rows, :] = normed
        gate_up = nn(normed, weight_ref[...])
        gate, up = gate_up[:, :half], gate_up[:, half:]
        gate_ref[rows, :] = gate
        up_ref[rows, :] = up
        hidden_ref[rows, :] = (gate * jax.nn.sigmoid(gate) * up).astype(BF16)


def mlp_first(normed, weight):
    rows = sum(part.shape[0] for part in normed)
    half = weight.shape[1] // 2
    wide = shaped((rows, half), F32)
    shapes = shaped((rows, half), BF16), wide, wide, shaped((rows, weight.shape[0]), BF16)
    return call(mlp_first_kernel, "mlp_first", shapes, (), *normed, weight)


def mlp_last_kernel(gate_in_ref, up_in_ref, down_ref, upstream_ref, gate_ref, up_ref):
    for first in range(0, gate_ref.shape[0], QUERY_ROWS):
        rows = slice(first, first + QUERY_ROWS)
        gate, up = gate_in_ref[rows, :], up_in_ref[rows, :]
        sigmoid = jax.nn.sigmoid(gate)
        grad = nt(upstream_ref[rows, :], down_ref[...])
        gate_ref[rows, :] = (
            grad * up * sigmoid * (1.0 + gate * (1.0 - sigmoid))
        ).astype(BF16)
        up_ref[rows, :] = (grad * gate * sigmoid).astype(BF16)


def mlp_last(gate, up, down, upstream):
    shape = shaped(gate.shape, BF16)
    return call(mlp_last_kernel, "mlp_last", (shape, shape), (), gate, up, down, upstream)


def rows_kernel(transposed, *refs):
    *left_refs, right_ref, own_ref, sent_ref = refs
    rows = own_ref.shape[0]
    for block, out_ref in enumerate((own_ref, sent_ref)):
        total, start = 0.0, 0
        for left_ref in left_refs:
            left = left_ref[block * rows : (block + 1) * rows, :]
            if transposed:
                total = total + nt(left, right_ref[:, start : start + left.shape[1]])
            else:
                total = total + nn(left, right_ref[start : start + left.shape[1], :])
            start += left.shape[1]
        out_ref[...] = total


def rows_product(lefts, right, transposed, name):
    columns = right.shape[0] if transposed else right.shape[1]
    shape = shaped((lefts[0].shape[0] // 2, columns), F32)
    kernel = functools.partial(rows_kernel, transposed)
    return call(kernel, name, (shape, shape), (), *lefts, right)


def norm_back(values, gain, upstream):
    inverse = lax.rsqrt(jnp.mean(values * values, axis=1, keepdims=True) + EPSILON)
    scaled = upstream * gain
    back = inverse * scaled - values * inverse**3 * jnp.mean(values * scaled, axis=1, keepdims=True)
    return back, jnp.sum(upstream * values * inverse, axis=0, keepdims=True)


def middle_back_kernel(own_ref, came_ref, hidden_ref, upstream_ref, gain_ref, grad_ref, low_ref, sum_ref):
    back, sums = norm_back(hidden_ref[...], gain_ref[...], own_ref[...] + came_ref[...])
    grad = upstream_ref[...].astype(F32) + back
    grad_ref[...] = grad
    low_ref[...] = grad.astype(BF16)
    sum_ref[...] = sums


def middle_back(own, came, hidden, upstream, gain):
    shapes = shaped(own.shape, F32), shaped(own.shape, BF16), shaped((1, own.shape[1]), F32)
    return call(
        middle_back_kernel, "middle_back", shapes, (), own, came, hidden, upstream, gain[None]
    )


def attended_kernel(core_ref, *refs):
    own_ref, *other_refs, weight_ref, grad_ref, rows_ref = refs
    rows = own_ref.shape[0]
    for block, parts in enumerate(([own_ref], other_refs)):
        first = (core_ref[0] ^ block) * rows
        for number, ref in enumerate(parts):
            size = ref.shape[0]
            place = pl.ds(pl.multiple_of(first + number * size, size), size)
            grad_ref[place, :] = nt(ref[...], weight_ref[...]).astype(BF16)
            rows_ref[place, :] = ref[...]


def attended_back(core, own, others, weight):
    rows, width = own.shape
    shapes = shaped((2 * rows, weight.shape[0]), BF16), shaped((2 * rows, width), BF16)
    return call(
        attended_kernel, "attended_back", shapes, (core.reshape(1),), own, *others, weight
    )


def gain_kernel(own_ref, came_ref, tokens_ref, before_ref, here_ref, sent_ref, sum_ref):
    total = 0.0
    for part, ref in enumerate((tokens_ref, before_ref)):
        grad = own_ref[part] + came_ref[part]
        values = ref[...].astype(F32)
        inverse = lax.rsqrt(jnp.mean(values * values, axis=1, keepdims=True) + EPSILON)
        total = total + jnp.sum(grad * values * inverse, axis=0, keepdims=True)
        if part == 0:
            here_ref[...] = grad
        else:
            sent_ref[...] = grad.astype(BF16)
    sum_ref[...] = total


def gain_terms(own, came, tokens, before):
    rows, width = tokens.shape
    shapes = shaped((rows, width), F32), shaped((rows, width), BF16), shaped((1, width), F32)
    return call(gain_kernel, "gain_terms", shapes, (), own, came, tokens, before)


def tokens_kernel(first_ref, here_ref, after_ref, tokens_ref, gain_ref, hidden_ref, out_ref):
    later = jnp.where(first_ref[0] == 0, after_ref[...].astype(F32), 0.0)
    back, _ = norm_back(tokens_ref[...].astype(F32), gain_ref[...], here_ref[...] + later)
    out_ref[...] = hidden_ref[...] + back


def tokens_back(first, here, after_rows, tokens, gain, grad_hidden):
    shape = shaped(here.shape, F32)
    arrays = here, after_rows, tokens, gain[None], grad_hidden
    return call(tokens_kernel, "tokens_back", shape, (first.reshape(1),), *arrays)


def pick(pair, index):
    return jnp.where(index == 0, pair[0], pair[1])


def in_order(own, other, index, axis):
    return jnp.where(
        index == 0,
        jnp.concatenate([own, other], axis=axis),
        jnp.concatenate([other, own], axis=axis),
    )


def block_of(matrix, index, size, axis=0):
    return lax.dynamic_slice_in_dim(matrix, index * size, size, axis)


def across(value, axis, bit):
    count = lax.axis_size(axis)
    return lax.ppermute(value, axis, [(place, place ^ bit) for place in range(count)])


def line_bits(count):
    return [1 << power for power in range(count.bit_length() - 1)]


def after(values, *earlier):
    return lax.optimization_barrier((values, earlier))[0]


def far_pieces(block, far, before=(), then=()):
    pieces, arrived = [block], ()
    for axis, bit in far:
        message = block if len(pieces) == 1 else jnp.stack(pieces)
        came = across(after(message, *before) if before else message, axis, bit)
        arrived = (came,)
        came = after(came, *then) if then else came
        pieces += [came] if len(pieces) == 1 else [came[index] for index in range(len(pieces))]
    return pieces, arrived


def other_cores(pieces, *earlier):
    own = pieces[0][1]
    first = across(after(own, *earlier) if earlier else own, "c", 1)
    if len(pieces) == 2:
        return [first, across(pieces[1][1], "c", 1)]
    rest = [piece[1] for piece in pieces[1:]]
    return [first] + (list(across(jnp.stack(rest), "c", 1)) if rest else [])


def side_kernel(cuts, *refs):
    count = (len(refs) - len(cuts)) // 2
    for index in range(count):
        for (first, last), out_ref in zip(cuts, refs[2 * count :]):
            out_ref[2 * index] = refs[index][0, :, first:last]
            out_ref[2 * index + 1] = refs[count + index][:, first:last]


def side_blocks(pieces, others, cuts):
    share = pieces[0].shape[1]
    shapes = [shaped((2 * len(pieces), share, last - first), BF16) for first, last in cuts]
    kernel = functools.partial(side_kernel, cuts)
    return call(kernel, "side_blocks", shapes, (), *pieces, *others)


def join_kernel(starts, *refs):
    count = len(refs) // 3
    for number, start in enumerate(starts):
        first_ref, second_ref, out_ref = refs[number], refs[count + number], refs[2 * count + number]
        size, _, columns = first_ref.shape
        out_ref[:size] = first_ref[...]
        out_ref[size:] = second_ref[start : start + size, :, :columns]


def join(firsts, seconds, starts):
    shapes = [shaped((2 * first.shape[0],) + first.shape[1:], first.dtype) for first in firsts]
    kernel = functools.partial(join_kernel, starts)
    return call(kernel, "join", shapes, (), *firsts, *seconds)


class Chain:
    def __init__(self, held, sides, order, step):
        self.sides = sides
        self.held, self.last, self.start = None, held, 0
        self.order, self.step = order, step


def take_all(chains, *earlier):
    lasts = [after(chain.last, *earlier) if earlier else chain.last for chain in chains]
    if chains[0].held is None:
        helds = lasts
    else:
        starts = [chain.start for chain in chains]
        helds = join([chain.held for chain in chains], lasts, starts)
    for chain, held in zip(chains, helds):
        chain.held, chain.start = held, 0


def advance_all(chains, *earlier):
    take_all(chains, *earlier)
    for chain in chains:
        chain.last = across(chain.held, *chain.order[chain.step])
        chain.step += 1
    return [chain.last for chain in chains]


def together_kernel(count, *refs):
    for number in range(count):
        first_ref, second_ref, short_ref, out_ref = refs[number::count]
        size = first_ref.shape[0]
        out_ref[:size] = first_ref[...]
        out_ref[size : 2 * size] = second_ref[...]
        out_ref[2 * size :, :, : short_ref.shape[2]] = short_ref[...]


def advance_together(longs, shorts):
    take_all(shorts)
    shapes = [
        shaped((2 * long.held.shape[0] + short.held.shape[0],) + long.held.shape[1:], BF16)
        for long, short in zip(longs, shorts)
    ]
    arrays = [long.held for long in longs] + [long.last for long in longs]
    arrays += [short.held for short in shorts]
    kernel = functools.partial(together_kernel, len(longs))
    messages = call(kernel, "together", shapes, (), *arrays)
    for long, short, message in zip(longs, shorts, messages):
        came = across(message, *long.order[long.step])
        count = 2 * long.held.shape[0]
        long.held, long.last, long.count = message, came, count
        short.last, short.start = came, count
        long.step += 1
        short.step += 1


def layout_kernel(plans, count_out, place_ref, *refs):
    out_refs = refs[-count_out:]
    for source, (line, sides, count, columns, steps, base, placed) in enumerate(plans):
        devices = 4 * line
        for index in range(count // sides):
            flips = dict(base)
            for power, (axis, bit) in enumerate(steps):
                if index >> power & 1:
                    flips[axis] = flips.get(axis, 0) ^ bit
            for number, by_column, side, core_flip, column in placed:
                strides = {"y": devices, "z": 2, "x": 1, "c": devices // 2}
                if not by_column:
                    strides["y"], strides["c"] = devices // 2, 0
                flips["c"] = core_flip
                target = 0
                for at, axis in enumerate(("y", "c", "z", "x")):
                    target += (place_ref[at] ^ flips.get(axis, 0)) * strides[axis]
                out_refs[number][target, :, column : column + columns] = refs[source][
                    index * sides + side, :, :columns
                ]


def layout_blocks(place, line, widths, chains):
    plans, sources = [], []
    for chain, columns, placed in chains:
        count = getattr(chain, "count", chain.held.shape[0])
        placed = [(number, widths[number][1], *rest) for number, *rest in placed]
        for base in ((), chain.order[-1:]):
            plans.append((line, chain.sides, count, columns, chain.order[:-1], base, placed))
        sources += [chain.held, chain.last]
    share = sources[0].shape[1]
    shapes = [
        shaped(((8 if by_column else 4) * line, share, width), BF16) for width, by_column in widths
    ]
    kernel = functools.partial(layout_kernel, plans, len(widths))
    outs = call(kernel, "layout_blocks", shapes, (place,), *sources)
    return [out.reshape(out.shape[0] * share, out.shape[2]) for out in outs]


def gathered_kernel(kernel, count, core_ref, *refs):
    copies = [
        pltpu.make_async_copy(refs[number], refs[number - count - 1], refs[-1].at[number])
        for number in range(count)
    ]
    for copy in copies:
        copy.start()
    for copy in copies:
        copy.wait()
    kernel(core_ref, *refs[-count - 1 : -1], *refs[count : -count - 1])


def sides_kernel(core_ref, *refs):
    *weight_refs, vector_ref, attn_ref, gate_up_ref = refs
    share, width = weight_refs[0].shape
    half, quarter = width // 2, width // 4
    for number, weight_ref in enumerate(weight_refs):
        out_ref, column = (attn_ref, number) if number < 3 else (gate_up_ref, number - 3)
        start = column * half
        for core in range(2):
            parts = [
                weight_ref[:, side * half + core * quarter : side * half + (core + 1) * quarter]
                for side in range(2)
            ]
            side = core ^ core_ref[0]
            if 0 < number < 3:
                for part in range(2):
                    start = half + 128 + part * half + (number - 1) * quarter
                    attn_ref[side, :, start : start + quarter] = parts[part]
            else:
                out_ref[side, :, start : start + half] = jnp.concatenate(parts, axis=1)
    for side in range(2):
        attn_ref[side, :, half : half + 128] = vector_ref[...]


def column_sides(core, weights, vectors):
    share, width = weights[0].shape
    shapes = (
        shaped((2, share, 3 * width // 2 + vectors.shape[1]), BF16),
        shaped((2, share, width), BF16),
    )
    arrays = [*weights, vectors]
    kernel = functools.partial(gathered_kernel, sides_kernel, len(arrays))
    return call(
        kernel, "column_sides", shapes, (core.reshape(1),), *arrays,
        scratch=[pltpu.VMEM(array.shape, array.dtype) for array in arrays]
        + [pltpu.SemaphoreType.DMA((len(arrays),))],
    )


def products_kernel(plans, mine_ref, *refs):
    outputs = iter(refs[sum(plan[1] + plan[2] for plan in plans) :])
    at = 0
    for share, lefts, rights, turned, chains in plans:
        left_refs, right_refs = refs[at : at + lefts], refs[at + lefts : at + lefts + rights]
        at += lefts + rights
        targets = [(next(outputs), next(outputs)) for _ in chains]
        size = left_refs[0].shape[0 if turned else 1] // 2
        wide = [ref[...] for ref in right_refs]
        wide = wide[0] if len(wide) == 1 else jnp.concatenate(wide, axis=1)
        starts = [sum(ref.shape[1] for ref in right_refs[:index]) for index in range(rights + 1)]
        for row_side in range(2):
            span = slice(row_side * size, (row_side + 1) * size)
            total, first = 0.0, 0
            for left_ref in left_refs:
                count = left_ref.shape[1 if turned else 0]
                right = wide[first : first + count]
                if turned:
                    total = total + nn(left_ref[span, :], right)
                else:
                    total = total + tn(left_ref[:, span], right)
                first += count
            for (which, columns, places), (kept_ref, sent_ref) in zip(chains, targets):
                result = total[:, starts[columns[0]] : starts[columns[-1] + 1]]

                def store(mine):
                    for block in range(size // share):
                        digit, target = places[row_side * (size // share) + block]
                        out_ref = kept_ref if digit == mine else sent_ref
                        out_ref[target] = result[block * share : (block + 1) * share].astype(BF16)

                pl.when(mine_ref[which] == 0)(functools.partial(store, 0))
                pl.when(mine_ref[which] == 1)(functools.partial(store, 1))


def products(mine, share, groups, name):
    plans, inputs, shapes = [], [], []
    count = 0
    for lefts, rights, chains, turned in groups:
        inputs += [*lefts, *rights]
        plan = []
        rows = lefts[0].shape[0 if turned else 1]
        for columns, dims, digit in chains:
            places = []
            for block in range(rows // share):
                index, rest = [], block
                for size in reversed(dims):
                    index.append(rest % size)
                    rest //= size
                index = index[::-1]
                value = index.pop(digit)
                flat = 0
                for size, digit_of in zip(dims[:digit] + dims[digit + 1 :], index):
                    flat = flat * size + digit_of
                places.append((value, flat))
            plan.append((count, columns, places))
            count += 1
            wide = sum(rights[column].shape[1] for column in columns)
            shape = (rows // share // 2, share, wide)
            shapes += [shaped(shape, BF16)] * 2
        plans.append((share, len(lefts), len(rights), turned, plan))
    kernel = functools.partial(products_kernel, plans)
    outs = call(kernel, name, shapes, (mine,), *inputs)
    return list(zip(outs[::2], outs[1::2]))


def back_kernel(core_ref, *refs):
    grad_q_refs, grad_kv_refs = refs[:2], refs[2:4]
    weight_ref, own_ref, sent_ref = refs[4:]
    chip_rows, quarter = grad_q_refs[0].shape
    rows = chip_rows // 2
    keys = weight_ref.shape[1] - 4 * quarter
    both = 0.0
    for part in range(2):
        first = keys + 2 * part * quarter
        both = both + nt(grad_kv_refs[part][...], weight_ref[:, first : first + 2 * quarter])
    grad_q = jnp.concatenate([ref[...] for ref in grad_q_refs], axis=1)
    here = nt(grad_q, weight_ref[:, : 2 * quarter]) + both[chip_rows:]
    for block in range(2):
        span = slice(block * rows, (block + 1) * rows)
        side = core_ref[0] ^ block

        def store(out_ref):
            out_ref[0] = here[span].astype(out_ref.dtype)
            out_ref[1] = both[span].astype(out_ref.dtype)

        pl.when(side == 0)(functools.partial(store, own_ref))
        pl.when(side == 1)(functools.partial(store, sent_ref))


def back_project(core, grad_q, grad_kv, weights):
    shape = (2, grad_q[0].shape[0] // 2, weights.shape[0])
    shapes = shaped(shape, F32), shaped(shape, BF16)
    arrays = *grad_q, *grad_kv, weights
    return call(back_kernel, "back_project", shapes, (core.reshape(1),), *arrays)


def step_kernel(plans, mine_ref, *refs):
    for number, plan in enumerate(plans):
        held_ref, came_ref = refs[plan["held"]], refs[plan["came"]]
        count, share, columns = held_ref.shape
        came_at, came_column = plan["came_at"]
        sent_at, sent_column = plan["sent_at"]

        def store(mine):
            for index in range(count):
                value = held_ref[index].astype(F32) + came_ref[
                    came_at + index, :share, came_column : came_column + columns
                ].astype(F32)
                digit, target = plan["places"][index]
                if digit == mine:
                    kept_ref = refs[plan["kept"]]
                    kept_ref[target] = value.astype(kept_ref.dtype)
                else:
                    sent_ref = refs[plan["sent"]]
                    sent_ref[sent_at + target, :share, sent_column : sent_column + columns] = (
                        value.astype(sent_ref.dtype)
                    )

        if plan["digit"] is None:
            store(0)
        else:
            pl.when(mine_ref[plan["digit"]] == 0)(functools.partial(store, 0))
            pl.when(mine_ref[plan["digit"]] == 1)(functools.partial(store, 1))


def finish_kernel(plans, core_ref, *refs):
    *own_refs, other_ref = refs[: -len(plans)]
    first_core = core_ref[0] == 0
    for plan, out_ref in zip(plans, refs[-len(plans) :]):
        for side, (source, column, other_column) in enumerate(plan):
            half = out_ref.shape[1] // 2
            own = own_refs[source][:, column : column + half // 2]
            other = other_ref[:, other_column : other_column + half // 2]
            pair = [jnp.where(first_core, own, other), jnp.where(first_core, other, own)]
            out_ref[:, side * half : (side + 1) * half] = jnp.concatenate(pair, axis=1)


def finish_columns(core, own, other, half, mixed):
    quarter = half // 2
    plans = []
    for index in range(len(own)):
        sources = [index, index]
        columns = [0, quarter]
        if mixed and index >= len(own) - 2:
            sources = [len(own) - 2, len(own) - 1]
            columns = [(index - len(own) + 2) * quarter] * 2
        plans.append([(s, col, s * half + col) for s, col in zip(sources, columns)])
    shapes = [shaped((own[0].shape[0], 2 * half), F32)] * len(own)
    kernel = functools.partial(finish_kernel, plans)
    return call(kernel, "finish_columns", shapes, (core.reshape(1),), *own, other)


def local(
    tokens,
    lengths,
    norm_attn,
    norm_mlp,
    query_scale,
    query_proj,
    key_proj,
    value_proj,
    output_proj,
    gate_proj,
    up_proj,
    down_proj,
    cotangent,
):
    place = {name: lax.axis_index(name) for name in ("y", "c", "z", "x")}
    y, c, x = place["y"], place["c"], place["x"]
    line = lax.axis_size("z")
    bits = line_bits(line)
    rows = tokens.shape[1]
    share, width = query_proj.shape
    half = width // 2
    quarter = width // 4
    chip_rows = 2 * rows
    length = 4 * rows

    near = ("z", 1)
    far = [("z", bit) for bit in reversed(bits[1:])]
    orders = (
        far + [("x", 1), ("y", 1), near],
        far + [("y", 1), near, ("x", 1)],
        far + [near, ("x", 1), ("y", 1)],
    )
    vector_columns = jnp.pad(
        jnp.stack([norm_attn, norm_mlp, query_scale], axis=1), ((0, 0), (0, 125))
    )
    attn_block, gate_up_block = column_sides(
        c, (query_proj, key_proj, value_proj, gate_proj, up_proj), vector_columns
    )
    own_tokens = tokens[0]
    other_tokens = across(own_tokens, "c", 1)
    other_cotangent = across(cotangent[0], "c", 1)
    before = across(own_tokens, "y", 1)
    other_before = across(before, "c", 1)
    chip_tokens = in_order(own_tokens, other_tokens, c, 0)
    chip_before = in_order(before, other_before, c, 0)
    all_tokens = jnp.concatenate([chip_before, chip_tokens], axis=0)

    attn_pieces, first = far_pieces(attn_block, far, (), (before,))
    attn_others = other_cores(attn_pieces, other_tokens, other_cotangent)
    cuts = (0, half + 128, 2 * half + 128, 3 * half + 128)
    attn_chains = [
        Chain(blocks, 2, order, len(far))
        for blocks, order in zip(
            side_blocks(attn_pieces, attn_others, list(zip(cuts, cuts[1:]))), orders
        )
    ]
    places_now = jnp.stack([place[name] for name in ("y", "c", "z", "x")])
    second = advance_all(attn_chains)
    gate_up_pieces, middle = far_pieces(gate_up_block, far, first, second)
    third = advance_all(attn_chains, other_before, *middle)
    output_pieces, late = far_pieces(output_proj, far, (*middle, *second, other_before))
    gate_up_sent = jnp.stack([piece[1] for piece in gate_up_pieces])
    gate_up_others = across(after(gate_up_sent, other_before), "c", 1)
    gate_up_sides = side_blocks(
        gate_up_pieces, list(gate_up_others), [(0, half), (half, width)]
    )
    mlp_chains = [
        Chain(blocks, 2, order, len(far)) for blocks, order in zip(gate_up_sides, orders)
    ]
    output_sides = [piece[:, cut : cut + half] for piece in output_pieces for cut in (0, half)]
    mlp_chains.append(Chain(jnp.stack(output_sides), 2, orders[2], len(far)))
    advance_together(attn_chains[1:] + attn_chains[:1], mlp_chains)
    fourth = [chain.last for chain in attn_chains]
    mlp_third = advance_all(mlp_chains)
    down_pieces, _ = far_pieces(down_proj, far, third)
    down_chains = [
        Chain(jnp.stack([piece[:, cut : cut + half] for piece in down_pieces]), 1, order, len(far))
        for cut, order in zip((0, half), orders)
    ]
    down_second = advance_all(down_chains, *fourth)

    doc_ends = jnp.cumsum(lengths[0])
    places = jnp.arange(length, dtype=jnp.int32)
    segment = jnp.sum((places[:, None] >= doc_ends[None, :]).astype(jnp.int32), axis=1)
    seg_here = block_of(segment, y, chip_rows)
    seg_before = jnp.where(y == 0, -1, segment[:chip_rows])
    seg_keys = jnp.concatenate([seg_before, seg_here])[None]
    seg_rows = seg_here[:, None]
    first_row = y * chip_rows + jnp.arange(rows, dtype=jnp.int32)
    upstream_b = [
        jnp.where((first_row + core * rows < doc_ends[-1])[:, None], rows_of, 0).astype(BF16)
        for core, rows_of in ((c, cotangent[0]), (1 - c, other_cotangent))
    ]
    upstream = upstream_b[0]
    upstream_b = jnp.concatenate(upstream_b, axis=0)
    both = ((0, 0), (1, 1))
    (attn_weights,) = layout_blocks(
        places_now,
        line,
        [(3 * half + 128, True)],
        [
            (chain, end - cut, [(0, side, flip, cut) for side, flip in both])
            for chain, cut, end in zip(attn_chains, cuts, cuts[1:])
        ],
    )
    q_raw, queries, keys_values, normed_before, normed_here, vectors, scale_rows = project(
        c, all_tokens, attn_weights
    )
    gain_a, gain_m = vectors[0], vectors[1]
    mlp_sent_last = advance_all(mlp_chains, queries)
    down_third = advance_all(down_chains, queries)
    queries = after(queries, *[chain.held for chain in mlp_chains + down_chains])
    attended_f, attended, lse = attention_forward(queries, keys_values, seg_rows, seg_keys)
    attended = after(attended, *mlp_sent_last, *down_third, upstream_b)
    for chain in mlp_chains:
        chain.last = after(chain.last, attended)
    down_last = advance_all(down_chains, attended)

    (proj_o,) = layout_blocks(
        places_now,
        line,
        [(width, False)],
        [(mlp_chains[2], half, [(0, 0, 0, 0), (0, 1, 0, half)])],
    )
    output_own, output_sent = output_project(c, attended, proj_o)
    hidden1, normed_own = norm_middle(
        output_own, across(output_sent, "c", 1), own_tokens, gain_m
    )
    normed_others = [
        across(normed_own[start : start + rows // 2], "c", 1) for start in (0, rows // 2)
    ]
    for chain in mlp_chains[:2]:
        chain.last = after(chain.last, output_sent)
    (proj_gu,) = layout_blocks(
        places_now,
        line,
        [(width, True)],
        [
            (chain, half, [(0, side, flip, cut) for side, flip in both])
            for chain, cut in zip(mlp_chains, (0, half))
        ],
    )
    hidden, gate_pre, up_pre, normed_m = mlp_first((normed_own, *normed_others), proj_gu)
    for chain in down_chains:
        chain.last = after(chain.last, hidden)
    (proj_d,) = layout_blocks(
        places_now,
        line,
        [(width, False)],
        [(chain, half, [(0, 0, 0, cut)]) for chain, cut in zip(down_chains, (0, half))],
    )

    digits = [("y", 1), ("c", 1)] + [("z", bit) for bit in reversed(bits)] + [("x", 1)]
    scatter_orders = [order[len(far) :][::-1] for order in orders]

    output_orders = [("x", 1), ("y", 1), near], [("y", 1), ("x", 1), near]

    def own_digit(axis, bit):
        return (place[axis] // bit) % 2

    def sizes_of(names, by_column):
        return tuple(1 if name == ("c", 1) and not by_column else 2 for name in names)

    def first_step(*groups, gate=(), name="products"):
        mine, plans, states = [], [], []
        for lefts, rights, columns, chain_orders, turned in groups:
            by_column = lefts[0].shape[0 if turned else 1] == width
            dims = sizes_of(digits, by_column)
            chains = []
            for which, order in zip(columns, chain_orders):
                at = digits.index(order[0])
                chains.append((which, dims, at))
                mine.append(own_digit(*order[0]))
                names = digits[:at] + digits[at + 1 :]
                states.append({"names": names, "by_column": by_column, "order": order, "step": 1})
            plans.append((lefts, rights, chains, turned))
        if share % 8 == 0:
            parts = products(jnp.stack(mine).astype(jnp.int32), share, plans, name)
        else:
            parts = []
            for lefts, rights, chains, turned in plans:
                left = jnp.concatenate([each.T if turned else each for each in lefts], axis=0)
                for which, dims, at in chains:
                    right = jnp.concatenate([rights[column] for column in which], axis=1)
                    part = tn(left, right).astype(BF16).reshape(dims + (share, right.shape[1]))
                    digit = mine[len(parts)]
                    parts.append(
                        [
                            lax.dynamic_index_in_dim(part, which_half, at, keepdims=False).reshape(
                                -1, share, right.shape[1]
                            )
                            for which_half in (digit, 1 - digit)
                        ]
                    )
        sent = [after(value, *gate) if gate else value for _, value in parts]
        for state, (kept, _), value in zip(states, parts, sent):
            state.update(held=kept, came=across(value, *state["order"][0]), came_at=(0, 0))
        return states, [value for _, value in parts]

    def step(states, names, *earlier, packed=None, dtype=BF16):
        mine, plans, inputs, shapes = [], [], [], []
        came = [after(state["came"], *earlier) if earlier else state["came"] for state in states]
        sources = {}
        for state, array in zip(states, came):
            key = id(state["came"])
            if key not in sources:
                sources[key] = len(inputs)
                inputs.append(array)
        new_states = []
        for number, (state, name) in enumerate(zip(states, names)):
            dims = sizes_of(state["names"], state["by_column"])
            held = state["held"]
            plan = {"came": sources[id(state["came"])], "came_at": state["came_at"]}
            plan["held"] = len(inputs)
            inputs.append(held)
            at = state["names"].index(name) if name in state["names"] else None
            if at is not None and dims[at] == 1:
                at = None
            rest = [index for index in range(len(dims)) if index != at]
            places = []
            for index in range(held.shape[0]):
                values, left_over = [], index
                for size in reversed(dims):
                    values.append(left_over % size)
                    left_over //= size
                values = values[::-1]
                flat = 0
                for axis_at in rest:
                    flat = flat * dims[axis_at] + values[axis_at]
                places.append((0 if at is None else values[at], flat))
            plan["places"] = places
            plan["digit"] = None if at is None else len(mine)
            if at is not None:
                mine.append(own_digit(*name))
            plan["sent_at"] = packed[1][number] if packed else (0, 0)
            plan["kept"] = len(shapes)
            count = held.shape[0] // (1 if at is None else 2)
            shapes.append(shaped((count,) + held.shape[1:], F32))
            if at is not None and not packed:
                plan["sent"] = len(shapes)
                shapes.append(shaped((count,) + held.shape[1:], dtype))
            plans.append(plan)
            names_left = [state["names"][axis_at] for axis_at in rest]
            new_states.append(dict(state, names=names_left, came_at=plan["sent_at"]))
        if packed:
            for plan in plans:
                plan["sent"] = len(shapes)
            shapes.append(shaped(packed[0], dtype))
        for plan in plans:
            plan["kept"] += 1 + len(inputs) - 1
            if "sent" in plan:
                plan["sent"] += len(inputs)
        if not mine:
            mine = [place["c"]]
        kernel = functools.partial(step_kernel, plans)
        outs = call(kernel, "step", shapes, (jnp.stack(mine).astype(jnp.int32),), *inputs)
        for plan, state in zip(plans, new_states):
            state["held"] = outs[plan["kept"] - len(inputs)]
        if packed:
            return new_states, outs[-1]
        return new_states, [
            outs[plan["sent"] - len(inputs)] if plan["digit"] is not None else None
            for plan in plans
        ]

    def halve(states, *earlier):
        names = [state["order"][state["step"]] for state in states]
        states, sent = step(states, names, *earlier)
        for state, value, name in zip(states, sent, names):
            state.update(came=across(value, *name), came_at=(0, 0), step=state["step"] + 1)
        return states, sent

    def halve_far(states, shape, places, *earlier):
        for axis, bit in far[::-1][:-1]:
            states, sent = step(states, [(axis, bit)] * len(states))
            for state, value in zip(states, sent):
                state.update(came=across(value, axis, bit), came_at=(0, 0))
        last = far[0]
        states, message = step(states, [last] * len(states), *earlier, packed=(shape, places))
        arrived = across(message, *last)
        for state in states:
            state.update(came=arrived)
        return states, message

    def join_columns(states):
        left, right = states
        joined = dict(left, came_at=(0, 0))
        for key in ("held", "came"):
            joined[key] = jnp.concatenate([left[key], right[key]], axis=2)
        return [joined]

    def received(states):
        return [state["came"] for state in states]

    down_states, down_sent = first_step(
        ((hidden,), (upstream_b,), ((0,),), scatter_orders[:1], False), name="products_down"
    )
    grad_gate, grad_up = mlp_last(gate_pre, up_pre, proj_d, after(upstream_b, *down_sent))
    gate_own, gate_sent = rows_product((grad_gate, grad_up), proj_gu, True, "gate_up_back")
    mlp_states, mlp_sent = first_step(
        (
            (normed_m,),
            after((grad_gate, grad_up), gate_sent),
            ((0,), (1,)),
            scatter_orders[1:],
            False,
        ),
        name="products_mlp",
    )
    mlp_states = down_states + mlp_states
    gate_own = after(gate_own, *mlp_sent)
    grad_hidden1, low_own, grad_gain_m = middle_back(
        gate_own, across(gate_sent, "c", 1), hidden1, upstream, gain_m
    )
    low_others = [across(low_own[start : start + rows // 2], "c", 1) for start in (0, rows // 2)]
    grad_attended, grad_hidden1_b = attended_back(c, low_own, low_others, proj_o)
    scale_row = scale_rows[:1]
    heads = half // HD
    residuals = (queries, keys_values), (attended_f, lse, seg_rows, seg_keys, q_raw, scale_row)
    grad_q_early, grad_kv_early, early_sums = attention_backward(
        0, heads // 2, *residuals[0], grad_attended, *residuals[1]
    )
    down_own, down_sent = rows_product(
        (after(hidden, grad_attended),), proj_d, False, "down_project"
    )
    down_other = across(down_sent, "c", 1)
    block_out = hidden1 + down_own + down_other
    mlp_states, mlp_sent = halve(mlp_states, grad_kv_early, down_other)
    grad_rows = after(grad_hidden1_b, *mlp_sent)
    output_rights = grad_rows[:, :half], grad_rows[:, half:]
    output_states, output_sent = first_step(
        ((attended,), output_rights, ((0,), (1,)), output_orders, False)
    )
    grad_attended = after(grad_attended, *mlp_sent, *output_sent)
    grad_q_late, grad_kv_late, late_sums = attention_backward(
        heads // 2, heads, *residuals[0], grad_attended, *residuals[1]
    )
    grad_scale = jnp.concatenate([early_sums[0], late_sums[0]]) * scale_rows[1]
    grads = (grad_q_early, grad_q_late), (grad_kv_early, grad_kv_late)
    mlp_states, mlp_sent = halve(mlp_states, grad_kv_late)
    output_states, output_sent = halve(output_states, grad_kv_late)
    grads = after(grads, *mlp_sent, *output_sent)
    attn_states, attn_sent = first_step(
        ((normed_here,), grads[0], ((0, 1),), scatter_orders[:1], False),
        ((normed_before, normed_here), grads[1], ((0,), (1,)), scatter_orders[1:], False),
        gate=received(mlp_states + output_states),
    )
    first_done = received(attn_states)
    grads = after(grads, *attn_sent)
    mlp_states, _ = halve_far(
        mlp_states, (3, share, width), ((2, 0), (0, 0), (0, half)), *attn_sent
    )
    back_own, back_sent = back_project(c, *grads, attn_weights)
    back_other = across(back_sent, "c", 1)
    output_states = join_columns(
        [dict(state, came=after(state["came"], *first_done)) for state in output_states]
    )
    output_states, _ = halve(output_states)
    attn_states, _ = halve(attn_states, mlp_states[0]["came"], back_own)
    second_done = received(attn_states)
    grad_here, grad_before, grad_gain_a = gain_terms(back_own, back_other, own_tokens, before)
    scale_rows = grad_scale.reshape(2, 1, quarter)
    scale_rows = jnp.where(
        c == 0,
        jnp.pad(scale_rows, ((0, 0), (0, 1), (0, 0))),
        jnp.pad(scale_rows, ((0, 0), (1, 0), (0, 0))),
    ).reshape(width)
    vector_terms = jnp.stack([grad_gain_a[0], grad_gain_m[0], scale_rows])
    vector_rows = min(8, share)
    vector_terms = jnp.moveaxis(vector_terms.reshape(3, -1, share), 0, 1)
    room = ((0, 0), (0, vector_rows - 3), (0, 128 - share))
    vector_terms = jnp.pad(vector_terms, room)
    vector_order = [near] + far[::-1] + [("x", 1), ("y", 1)]
    vector_state = {"names": digits, "by_column": True, "order": vector_order, "step": 0}
    zero_terms = jnp.zeros(vector_terms.shape, BF16)
    vector_states = [dict(vector_state, held=vector_terms, came=zero_terms, came_at=(0, 0))]
    vector_states, _ = halve(vector_states)
    attn_states, _ = halve(attn_states, *received(output_states + vector_states))
    third_done = received(attn_states)
    output_states, _ = halve_far(output_states, (1, share, width), ((0, 0),))
    for _ in far:
        vector_states, _ = halve(vector_states)
    vector_first = received(vector_states)
    vector_states, _ = halve(vector_states, *third_done)
    vector_second = received(vector_states)
    grad_after = across(after(grad_before, *third_done), "y", 1)
    grad_inputs = tokens_back(y, grad_here, grad_after, own_tokens, gain_a, grad_hidden1)

    attn_places = [(0, number * half) for number in range(3)]
    final_states, final_message = halve_far(
        attn_states, (2, share, 3 * half), attn_places, *received(output_states), *vector_first
    )
    vector_states, _ = halve(vector_states, grad_after)
    vector_third = received(vector_states)
    mlp_states, sent = step(
        mlp_states,
        [("c", 1)] * 3,
        final_message,
        packed=((1, share, width), ((0, 0), (0, 0), (0, half))),
        dtype=F32,
    )
    mlp_parts = [state["held"][0] for state in mlp_states]
    gate_up_other = across(sent[0], "c", 1)
    gate_up_grads = finish_columns(c, mlp_parts[1:], gate_up_other, half, False)
    final_states, sent = step(
        final_states,
        [("c", 1)] * 3,
        grad_after,
        gate_up_other,
        packed=((1, share, 3 * half), attn_places),
        dtype=F32,
    )
    output_states, _ = step(output_states, [("c", 1)], final_message)
    own_parts = [state["held"][0] for state in final_states + output_states]
    other = across(sent[0], "c", 1)
    attn_grads = finish_columns(c, own_parts[:3], other, half, True)
    vector_states, vector_sent = step(vector_states, [("c", 1)], dtype=F32)
    vector_other = across(vector_sent[0][0], "c", 1)
    summed = (vector_states[0]["held"][0] + vector_other)[:, :share]
    return (
        block_out.astype(BF16)[None],
        grad_inputs[None],
        summed[0],
        summed[1],
        summed[2],
        *attn_grads,
        own_parts[3],
        *gate_up_grads,
        mlp_parts[0],
    )


def solution(mesh):
    seq, dp = mesh.devices.shape
    axes = Mesh(mesh.devices.reshape(seq // 2, 2, dp // 2, 2), ("y", "c", "z", "x"))
    batch, places, every = ("z", "x"), ("y", "c"), ("y", "c", "z", "x")
    activations = P(batch, places, None)
    vector, matrix = P(every), P(every, None)
    return jax.shard_map(
        local,
        mesh=axes,
        in_specs=(activations, P(batch, None)) + (vector,) * 3 + (matrix,) * 7 + (activations,),
        out_specs=(activations, activations) + (vector,) * 3 + (matrix,) * 7,
        check_vma=False,
    )
```

```python
import functools

import jax
import jax.numpy as jnp
from jax import lax
from jax.experimental import pallas as pl
from jax.experimental.pallas import tpu as pltpu
from jax.sharding import Mesh, PartitionSpec as P

H = 16
HD = 80
EPSILON = 1e-06
R_SOFTPLUS = 1.442695041
MASKED = -1e30
QUERY_ROWS = 256
VMEM_BYTES = 24 << 20
VMEM_MOST = 56 << 20
SPEED = 4600000000
COSTS = {
    "attended_back": 1, "middle_back": 1,
    "project": 5,
    "attention_forward": 13,
    "output_project": 0,
    "mlp_middle": 3,
    "gate_up_back": 3,
    "products": 6,
    "attention_backward": 10,
    "back_project": 0,
    "join": 3,
    "tokens_back": 3,
    "layout_blocks": 2,
    "norm_middle": 0,
    "mlp_first": 2,
    "products_down": 2,
    "mlp_last": 2,
    "products_mlp": 4,
    "attention_early": 5,
}
F32 = jnp.float32
BF16 = jnp.bfloat16


def nn(left, right):
    return jnp.dot(left, right, preferred_element_type=F32)


def nt(left, right):
    return lax.dot_general(left, right, (((1,), (1,)), ((), ())), preferred_element_type=F32)


def tn(left, right):
    return lax.dot_general(left, right, (((0,), (0,)), ((), ())), preferred_element_type=F32)


def allowed_pairs(seg_rows, seg_keys, half, first, rows):
    total = seg_keys.shape[1]
    row_ids = lax.broadcasted_iota(jnp.int32, (rows, total), 0) + (first + half)
    col_ids = lax.broadcasted_iota(jnp.int32, (rows, total), 1)
    return (seg_rows == seg_keys) & (col_ids <= row_ids)


WHOLE = pl.BlockSpec(memory_space=pltpu.VMEM)
SCALARS = pl.BlockSpec(memory_space=pltpu.SMEM)
ANYWHERE = pl.BlockSpec(memory_space=pl.ANY)


def call(kernel, name, out_shape, scalars, *arrays, scratch=()):
    specs = [SCALARS] * len(scalars) + [ANYWHERE if scratch else WHOLE] * len(arrays)
    return pl.pallas_call(
        kernel,
        out_shape=out_shape,
        in_specs=specs,
        out_specs=jax.tree.map(lambda shape: WHOLE, out_shape),
        compiler_params=pltpu.CompilerParams(vmem_limit_bytes=VMEM_MOST if scratch else VMEM_BYTES),
        scratch_shapes=scratch,
        cost_estimate=pl.CostEstimate(flops=COSTS.get(name, 2) * SPEED, bytes_accessed=0, transcendentals=0),
        name=name,
    )(*scalars, *arrays)


def shaped(shape, dtype):
    return jax.ShapeDtypeStruct(tuple(shape), dtype)


def project_kernel(
    core_ref, tokens_ref, weight_ref, raw_ref, q_ref, kv_ref, before_ref, here_ref, vectors_ref,
    scale_ref
):
    chip_rows, half = raw_ref.shape
    quarter = half // 2
    vectors = weight_ref[:, half : half + 128].astype(F32).T[:8]
    keys = half + 128
    vectors_ref[...] = vectors
    gain = vectors[0:1]
    logits = [
        jnp.concatenate(
            [vectors[2:3, side * half + core * quarter :][:, :quarter] for side in range(2)], axis=1
        )
        for core in range(2)
    ]
    logit = jnp.where(core_ref[0] == 0, logits[0], logits[1])
    softplus = jnp.maximum(logit, 0.0) + jnp.log1p(jnp.exp(-jnp.abs(logit)))
    scale = R_SOFTPLUS * HD ** (-0.5) * softplus
    scale_ref[0:1] = scale
    scale_ref[1:2] = R_SOFTPLUS * HD ** (-0.5) / (1.0 + jnp.exp(-logit))
    for first in range(0, 2 * chip_rows, QUERY_ROWS):
        rows = slice(first, first + QUERY_ROWS)
        values = tokens_ref[rows, :].astype(F32)
        inverse = lax.rsqrt(jnp.mean(values * values, axis=1, keepdims=True) + EPSILON)
        normed = (values * inverse * gain).astype(BF16)
        kv_ref[rows, :] = nn(normed, weight_ref[:, keys : keys + 2 * half]).astype(BF16)
        if first >= chip_rows:
            here = slice(first - chip_rows, first - chip_rows + QUERY_ROWS)
            here_ref[here, :] = normed
            raw = nn(normed, weight_ref[:, :half])
            raw_ref[here, :] = raw
            q_ref[here, :] = (raw * scale).astype(BF16)
        else:
            before_ref[rows, :] = normed


def project(core, tokens, weights):
    rows, width = tokens.shape
    half = width // 2
    shapes = (
        shaped((rows // 2, half), F32),
        shaped((rows // 2, half), BF16),
        shaped((rows, width), BF16),
        shaped((rows // 2, width), BF16),
        shaped((rows // 2, width), BF16),
        shaped((8, width), F32),
        shaped((2, half), F32),
    )
    return call(project_kernel, "project", shapes, (core.reshape(1),), tokens, weights)


def key_value_columns(head, width):
    half = width // 2
    start = head * HD // half * width + head * HD % half
    return slice(start, start + HD), slice(start + half, start + half + HD)


def forward_kernel(q_ref, kv_ref, segq_ref, segk_ref, out_ref, low_ref, lse_ref):
    half, width = q_ref.shape
    for first in range(0, half, QUERY_ROWS):
        rows = slice(first, first + QUERY_ROWS)
        end = half + first + QUERY_ROWS
        allowed = allowed_pairs(segq_ref[rows, :], segk_ref[:, :end], half, first, QUERY_ROWS)
        outs, lses = [], []
        for head in range(width // HD):
            cols = slice(head * HD, (head + 1) * HD)
            key_cols, value_cols = key_value_columns(head, width)
            scores = jnp.where(allowed, nt(q_ref[rows, cols], kv_ref[:end, key_cols]), MASKED)
            top = jnp.max(scores, axis=1, keepdims=True)
            exps = jnp.exp(scores - top)
            total = jnp.sum(exps, axis=1, keepdims=True)
            probs = (exps * (1.0 / total)).astype(BF16)
            outs.append(nn(probs, kv_ref[:end, value_cols]))
            lses.append(top + jnp.log(total))
        out = jnp.concatenate(outs, axis=1)
        out_ref[rows, :] = out
        low_ref[rows, :] = out.astype(BF16)
        lse_ref[rows, :] = jnp.concatenate(lses, axis=1)


def attention_forward(q, kv, segq, segk):
    shapes = (
        shaped(q.shape, F32),
        shaped(q.shape, BF16),
        shaped((q.shape[0], q.shape[1] // HD), F32),
    )
    return call(forward_kernel, "attention_forward", shapes, (), q, kv, segq, segk)


def backward_kernel(first_head, last_head, *refs):
    q_ref, kv_ref, go_ref, out_ref, lse_ref, segq_ref, segk_ref, raw_ref, scale_ref = refs[:9]
    dq_ref, dkv_ref, sum_ref = refs[9:]
    half, width = q_ref.shape
    heads = range(first_head, last_head)
    span = slice(first_head * HD, last_head * HD)
    dks, dvs = [None] * len(heads), [None] * len(heads)
    sums = 0.0
    for first in reversed(range(0, half, QUERY_ROWS)):
        rows = slice(first, first + QUERY_ROWS)
        end = half + first + QUERY_ROWS
        allowed = allowed_pairs(segq_ref[rows, :], segk_ref[:, :end], half, first, QUERY_ROWS)
        products = go_ref[rows, :].astype(F32) * out_ref[rows, :]
        dqs = []
        for number, head in enumerate(heads):
            cols = slice(head * HD, (head + 1) * HD)
            key_cols, value_cols = key_value_columns(head, width)
            queries, keys = q_ref[rows, cols], kv_ref[:end, key_cols]
            values = kv_ref[:end, value_cols]
            grads = go_ref[rows, cols]
            scores = jnp.where(allowed, nt(queries, keys), MASKED)
            probs = jnp.exp(scores - lse_ref[rows, head : head + 1])
            delta = jnp.sum(products[:, cols], axis=1, keepdims=True)
            grad_scores = (probs * (nt(grads, values) - delta)).astype(BF16)
            dqs.append(nn(grad_scores, keys))
            for sums_of, term in (
                (dks, tn(grad_scores, queries)),
                (dvs, tn(probs.astype(BF16), grads)),
            ):
                held = sums_of[number]
                if held is None:
                    sums_of[number] = term
                else:
                    sums_of[number] = jnp.concatenate([held[:end] + term, held[end:]], axis=0)
        dq = jnp.concatenate(dqs, axis=1)
        sums = sums + jnp.sum(dq * raw_ref[rows, span], axis=0, keepdims=True)
        dq_ref[rows, :] = (dq * scale_ref[:, span]).astype(BF16)
    sum_ref[...] = sums
    dkv_ref[...] = jnp.concatenate(dks + dvs, axis=1).astype(BF16)


def attention_backward(first_head, last_head, q, kv, *rest):
    columns = (last_head - first_head) * HD
    shapes = (
        shaped((q.shape[0], columns), BF16),
        shaped((kv.shape[0], 2 * columns), BF16),
        shaped((1, columns), F32),
    )
    kernel = functools.partial(backward_kernel, first_head, last_head)
    name = "attention_backward" if first_head else "attention_early"
    return call(kernel, name, shapes, (), q, kv, *rest)


def output_kernel(core_ref, attended_ref, weight_ref, own_ref, sent_ref):
    rows = own_ref.shape[0]
    for block in range(2):
        result = nn(attended_ref[block * rows : (block + 1) * rows, :], weight_ref[...])
        side = core_ref[0] ^ block

        def store(out_ref):
            out_ref[...] = result

        pl.when(side == 0)(functools.partial(store, own_ref))
        pl.when(side == 1)(functools.partial(store, sent_ref))


def output_project(core, attended, weight):
    shape = shaped((attended.shape[0] // 2, weight.shape[1]), F32)
    return call(
        output_kernel, "output_project", (shape, shape), (core.reshape(1),), attended, weight
    )


def norm_kernel(own_ref, came_ref, tokens_ref, gain_ref, hidden_ref, normed_ref):
    hidden = tokens_ref[...].astype(F32) + own_ref[...] + came_ref[...]
    hidden_ref[...] = hidden
    inverse = lax.rsqrt(jnp.mean(hidden * hidden, axis=1, keepdims=True) + EPSILON)
    normed_ref[...] = (hidden * inverse * gain_ref[...]).astype(BF16)


def norm_middle(own, came, tokens, gain):
    shapes = shaped(own.shape, F32), shaped(own.shape, BF16)
    return call(norm_kernel, "norm_middle", shapes, (), own, came, tokens, gain[None])


def mlp_first_kernel(*refs):
    *normed_refs, weight_ref, hidden_ref, gate_ref, up_ref, normed_ref = refs
    half = hidden_ref.shape[1]
    start = 0
    for ref in normed_refs:
        rows = slice(start, start + ref.shape[0])
        start += ref.shape[0]
        normed = ref[...]
        normed_ref[rows, :] = normed
        gate_up = nn(normed, weight_ref[...])
        gate, up = gate_up[:, :half], gate_up[:, half:]
        gate_ref[rows, :] = gate
        up_ref[rows, :] = up
        hidden_ref[rows, :] = (gate * jax.nn.sigmoid(gate) * up).astype(BF16)


def mlp_first(normed, weight):
    rows = sum(part.shape[0] for part in normed)
    half = weight.shape[1] // 2
    wide = shaped((rows, half), F32)
    shapes = shaped((rows, half), BF16), wide, wide, shaped((rows, weight.shape[0]), BF16)
    return call(mlp_first_kernel, "mlp_first", shapes, (), *normed, weight)


def mlp_last_kernel(gate_in_ref, up_in_ref, down_ref, upstream_ref, gate_ref, up_ref):
    for first in range(0, gate_ref.shape[0], QUERY_ROWS):
        rows = slice(first, first + QUERY_ROWS)
        gate, up = gate_in_ref[rows, :], up_in_ref[rows, :]
        sigmoid = jax.nn.sigmoid(gate)
        grad = nt(upstream_ref[rows, :], down_ref[...])
        gate_ref[rows, :] = (
            grad * up * sigmoid * (1.0 + gate * (1.0 - sigmoid))
        ).astype(BF16)
        up_ref[rows, :] = (grad * gate * sigmoid).astype(BF16)


def mlp_last(gate, up, down, upstream):
    shape = shaped(gate.shape, BF16)
    return call(mlp_last_kernel, "mlp_last", (shape, shape), (), gate, up, down, upstream)


def rows_kernel(transposed, *refs):
    *left_refs, right_ref, own_ref, sent_ref = refs
    rows = own_ref.shape[0]
    for block, out_ref in enumerate((own_ref, sent_ref)):
        total, start = 0.0, 0
        for left_ref in left_refs:
            left = left_ref[block * rows : (block + 1) * rows, :]
            if transposed:
                total = total + nt(left, right_ref[:, start : start + left.shape[1]])
            else:
                total = total + nn(left, right_ref[start : start + left.shape[1], :])
            start += left.shape[1]
        out_ref[...] = total


def rows_product(lefts, right, transposed, name):
    columns = right.shape[0] if transposed else right.shape[1]
    shape = shaped((lefts[0].shape[0] // 2, columns), F32)
    kernel = functools.partial(rows_kernel, transposed)
    return call(kernel, name, (shape, shape), (), *lefts, right)


def norm_back(values, gain, upstream):
    inverse = lax.rsqrt(jnp.mean(values * values, axis=1, keepdims=True) + EPSILON)
    scaled = upstream * gain
    back = inverse * scaled - values * inverse**3 * jnp.mean(values * scaled, axis=1, keepdims=True)
    return back, jnp.sum(upstream * values * inverse, axis=0, keepdims=True)


def middle_back_kernel(own_ref, came_ref, hidden_ref, upstream_ref, gain_ref, grad_ref, low_ref, sum_ref):
    back, sums = norm_back(hidden_ref[...], gain_ref[...], own_ref[...] + came_ref[...])
    grad = upstream_ref[...].astype(F32) + back
    grad_ref[...] = grad
    low_ref[...] = grad.astype(BF16)
    sum_ref[...] = sums


def middle_back(own, came, hidden, upstream, gain):
    shapes = shaped(own.shape, F32), shaped(own.shape, BF16), shaped((1, own.shape[1]), F32)
    return call(
        middle_back_kernel, "middle_back", shapes, (), own, came, hidden, upstream, gain[None]
    )


def attended_kernel(core_ref, *refs):
    own_ref, *other_refs, weight_ref, grad_ref, rows_ref = refs
    rows = own_ref.shape[0]
    for block, parts in enumerate(([own_ref], other_refs)):
        first = (core_ref[0] ^ block) * rows
        for number, ref in enumerate(parts):
            size = ref.shape[0]
            place = pl.ds(pl.multiple_of(first + number * size, size), size)
            grad_ref[place, :] = nt(ref[...], weight_ref[...]).astype(BF16)
            rows_ref[place, :] = ref[...]


def attended_back(core, own, others, weight):
    rows, width = own.shape
    shapes = shaped((2 * rows, weight.shape[0]), BF16), shaped((2 * rows, width), BF16)
    return call(
        attended_kernel, "attended_back", shapes, (core.reshape(1),), own, *others, weight
    )


def gain_kernel(own_ref, came_ref, tokens_ref, before_ref, here_ref, sent_ref, sum_ref):
    total = 0.0
    for part, ref in enumerate((tokens_ref, before_ref)):
        grad = own_ref[part] + came_ref[part]
        values = ref[...].astype(F32)
        inverse = lax.rsqrt(jnp.mean(values * values, axis=1, keepdims=True) + EPSILON)
        total = total + jnp.sum(grad * values * inverse, axis=0, keepdims=True)
        if part == 0:
            here_ref[...] = grad
        else:
            sent_ref[...] = grad.astype(BF16)
    sum_ref[...] = total


def gain_terms(own, came, tokens, before):
    rows, width = tokens.shape
    shapes = shaped((rows, width), F32), shaped((rows, width), BF16), shaped((1, width), F32)
    return call(gain_kernel, "gain_terms", shapes, (), own, came, tokens, before)


def tokens_kernel(first_ref, here_ref, after_ref, tokens_ref, gain_ref, hidden_ref, out_ref):
    later = jnp.where(first_ref[0] == 0, after_ref[...].astype(F32), 0.0)
    back, _ = norm_back(tokens_ref[...].astype(F32), gain_ref[...], here_ref[...] + later)
    out_ref[...] = hidden_ref[...] + back


def tokens_back(first, here, after_rows, tokens, gain, grad_hidden):
    shape = shaped(here.shape, F32)
    arrays = here, after_rows, tokens, gain[None], grad_hidden
    return call(tokens_kernel, "tokens_back", shape, (first.reshape(1),), *arrays)


def pick(pair, index):
    return jnp.where(index == 0, pair[0], pair[1])


def in_order(own, other, index, axis):
    return jnp.where(
        index == 0,
        jnp.concatenate([own, other], axis=axis),
        jnp.concatenate([other, own], axis=axis),
    )


def block_of(matrix, index, size, axis=0):
    return lax.dynamic_slice_in_dim(matrix, index * size, size, axis)


def across(value, axis, bit):
    count = lax.axis_size(axis)
    return lax.ppermute(value, axis, [(place, place ^ bit) for place in range(count)])


def line_bits(count):
    return [1 << power for power in range(count.bit_length() - 1)]


def after(values, *earlier):
    return lax.optimization_barrier((values, earlier))[0]


def far_pieces(block, far, before=(), then=()):
    pieces, arrived = [block], ()
    for axis, bit in far:
        message = block if len(pieces) == 1 else jnp.stack(pieces)
        came = across(after(message, *before) if before else message, axis, bit)
        arrived = (came,)
        came = after(came, *then) if then else came
        pieces += [came] if len(pieces) == 1 else [came[index] for index in range(len(pieces))]
    return pieces, arrived


def other_cores(pieces, *earlier):
    own = pieces[0][1]
    first = across(after(own, *earlier) if earlier else own, "c", 1)
    if len(pieces) == 2:
        return [first, across(pieces[1][1], "c", 1)]
    rest = [piece[1] for piece in pieces[1:]]
    return [first] + (list(across(jnp.stack(rest), "c", 1)) if rest else [])


def side_kernel(cuts, *refs):
    count = (len(refs) - len(cuts)) // 2
    for index in range(count):
        for (first, last), out_ref in zip(cuts, refs[2 * count :]):
            out_ref[2 * index] = refs[index][0, :, first:last]
            out_ref[2 * index + 1] = refs[count + index][:, first:last]


def side_blocks(pieces, others, cuts):
    share = pieces[0].shape[1]
    shapes = [shaped((2 * len(pieces), share, last - first), BF16) for first, last in cuts]
    kernel = functools.partial(side_kernel, cuts)
    return call(kernel, "side_blocks", shapes, (), *pieces, *others)


def join_kernel(starts, *refs):
    count = len(refs) // 3
    for number, start in enumerate(starts):
        first_ref, second_ref, out_ref = refs[number], refs[count + number], refs[2 * count + number]
        size, _, columns = first_ref.shape
        out_ref[:size] = first_ref[...]
        out_ref[size:] = second_ref[start : start + size, :, :columns]


def join(firsts, seconds, starts):
    shapes = [shaped((2 * first.shape[0],) + first.shape[1:], first.dtype) for first in firsts]
    kernel = functools.partial(join_kernel, starts)
    return call(kernel, "join", shapes, (), *firsts, *seconds)


class Chain:
    def __init__(self, held, sides, order, step):
        self.sides = sides
        self.held, self.last, self.start = None, held, 0
        self.order, self.step = order, step


def take_all(chains, *earlier):
    lasts = [after(chain.last, *earlier) if earlier else chain.last for chain in chains]
    if chains[0].held is None:
        helds = lasts
    else:
        starts = [chain.start for chain in chains]
        helds = join([chain.held for chain in chains], lasts, starts)
    for chain, held in zip(chains, helds):
        chain.held, chain.start = held, 0


def advance_all(chains, *earlier):
    take_all(chains, *earlier)
    for chain in chains:
        chain.last = across(chain.held, *chain.order[chain.step])
        chain.step += 1
    return [chain.last for chain in chains]


def together_kernel(count, *refs):
    for number in range(count):
        first_ref, second_ref, short_ref, out_ref = refs[number::count]
        size = first_ref.shape[0]
        out_ref[:size] = first_ref[...]
        out_ref[size : 2 * size] = second_ref[...]
        out_ref[2 * size :, :, : short_ref.shape[2]] = short_ref[...]


def advance_together(longs, shorts):
    take_all(shorts)
    shapes = [
        shaped((2 * long.held.shape[0] + short.held.shape[0],) + long.held.shape[1:], BF16)
        for long, short in zip(longs, shorts)
    ]
    arrays = [long.held for long in longs] + [long.last for long in longs]
    arrays += [short.held for short in shorts]
    kernel = functools.partial(together_kernel, len(longs))
    messages = call(kernel, "together", shapes, (), *arrays)
    for long, short, message in zip(longs, shorts, messages):
        came = across(message, *long.order[long.step])
        count = 2 * long.held.shape[0]
        long.held, long.last, long.count = message, came, count
        short.last, short.start = came, count
        long.step += 1
        short.step += 1


def layout_kernel(plans, count_out, place_ref, *refs):
    out_refs = refs[-count_out:]
    for source, (line, sides, count, columns, steps, base, placed) in enumerate(plans):
        devices = 4 * line
        for index in range(count // sides):
            flips = dict(base)
            for power, (axis, bit) in enumerate(steps):
                if index >> power & 1:
                    flips[axis] = flips.get(axis, 0) ^ bit
            for number, by_column, side, core_flip, column in placed:
                strides = {"y": devices, "z": 2, "x": 1, "c": devices // 2}
                if not by_column:
                    strides["y"], strides["c"] = devices // 2, 0
                flips["c"] = core_flip
                target = 0
                for at, axis in enumerate(("y", "c", "z", "x")):
                    target += (place_ref[at] ^ flips.get(axis, 0)) * strides[axis]
                out_refs[number][target, :, column : column + columns] = refs[source][
                    index * sides + side, :, :columns
                ]


def layout_blocks(place, line, widths, chains):
    plans, sources = [], []
    for chain, columns, placed in chains:
        count = getattr(chain, "count", chain.held.shape[0])
        placed = [(number, widths[number][1], *rest) for number, *rest in placed]
        for base in ((), chain.order[-1:]):
            plans.append((line, chain.sides, count, columns, chain.order[:-1], base, placed))
        sources += [chain.held, chain.last]
    share = sources[0].shape[1]
    shapes = [
        shaped(((8 if by_column else 4) * line, share, width), BF16) for width, by_column in widths
    ]
    kernel = functools.partial(layout_kernel, plans, len(widths))
    outs = call(kernel, "layout_blocks", shapes, (place,), *sources)
    return [out.reshape(out.shape[0] * share, out.shape[2]) for out in outs]


def gathered_kernel(kernel, count, core_ref, *refs):
    copies = [
        pltpu.make_async_copy(refs[number], refs[number - count - 1], refs[-1].at[number])
        for number in range(count)
    ]
    for copy in copies:
        copy.start()
    for copy in copies:
        copy.wait()
    kernel(core_ref, *refs[-count - 1 : -1], *refs[count : -count - 1])


def sides_kernel(core_ref, *refs):
    *weight_refs, vector_ref, attn_ref, gate_up_ref = refs
    share, width = weight_refs[0].shape
    half, quarter = width // 2, width // 4
    for number, weight_ref in enumerate(weight_refs):
        out_ref, column = (attn_ref, number) if number < 3 else (gate_up_ref, number - 3)
        start = column * half
        for core in range(2):
            parts = [
                weight_ref[:, side * half + core * quarter : side * half + (core + 1) * quarter]
                for side in range(2)
            ]
            side = core ^ core_ref[0]
            if 0 < number < 3:
                for part in range(2):
                    start = half + 128 + part * half + (number - 1) * quarter
                    attn_ref[side, :, start : start + quarter] = parts[part]
            else:
                out_ref[side, :, start : start + half] = jnp.concatenate(parts, axis=1)
    for side in range(2):
        attn_ref[side, :, half : half + 128] = vector_ref[...]


def column_sides(core, weights, vectors):
    share, width = weights[0].shape
    shapes = (
        shaped((2, share, 3 * width // 2 + vectors.shape[1]), BF16),
        shaped((2, share, width), BF16),
    )
    arrays = [*weights, vectors]
    kernel = functools.partial(gathered_kernel, sides_kernel, len(arrays))
    return call(
        kernel, "column_sides", shapes, (core.reshape(1),), *arrays,
        scratch=[pltpu.VMEM(array.shape, array.dtype) for array in arrays]
        + [pltpu.SemaphoreType.DMA((len(arrays),))],
    )


def products_kernel(plans, mine_ref, *refs):
    outputs = iter(refs[sum(plan[1] + plan[2] for plan in plans) :])
    at = 0
    for share, lefts, rights, turned, chains in plans:
        left_refs, right_refs = refs[at : at + lefts], refs[at + lefts : at + lefts + rights]
        at += lefts + rights
        targets = [(next(outputs), next(outputs)) for _ in chains]
        size = left_refs[0].shape[0 if turned else 1] // 2
        wide = [ref[...] for ref in right_refs]
        wide = wide[0] if len(wide) == 1 else jnp.concatenate(wide, axis=1)
        starts = [sum(ref.shape[1] for ref in right_refs[:index]) for index in range(rights + 1)]
        for row_side in range(2):
            span = slice(row_side * size, (row_side + 1) * size)
            total, first = 0.0, 0
            for left_ref in left_refs:
                count = left_ref.shape[1 if turned else 0]
                right = wide[first : first + count]
                if turned:
                    total = total + nn(left_ref[span, :], right)
                else:
                    total = total + tn(left_ref[:, span], right)
                first += count
            for (which, columns, places), (kept_ref, sent_ref) in zip(chains, targets):
                result = total[:, starts[columns[0]] : starts[columns[-1] + 1]]

                def store(mine):
                    for block in range(size // share):
                        digit, target = places[row_side * (size // share) + block]
                        out_ref = kept_ref if digit == mine else sent_ref
                        out_ref[target] = result[block * share : (block + 1) * share].astype(BF16)

                pl.when(mine_ref[which] == 0)(functools.partial(store, 0))
                pl.when(mine_ref[which] == 1)(functools.partial(store, 1))


def products(mine, share, groups, name):
    plans, inputs, shapes = [], [], []
    count = 0
    for lefts, rights, chains, turned in groups:
        inputs += [*lefts, *rights]
        plan = []
        rows = lefts[0].shape[0 if turned else 1]
        for columns, dims, digit in chains:
            places = []
            for block in range(rows // share):
                index, rest = [], block
                for size in reversed(dims):
                    index.append(rest % size)
                    rest //= size
                index = index[::-1]
                value = index.pop(digit)
                flat = 0
                for size, digit_of in zip(dims[:digit] + dims[digit + 1 :], index):
                    flat = flat * size + digit_of
                places.append((value, flat))
            plan.append((count, columns, places))
            count += 1
            wide = sum(rights[column].shape[1] for column in columns)
            shape = (rows // share // 2, share, wide)
            shapes += [shaped(shape, BF16)] * 2
        plans.append((share, len(lefts), len(rights), turned, plan))
    kernel = functools.partial(products_kernel, plans)
    outs = call(kernel, name, shapes, (mine,), *inputs)
    return list(zip(outs[::2], outs[1::2]))


def back_kernel(core_ref, *refs):
    grad_q_refs, grad_kv_refs = refs[:2], refs[2:4]
    weight_ref, own_ref, sent_ref = refs[4:]
    chip_rows, quarter = grad_q_refs[0].shape
    rows = chip_rows // 2
    keys = weight_ref.shape[1] - 4 * quarter
    both = 0.0
    for part in range(2):
        first = keys + 2 * part * quarter
        both = both + nt(grad_kv_refs[part][...], weight_ref[:, first : first + 2 * quarter])
    grad_q = jnp.concatenate([ref[...] for ref in grad_q_refs], axis=1)
    here = nt(grad_q, weight_ref[:, : 2 * quarter]) + both[chip_rows:]
    for block in range(2):
        span = slice(block * rows, (block + 1) * rows)
        side = core_ref[0] ^ block

        def store(out_ref):
            out_ref[0] = here[span].astype(out_ref.dtype)
            out_ref[1] = both[span].astype(out_ref.dtype)

        pl.when(side == 0)(functools.partial(store, own_ref))
        pl.when(side == 1)(functools.partial(store, sent_ref))


def back_project(core, grad_q, grad_kv, weights):
    shape = (2, grad_q[0].shape[0] // 2, weights.shape[0])
    shapes = shaped(shape, F32), shaped(shape, BF16)
    arrays = *grad_q, *grad_kv, weights
    return call(back_kernel, "back_project", shapes, (core.reshape(1),), *arrays)


def step_kernel(plans, mine_ref, *refs):
    for number, plan in enumerate(plans):
        held_ref, came_ref = refs[plan["held"]], refs[plan["came"]]
        count, share, columns = held_ref.shape
        came_at, came_column = plan["came_at"]
        sent_at, sent_column = plan["sent_at"]

        def store(mine):
            for index in range(count):
                value = held_ref[index].astype(F32) + came_ref[
                    came_at + index, :share, came_column : came_column + columns
                ].astype(F32)
                digit, target = plan["places"][index]
                if digit == mine:
                    kept_ref = refs[plan["kept"]]
                    kept_ref[target] = value.astype(kept_ref.dtype)
                else:
                    sent_ref = refs[plan["sent"]]
                    sent_ref[sent_at + target, :share, sent_column : sent_column + columns] = (
                        value.astype(sent_ref.dtype)
                    )

        if plan["digit"] is None:
            store(0)
        else:
            pl.when(mine_ref[plan["digit"]] == 0)(functools.partial(store, 0))
            pl.when(mine_ref[plan["digit"]] == 1)(functools.partial(store, 1))


def finish_kernel(plans, core_ref, *refs):
    *own_refs, other_ref = refs[: -len(plans)]
    first_core = core_ref[0] == 0
    for plan, out_ref in zip(plans, refs[-len(plans) :]):
        for side, (source, column, other_column) in enumerate(plan):
            half = out_ref.shape[1] // 2
            own = own_refs[source][:, column : column + half // 2]
            other = other_ref[:, other_column : other_column + half // 2]
            pair = [jnp.where(first_core, own, other), jnp.where(first_core, other, own)]
            out_ref[:, side * half : (side + 1) * half] = jnp.concatenate(pair, axis=1)


def finish_columns(core, own, other, half, mixed):
    quarter = half // 2
    plans = []
    for index in range(len(own)):
        sources = [index, index]
        columns = [0, quarter]
        if mixed and index >= len(own) - 2:
            sources = [len(own) - 2, len(own) - 1]
            columns = [(index - len(own) + 2) * quarter] * 2
        plans.append([(s, col, s * half + col) for s, col in zip(sources, columns)])
    shapes = [shaped((own[0].shape[0], 2 * half), F32)] * len(own)
    kernel = functools.partial(finish_kernel, plans)
    return call(kernel, "finish_columns", shapes, (core.reshape(1),), *own, other)


def local(
    tokens,
    lengths,
    norm_attn,
    norm_mlp,
    query_scale,
    query_proj,
    key_proj,
    value_proj,
    output_proj,
    gate_proj,
    up_proj,
    down_proj,
    cotangent,
):
    place = {name: lax.axis_index(name) for name in ("y", "c", "z", "x")}
    y, c, x = place["y"], place["c"], place["x"]
    line = lax.axis_size("z")
    bits = line_bits(line)
    rows = tokens.shape[1]
    share, width = query_proj.shape
    half = width // 2
    quarter = width // 4
    chip_rows = 2 * rows
    length = 4 * rows

    near = ("z", 1)
    far = [("z", bit) for bit in reversed(bits[1:])]
    orders = (
        far + [("x", 1), ("y", 1), near],
        far + [("y", 1), near, ("x", 1)],
        far + [near, ("x", 1), ("y", 1)],
    )
    vector_columns = jnp.pad(
        jnp.stack([norm_attn, norm_mlp, query_scale], axis=1), ((0, 0), (0, 125))
    )
    attn_block, gate_up_block = column_sides(
        c, (query_proj, key_proj, value_proj, gate_proj, up_proj), vector_columns
    )
    own_tokens = tokens[0]
    other_tokens = across(own_tokens, "c", 1)
    other_cotangent = across(cotangent[0], "c", 1)
    before = across(own_tokens, "y", 1)
    other_before = across(before, "c", 1)
    chip_tokens = in_order(own_tokens, other_tokens, c, 0)
    chip_before = in_order(before, other_before, c, 0)
    all_tokens = jnp.concatenate([chip_before, chip_tokens], axis=0)

    attn_pieces, first = far_pieces(attn_block, far, (), (before,))
    attn_others = other_cores(attn_pieces, other_tokens, other_cotangent)
    cuts = (0, half + 128, 2 * half + 128, 3 * half + 128)
    attn_chains = [
        Chain(blocks, 2, order, len(far))
        for blocks, order in zip(
            side_blocks(attn_pieces, attn_others, list(zip(cuts, cuts[1:]))), orders
        )
    ]
    places_now = jnp.stack([place[name] for name in ("y", "c", "z", "x")])
    second = advance_all(attn_chains)
    gate_up_pieces, middle = far_pieces(gate_up_block, far, first, second)
    third = advance_all(attn_chains, other_before, *middle)
    output_pieces, late = far_pieces(output_proj, far, (*middle, *second, other_before))
    gate_up_sent = jnp.stack([piece[1] for piece in gate_up_pieces])
    gate_up_others = across(after(gate_up_sent, other_before), "c", 1)
    gate_up_sides = side_blocks(
        gate_up_pieces, list(gate_up_others), [(0, half), (half, width)]
    )
    mlp_chains = [
        Chain(blocks, 2, order, len(far)) for blocks, order in zip(gate_up_sides, orders)
    ]
    output_sides = [piece[:, cut : cut + half] for piece in output_pieces for cut in (0, half)]
    mlp_chains.append(Chain(jnp.stack(output_sides), 2, orders[2], len(far)))
    advance_together(attn_chains[1:] + attn_chains[:1], mlp_chains)
    fourth = [chain.last for chain in attn_chains]
    mlp_third = advance_all(mlp_chains)
    down_pieces, _ = far_pieces(down_proj, far, third)
    down_chains = [
        Chain(jnp.stack([piece[:, cut : cut + half] for piece in down_pieces]), 1, order, len(far))
        for cut, order in zip((0, half), orders)
    ]
    down_second = advance_all(down_chains, *fourth)

    doc_ends = jnp.cumsum(lengths[0])
    places = jnp.arange(length, dtype=jnp.int32)
    segment = jnp.sum((places[:, None] >= doc_ends[None, :]).astype(jnp.int32), axis=1)
    seg_here = block_of(segment, y, chip_rows)
    seg_before = jnp.where(y == 0, -1, segment[:chip_rows])
    seg_keys = jnp.concatenate([seg_before, seg_here])[None]
    seg_rows = seg_here[:, None]
    first_row = y * chip_rows + jnp.arange(rows, dtype=jnp.int32)
    upstream_b = [
        jnp.where((first_row + core * rows < doc_ends[-1])[:, None], rows_of, 0).astype(BF16)
        for core, rows_of in ((c, cotangent[0]), (1 - c, other_cotangent))
    ]
    upstream = upstream_b[0]
    upstream_b = jnp.concatenate(upstream_b, axis=0)
    both = ((0, 0), (1, 1))
    (attn_weights,) = layout_blocks(
        places_now,
        line,
        [(3 * half + 128, True)],
        [
            (chain, end - cut, [(0, side, flip, cut) for side, flip in both])
            for chain, cut, end in zip(attn_chains, cuts, cuts[1:])
        ],
    )
    q_raw, queries, keys_values, normed_before, normed_here, vectors, scale_rows = project(
        c, all_tokens, attn_weights
    )
    gain_a, gain_m = vectors[0], vectors[1]
    mlp_sent_last = advance_all(mlp_chains, queries)
    down_third = advance_all(down_chains, queries)
    queries = after(queries, *[chain.held for chain in mlp_chains + down_chains])
    attended_f, attended, lse = attention_forward(queries, keys_values, seg_rows, seg_keys)
    attended = after(attended, *mlp_sent_last, *down_third, upstream_b)
    for chain in mlp_chains:
        chain.last = after(chain.last, attended)
    down_last = advance_all(down_chains, attended)

    (proj_o,) = layout_blocks(
        places_now,
        line,
        [(width, False)],
        [(mlp_chains[2], half, [(0, 0, 0, 0), (0, 1, 0, half)])],
    )
    output_own, output_sent = output_project(c, attended, proj_o)
    hidden1, normed_own = norm_middle(
        output_own, across(output_sent, "c", 1), own_tokens, gain_m
    )
    normed_others = [
        across(normed_own[start : start + rows // 2], "c", 1) for start in (0, rows // 2)
    ]
    for chain in mlp_chains[:2]:
        chain.last = after(chain.last, output_sent)
    (proj_gu,) = layout_blocks(
        places_now,
        line,
        [(width, True)],
        [
            (chain, half, [(0, side, flip, cut) for side, flip in both])
            for chain, cut in zip(mlp_chains, (0, half))
        ],
    )
    hidden, gate_pre, up_pre, normed_m = mlp_first((normed_own, *normed_others), proj_gu)
    for chain in down_chains:
        chain.last = after(chain.last, hidden)
    (proj_d,) = layout_blocks(
        places_now,
        line,
        [(width, False)],
        [(chain, half, [(0, 0, 0, cut)]) for chain, cut in zip(down_chains, (0, half))],
    )

    digits = [("y", 1), ("c", 1)] + [("z", bit) for bit in reversed(bits)] + [("x", 1)]
    scatter_orders = [order[len(far) :][::-1] for order in orders]

    output_orders = [("x", 1), ("y", 1), near], [("y", 1), ("x", 1), near]

    def own_digit(axis, bit):
        return (place[axis] // bit) % 2

    def sizes_of(names, by_column):
        return tuple(1 if name == ("c", 1) and not by_column else 2 for name in names)

    def first_step(*groups, gate=(), name="products"):
        mine, plans, states = [], [], []
        for lefts, rights, columns, chain_orders, turned in groups:
            by_column = lefts[0].shape[0 if turned else 1] == width
            dims = sizes_of(digits, by_column)
            chains = []
            for which, order in zip(columns, chain_orders):
                at = digits.index(order[0])
                chains.append((which, dims, at))
                mine.append(own_digit(*order[0]))
                names = digits[:at] + digits[at + 1 :]
                states.append({"names": names, "by_column": by_column, "order": order, "step": 1})
            plans.append((lefts, rights, chains, turned))
        if share % 8 == 0:
            parts = products(jnp.stack(mine).astype(jnp.int32), share, plans, name)
        else:
            parts = []
            for lefts, rights, chains, turned in plans:
                left = jnp.concatenate([each.T if turned else each for each in lefts], axis=0)
                for which, dims, at in chains:
                    right = jnp.concatenate([rights[column] for column in which], axis=1)
                    part = tn(left, right).astype(BF16).reshape(dims + (share, right.shape[1]))
                    digit = mine[len(parts)]
                    parts.append(
                        [
                            lax.dynamic_index_in_dim(part, which_half, at, keepdims=False).reshape(
                                -1, share, right.shape[1]
                            )
                            for which_half in (digit, 1 - digit)
                        ]
                    )
        sent = [after(value, *gate) if gate else value for _, value in parts]
        for state, (kept, _), value in zip(states, parts, sent):
            state.update(held=kept, came=across(value, *state["order"][0]), came_at=(0, 0))
        return states, [value for _, value in parts]

    def step(states, names, *earlier, packed=None, dtype=BF16):
        mine, plans, inputs, shapes = [], [], [], []
        came = [after(state["came"], *earlier) if earlier else state["came"] for state in states]
        sources = {}
        for state, array in zip(states, came):
            key = id(state["came"])
            if key not in sources:
                sources[key] = len(inputs)
                inputs.append(array)
        new_states = []
        for number, (state, name) in enumerate(zip(states, names)):
            dims = sizes_of(state["names"], state["by_column"])
            held = state["held"]
            plan = {"came": sources[id(state["came"])], "came_at": state["came_at"]}
            plan["held"] = len(inputs)
            inputs.append(held)
            at = state["names"].index(name) if name in state["names"] else None
            if at is not None and dims[at] == 1:
                at = None
            rest = [index for index in range(len(dims)) if index != at]
            places = []
            for index in range(held.shape[0]):
                values, left_over = [], index
                for size in reversed(dims):
                    values.append(left_over % size)
                    left_over //= size
                values = values[::-1]
                flat = 0
                for axis_at in rest:
                    flat = flat * dims[axis_at] + values[axis_at]
                places.append((0 if at is None else values[at], flat))
            plan["places"] = places
            plan["digit"] = None if at is None else len(mine)
            if at is not None:
                mine.append(own_digit(*name))
            plan["sent_at"] = packed[1][number] if packed else (0, 0)
            plan["kept"] = len(shapes)
            count = held.shape[0] // (1 if at is None else 2)
            shapes.append(shaped((count,) + held.shape[1:], F32))
            if at is not None and not packed:
                plan["sent"] = len(shapes)
                shapes.append(shaped((count,) + held.shape[1:], dtype))
            plans.append(plan)
            names_left = [state["names"][axis_at] for axis_at in rest]
            new_states.append(dict(state, names=names_left, came_at=plan["sent_at"]))
        if packed:
            for plan in plans:
                plan["sent"] = len(shapes)
            shapes.append(shaped(packed[0], dtype))
        for plan in plans:
            plan["kept"] += 1 + len(inputs) - 1
            if "sent" in plan:
                plan["sent"] += len(inputs)
        if not mine:
            mine = [place["c"]]
        kernel = functools.partial(step_kernel, plans)
        outs = call(kernel, "step", shapes, (jnp.stack(mine).astype(jnp.int32),), *inputs)
        for plan, state in zip(plans, new_states):
            state["held"] = outs[plan["kept"] - len(inputs)]
        if packed:
            return new_states, outs[-1]
        return new_states, [
            outs[plan["sent"] - len(inputs)] if plan["digit"] is not None else None
            for plan in plans
        ]

    def halve(states, *earlier):
        names = [state["order"][state["step"]] for state in states]
        states, sent = step(states, names, *earlier)
        for state, value, name in zip(states, sent, names):
            state.update(came=across(value, *name), came_at=(0, 0), step=state["step"] + 1)
        return states, sent

    def halve_far(states, shape, places, *earlier):
        for axis, bit in far[::-1][:-1]:
            states, sent = step(states, [(axis, bit)] * len(states))
            for state, value in zip(states, sent):
                state.update(came=across(value, axis, bit), came_at=(0, 0))
        last = far[0]
        states, message = step(states, [last] * len(states), *earlier, packed=(shape, places))
        arrived = across(message, *last)
        for state in states:
            state.update(came=arrived)
        return states, message

    def join_columns(states):
        left, right = states
        joined = dict(left, came_at=(0, 0))
        for key in ("held", "came"):
            joined[key] = jnp.concatenate([left[key], right[key]], axis=2)
        return [joined]

    def received(states):
        return [state["came"] for state in states]

    down_states, down_sent = first_step(
        ((hidden,), (upstream_b,), ((0,),), scatter_orders[:1], False), name="products_down"
    )
    grad_gate, grad_up = mlp_last(gate_pre, up_pre, proj_d, after(upstream_b, *down_sent))
    gate_own, gate_sent = rows_product((grad_gate, grad_up), proj_gu, True, "gate_up_back")
    mlp_states, mlp_sent = first_step(
        (
            (normed_m,),
            after((grad_gate, grad_up), gate_sent),
            ((0,), (1,)),
            scatter_orders[1:],
            False,
        ),
        name="products_mlp",
    )
    mlp_states = down_states + mlp_states
    gate_own = after(gate_own, *mlp_sent)
    grad_hidden1, low_own, grad_gain_m = middle_back(
        gate_own, across(gate_sent, "c", 1), hidden1, upstream, gain_m
    )
    low_others = [across(low_own[start : start + rows // 2], "c", 1) for start in (0, rows // 2)]
    grad_attended, grad_hidden1_b = attended_back(c, low_own, low_others, proj_o)
    scale_row = scale_rows[:1]
    heads = half // HD
    residuals = (queries, keys_values), (attended_f, lse, seg_rows, seg_keys, q_raw, scale_row)
    grad_q_early, grad_kv_early, early_sums = attention_backward(
        0, heads // 2, *residuals[0], grad_attended, *residuals[1]
    )
    down_own, down_sent = rows_product(
        (after(hidden, grad_attended),), proj_d, False, "down_project"
    )
    down_other = across(down_sent, "c", 1)
    block_out = hidden1 + down_own + down_other
    mlp_states, mlp_sent = halve(mlp_states, grad_kv_early, down_other)
    grad_rows = after(grad_hidden1_b, *mlp_sent)
    output_rights = grad_rows[:, :half], grad_rows[:, half:]
    output_states, output_sent = first_step(
        ((attended,), output_rights, ((0,), (1,)), output_orders, False)
    )
    grad_attended = after(grad_attended, *mlp_sent, *output_sent)
    grad_q_late, grad_kv_late, late_sums = attention_backward(
        heads // 2, heads, *residuals[0], grad_attended, *residuals[1]
    )
    grad_scale = jnp.concatenate([early_sums[0], late_sums[0]]) * scale_rows[1]
    grads = (grad_q_early, grad_q_late), (grad_kv_early, grad_kv_late)
    mlp_states, mlp_sent = halve(mlp_states, grad_kv_late)
    output_states, output_sent = halve(output_states, grad_kv_late)
    grads = after(grads, *mlp_sent, *output_sent)
    attn_states, attn_sent = first_step(
        ((normed_here,), grads[0], ((0, 1),), scatter_orders[:1], False),
        ((normed_before, normed_here), grads[1], ((0,), (1,)), scatter_orders[1:], False),
        gate=received(mlp_states + output_states),
    )
    first_done = received(attn_states)
    grads = after(grads, *attn_sent)
    mlp_states, _ = halve_far(
        mlp_states, (3, share, width), ((2, 0), (0, 0), (0, half)), *attn_sent
    )
    back_own, back_sent = back_project(c, *grads, attn_weights)
    back_other = across(back_sent, "c", 1)
    output_states = join_columns(
        [dict(state, came=after(state["came"], *first_done)) for state in output_states]
    )
    output_states, _ = halve(output_states)
    attn_states, _ = halve(attn_states, mlp_states[0]["came"], back_own)
    second_done = received(attn_states)
    grad_here, grad_before, grad_gain_a = gain_terms(back_own, back_other, own_tokens, before)
    scale_rows = grad_scale.reshape(2, 1, quarter)
    scale_rows = jnp.where(
        c == 0,
        jnp.pad(scale_rows, ((0, 0), (0, 1), (0, 0))),
        jnp.pad(scale_rows, ((0, 0), (1, 0), (0, 0))),
    ).reshape(width)
    vector_terms = jnp.stack([grad_gain_a[0], grad_gain_m[0], scale_rows])
    vector_rows = min(8, share)
    vector_terms = jnp.moveaxis(vector_terms.reshape(3, -1, share), 0, 1)
    room = ((0, 0), (0, vector_rows - 3), (0, 128 - share))
    vector_terms = jnp.pad(vector_terms, room)
    vector_order = [near] + far[::-1] + [("x", 1), ("y", 1)]
    vector_state = {"names": digits, "by_column": True, "order": vector_order, "step": 0}
    zero_terms = jnp.zeros(vector_terms.shape, BF16)
    vector_states = [dict(vector_state, held=vector_terms, came=zero_terms, came_at=(0, 0))]
    vector_states, _ = halve(vector_states)
    attn_states, _ = halve(attn_states, *received(output_states + vector_states))
    third_done = received(attn_states)
    output_states, _ = halve_far(output_states, (1, share, width), ((0, 0),))
    for _ in far:
        vector_states, _ = halve(vector_states)
    vector_first = received(vector_states)
    vector_states, _ = halve(vector_states, *third_done)
    vector_second = received(vector_states)
    grad_after = across(after(grad_before, *third_done), "y", 1)
    grad_inputs = tokens_back(y, grad_here, grad_after, own_tokens, gain_a, grad_hidden1)

    attn_places = [(0, number * half) for number in range(3)]
    final_states, final_message = halve_far(
        attn_states, (2, share, 3 * half), attn_places, *received(output_states), *vector_first
    )
    vector_states, _ = halve(vector_states, grad_after)
    vector_third = received(vector_states)
    mlp_states, sent = step(
        mlp_states,
        [("c", 1)] * 3,
        final_message,
        packed=((1, share, width), ((0, 0), (0, 0), (0, half))),
        dtype=F32,
    )
    mlp_parts = [state["held"][0] for state in mlp_states]
    gate_up_other = across(sent[0], "c", 1)
    gate_up_grads = finish_columns(c, mlp_parts[1:], gate_up_other, half, False)
    final_states, sent = step(
        final_states,
        [("c", 1)] * 3,
        grad_after,
        gate_up_other,
        packed=((1, share, 3 * half), attn_places),
        dtype=F32,
    )
    output_states, _ = step(output_states, [("c", 1)], final_message)
    own_parts = [state["held"][0] for state in final_states + output_states]
    other = across(sent[0], "c", 1)
    attn_grads = finish_columns(c, own_parts[:3], other, half, True)
    vector_states, vector_sent = step(vector_states, [("c", 1)], dtype=F32)
    vector_other = across(vector_sent[0][0], "c", 1)
    summed = (vector_states[0]["held"][0] + vector_other)[:, :share]
    return (
        block_out.astype(BF16)[None],
        grad_inputs[None],
        summed[0],
        summed[1],
        summed[2],
        *attn_grads,
        own_parts[3],
        *gate_up_grads,
        mlp_parts[0],
    )


def solution(mesh):
    seq, dp = mesh.devices.shape
    axes = Mesh(mesh.devices.reshape(seq // 2, 2, dp // 2, 2), ("y", "c", "z", "x"))
    batch, places, every = ("z", "x"), ("y", "c"), ("y", "c", "z", "x")
    activations = P(batch, places, None)
    vector, matrix = P(every), P(every, None)
    return jax.shard_map(
        local,
        mesh=axes,
        in_specs=(activations, P(batch, None)) + (vector,) * 3 + (matrix,) * 7 + (activations,),
        out_specs=(activations, activations) + (vector,) * 3 + (matrix,) * 7,
        check_vma=False,
    )
```
